32 devices in a mesh: sec: 8 (over y, x, core), tile: 4 (over z).
Axes of the slice: x: 2, y: 2, z: 4, core: 2. Of those that a mesh axis runs over, the one named last changes fastest.
Arguments:
- in_plane_force: float32 [2, 16, 256, 256], P(None, 'sec', 'tile'), may hold values from -6 to 6
- stiffness: float32 [16, 256, 256], P('sec', 'tile'), may hold values from 0.5 to 2
- stiffness_z: float32 [16, 256, 256], P(None, ('tile', 'sec')), may hold values from 0.3 to 1.5
- patch_dest: int32 [8, 4, 256, 1], P('sec', 'tile'), may hold values from 0 to 7; in each aligned block of 256 rows (0 to 255, 256 to 511, ..., all dimensions but the last counted through in order) at most 64 rows name the same one
- patch_pos: int32 [8, 4, 256], P('sec', 'tile'), may hold values from 0 to 31
- patch_flow: float32 [8, 4, 256, 2, 128], P('sec', 'tile'), may hold values from -6 to 6
- patch_conf: float32 [8, 4, 256, 128], P('sec', 'tile'), may hold values from 0.2 to 1
Outputs:
- displacement: float32 [2, 16, 256, 256], P(None, None, ('tile', 'sec'))
The draws below stay inside these ranges and needn't reach their ends.
Inputs may be any that keep to these rules, and one draw needn't show every extreme that they name: `patch_dest`: among the 256 patches of one section group and tile, at most 64 name the same owner; in some of them an owner is named exactly 64 times.
All inputs are finite; a program needn't handle non-finite values.
Results may differ from the reference program's by a relative error of at most 0.00002.
Values sent between devices are 32-bit elements; how exact they have to be, the bound alone decides.
No kernel may reach another device: no remote copies, remote signals or barrier semaphores. Data moves between devices by JAX's collectives and lax.ppermute only.
A program may use at most 64 MiB of HBM per device.

```python
import math
import jax
import jax.numpy as jnp
import numpy as np
from jax import lax

ZD = 2
YD = 64
XN = 256
PW = 128
P_DEV = 256
ISTEPS = 8
ZSTEPS = 8
Z = 16
YT = 256
YO = 8
XB = 2
CAP = 64
N_SEC = 8
N_TILE = 4


def touch_ends(entries, own_key, least, top_value):
    index_at = [jax.random.randint(jax.random.fold_in(own_key, axis), (), 0, length) for axis, length in enumerate(entries.shape)]
    longest = entries.shape.index(max(entries.shape))
    next_to = index_at[:longest] + [(index_at[longest] + 1) % entries.shape[longest]] + index_at[longest + 1:]
    return entries.at[tuple(index_at)].set(least).at[tuple(next_to)].set(top_value)


def shard_levels(stream_key, extent, shards, low, high):
    def one(axis_at, parts):
        heights = jax.random.uniform(jax.random.fold_in(jax.random.fold_in(stream_key, 6), axis_at), (parts,), jnp.float32, low / len(shards), high / len(shards))
        return jnp.repeat(jnp.exp(heights), extent[axis_at] // parts).reshape((-1,) + (1,) * (len(extent) - axis_at - 1))

    level = one(*shards[0])
    for cut in shards[1:]:
        level = level * one(*cut)
    return level


def shared_out(own_key, own, number, rows, count, top, limit, slope):
    order = jax.random.permutation(own_key, count)
    packed, common = load_shares(count, rows * top, limit, slope, True), load_shares(count, rows * top, limit, slope, False)
    places = jnp.arange(count)

    def named(sizes, turn):
        used = int((sizes > 0).sum())
        fixed = max(1, used // 4)
        passed = fixed + (places - fixed + turn * (used - fixed)) % max(1, count - fixed)
        return jnp.zeros((count,), jnp.int32).at[order[jnp.where(places < fixed, places, passed)]].set(jnp.asarray(sizes, jnp.int32))

    sizes = jnp.where(number % 4 == 0, named(packed, number // 4), named(common, number - number // 4 - 1))
    mixed = jax.random.permutation(jax.random.fold_in(own, 3), count)
    source_of, receiver = mixed[0:count // 2 * 2:2], mixed[1:count // 2 * 2:2]
    room = jnp.minimum(sizes[source_of] - 1, limit - sizes[receiver]) // 2
    room = jnp.where((source_of == order[0]) | (receiver == order[0]) | (sizes[receiver] == 0), 0, jnp.maximum(room, 0))
    passed = jax.random.randint(jax.random.fold_in(own, 4), (count // 2,), 0, 1 << 20) % (room + 1)
    sizes = sizes.at[source_of].add(-passed).at[receiver].add(passed)
    labels = jnp.searchsorted(jnp.cumsum(sizes), jnp.arange(rows * top), side="right").astype(jnp.int32)
    listing = labels.reshape(top, rows).T
    listing = listing[jax.random.permutation(jax.random.fold_in(own, 1), rows)]
    turn = jax.random.randint(jax.random.fold_in(own, 2), (rows, 1), 0, top)
    return jnp.take_along_axis(listing, (jnp.arange(top)[None, :] + turn) % top, axis=1)


def load_shares(count, total, most, lean, full):
    weights = [(1 << 20) // math.isqrt(rank ** lean) + 1 for rank in range(1, count + 1)]
    largest = most if full else min(most, max(-(-total // count), total * weights[0] // sum(weights)))
    least = 1 if total - largest >= count - 1 else 0
    counts, surplus = [largest] + [least] * (count - 1), total - largest - least * (count - 1)
    while surplus > 0:
        candidates = [i for i in range(1, count) if counts[i] < largest] or [i for i in range(1, count) if counts[i] < most]
        mass, remaining = sum([weights[i] for i in candidates]), surplus
        for i in candidates:
            extra = min(most - counts[i], max(1, remaining * weights[i] // mass), surplus)
            counts[i] = counts[i] + extra
            surplus = surplus - extra
    return np.array(counts)


def normal_values(rng, extent, width, bound, cuts=(), held_as=jnp.bfloat16):
    gain = shard_levels(rng, extent, cuts, -0.22, 0.18) if cuts else 1.0
    values = jax.random.normal(rng, extent, jnp.float32) * width * gain
    return jnp.minimum(jnp.maximum(values, -bound), bound).astype(held_as)


def setup_inputs(seed: int = 0) -> dict:
    keys = jax.random.split(jax.random.key(seed), 8)
    in_plane_force = normal_values(keys[0], (2, Z, YT, XN), 1.0, 6.0, ((1, 8), (2, 4)), jnp.float32)
    stiffness = jnp.clip(jnp.exp(math.log(2.0) - 1.3862944 * jax.random.uniform(keys[1], (Z, YT, XN), jnp.float32) ** shard_levels(keys[1], (Z, YT, XN), ((0, 8), (1, 4)), -0.2, 0.2)), 0.5, 2.0)
    stiffness_z = jnp.clip(jnp.exp(math.log(1.5) - 1.60943787 * jax.random.uniform(keys[2], (Z, YT, XN), jnp.float32) ** shard_levels(keys[2], (Z, YT, XN), ((1, 32),), -0.2, 0.2)), 0.3, 1.5)
    patch_dest_keys = jax.random.split(jax.random.fold_in(keys[3], 1), N_SEC * N_TILE * P_DEV // P_DEV)
    patch_dest_turns = jax.random.permutation(jax.random.fold_in(keys[3], 3), N_SEC * N_TILE * P_DEV // P_DEV)
    patch_dest = jax.vmap(lambda own, number: shared_out(jax.random.fold_in(keys[3], 2), own, number, P_DEV, N_SEC, 1, CAP, 2))(patch_dest_keys, patch_dest_turns).reshape((N_SEC, N_TILE, P_DEV, 1))
    patch_pos = touch_ends(jax.random.randint(keys[4], (N_SEC, N_TILE, P_DEV), 0, ZD * YO * XB), jax.random.fold_in(keys[4], 1), 0, (ZD * YO * XB) - 1).astype(jnp.int32)
    patch_flow = normal_values(keys[5], (N_SEC, N_TILE, P_DEV, 2, PW), 1.0, 6.0, ((0, 8), (1, 4)), jnp.float32)
    patch_conf = jnp.clip(0.2 + 0.8 * jax.random.uniform(keys[6], (N_SEC, N_TILE, P_DEV, PW), jnp.float32) ** shard_levels(keys[6], (N_SEC, N_TILE, P_DEV, PW), ((0, 8), (1, 4)), -0.2, 0.2), 0.2, 1.0)
    return {"in_plane_force": in_plane_force, "stiffness": stiffness, "stiffness_z": stiffness_z, "patch_dest": patch_dest, "patch_pos": patch_pos, "patch_flow": patch_flow, "patch_conf": patch_conf}


STEP_PLANE = 0.12
STEP_CROSS = 0.15


def plane_laplace(field):
    padded = jnp.pad(field, ((0, 0), (0, 0), (1, 1), (1, 1)))
    return padded[:, :, 2:, 1:-1] + padded[:, :, :-2, 1:-1] + padded[:, :, 1:-1, 2:] + padded[:, :, 1:-1, :-2] - 4.0 * field


def cross_steps(field, pull, weight, stiffness_z):
    for step in range(ZSTEPS):
        zero_layer = jnp.zeros(field.shape[:1] + (1,) + field.shape[2:], jnp.float32)
        below = jnp.concatenate([zero_layer, field[:, :-1]], axis=1)
        above = jnp.concatenate([field[:, 1:], zero_layer], axis=1)
        stretch = pull - weight[None] * (field - below)
        stretch_above = jnp.concatenate([stretch[:, 1:], zero_layer], axis=1)
        field = field + STEP_CROSS * (stiffness_z[None] * (above + below - 2.0 * field) + stretch - stretch_above)
    return field


def reference(in_plane_force, stiffness, stiffness_z, patch_dest, patch_pos, patch_flow, patch_conf):
    field = jnp.zeros(in_plane_force.shape, jnp.float32)
    for step in range(ISTEPS):
        field = field + STEP_PLANE * (stiffness[None] * plane_laplace(field) + in_plane_force)
    group = lax.broadcasted_iota(jnp.int32, (N_SEC, N_TILE, P_DEV), 0)
    tile_index = lax.broadcasted_iota(jnp.int32, (N_SEC, N_TILE, P_DEV), 1)
    layer = patch_pos // (YO * XB)
    inner_row = (patch_pos // XB) % YO
    column_block = patch_pos % XB
    section = group * ZD + layer
    node_row = tile_index * YD + patch_dest[..., 0] * YO + inner_row
    target = ((section * YT + node_row) * XB + column_block).reshape(-1).astype(jnp.int32)
    weighted = patch_conf[:, :, :, None, :] * patch_flow
    payload = jnp.concatenate([weighted, patch_conf[:, :, :, None, :]], axis=3).reshape(-1, 3, PW)
    grid = jnp.zeros((Z * YT * XB, 3, PW), jnp.float32).at[target].add(payload)
    grid = grid.reshape(Z, YT, XB, 3, PW).transpose(3, 0, 1, 2, 4).reshape(3, Z, YT, XN)
    return cross_steps(field, grid[:2], grid[2], stiffness_z)
```

```python
import functools

import jax
import jax.numpy as jnp
from jax import lax
from jax.experimental import pallas as pl
from jax.experimental.pallas import tpu as pltpu
from jax.sharding import PartitionSpec as P

ISTEPS = 8
ZSTEPS = 8


STEP_PLANE = 0.12
STEP_CROSS = 0.15

HALO = -(-(ISTEPS - 1) // 8) * 8

VMEM = pl.BlockSpec(memory_space=pltpu.VMEM)


def spread_kernel(layers, inner_rows, blocks, dest_ref, pos_ref, flow_ref, conf_ref, out_ref):
    groups = out_ref.shape[0]
    count, width = conf_ref.shape
    place = pos_ref[...]
    layer = place // (inner_rows * blocks)
    inner_row = place // blocks % inner_rows
    column_block = place % blocks
    slot = (dest_ref[...] * layers + layer) * inner_rows + inner_row
    slots = groups * layers * inner_rows
    conf = conf_ref[...]
    terms = [flow_ref[pl.ds(c, count, stride=2), :] * conf for c in range(2)] + [conf]
    rest = jnp.concatenate(terms, axis=1)
    parts = []
    for _ in range(3):
        parts.append(rest.astype(jnp.bfloat16))
        rest = rest - parts[-1].astype(jnp.float32)
    numbers = lax.broadcasted_iota(jnp.int32, (slots, count), 0)
    for b in range(blocks):
        key = jnp.where(column_block == b, slot, -1)
        hit = jnp.where(numbers == key, 1.0, 0.0).astype(jnp.bfloat16)
        total = sum(jnp.dot(hit, part, preferred_element_type=jnp.float32) for part in reversed(parts))
        for o in range(groups):
            for l in range(layers):
                start = (o * layers + l) * inner_rows
                for c in range(3):
                    out_ref[o, c, l, :, b * width : (b + 1) * width] = total[
                        start : start + inner_rows, c * width : (c + 1) * width
                    ]


def shifted(blocks, lane, width):
    ahead = [pltpu.roll(x, width - 1, 1) for x in blocks]
    behind = [pltpu.roll(x, 1, 1) for x in blocks]
    zero = jnp.zeros_like(blocks[0])
    right = [jnp.where(lane == width - 1, after, own) for own, after in zip(ahead, ahead[1:] + [zero])]
    left = [jnp.where(lane == 0, before, own) for own, before in zip(behind, [zero] + behind[:-1])]
    return left, right


def plane_kernel(force_ref, stiff_ref, before_ref, after_ref, forces_ref, out_ref):
    _, layers, rows, columns = force_ref.shape
    out_ref[:, 2:] = forces_ref[...]
    groups = out_ref.shape[0]
    inner_rows = rows // groups
    width = 128
    total = rows + 2 * HALO
    lane = lax.broadcasted_iota(jnp.int32, (total, width), 1)
    spans = [slice(i * width, (i + 1) * width) for i in range(columns // width)]
    for l in range(layers):
        spring, keep = [], []
        for span in spans:
            k = STEP_PLANE * jnp.concatenate(
                [before_ref[2, l, :, span], stiff_ref[l, :, span], after_ref[2, l, :, span]], axis=0
            )
            spring.append(k)
            keep.append(1.0 - 4.0 * k)
        for c in range(2):
            push = [
                STEP_PLANE
                * jnp.concatenate(
                    [before_ref[c, l, :, span], force_ref[c, l, :, span], after_ref[c, l, :, span]], axis=0
                )
                for span in spans
            ]
            field = push
            for step in range(1, ISTEPS):
                left, right = shifted(field, lane, width)
                field = [
                    k * (pltpu.roll(x, 1, 0) + pltpu.roll(x, total - 1, 0) + a + b) + (g * x + f)
                    for x, a, b, k, g, f in zip(field, left, right, spring, keep, push)
                ]
            for span, x in zip(spans, field):
                for o in range(groups):
                    start = HALO + o * inner_rows
                    out_ref[o, c, l, :, span] = x[start : start + inner_rows]


def cross_kernel(moved_ref, stiff_ref, out_ref):
    groups, _, layers, inner_rows, columns = moved_ref.shape
    sections = groups * layers
    width = 128
    zero = jnp.zeros((1, inner_rows, width), jnp.float32)
    for i in range(columns // width):
        span = slice(i * width, (i + 1) * width)

        def channel(c):
            return moved_ref[:, c, :, :, span].reshape(sections, inner_rows, width)

        spring = STEP_CROSS * stiff_ref[:, :, span]
        weight = STEP_CROSS * channel(4)
        for c in range(2):
            pull = STEP_CROSS * channel(2 + c)
            field = channel(c)
            for step in range(ZSTEPS):
                rise = field - jnp.concatenate([zero, field[:-1]], axis=0)
                rise_above = jnp.concatenate([rise[1:], -field[-1:]], axis=0)
                stretch = pull - weight * rise
                stretch_above = jnp.concatenate([stretch[1:], zero], axis=0)
                field = field + (spring * (rise_above - rise) + (stretch - stretch_above))
            out_ref[c, :, :, span] = field


def per_device(
    in_plane_force, stiffness, stiffness_z, patch_dest, patch_pos, patch_flow, patch_conf
):
    groups = lax.axis_size("sec")
    tiles = lax.axis_size("tile")
    layers, rows, columns = stiffness.shape
    inner_rows = rows // groups
    width = patch_flow.shape[-1]
    blocks = columns // width
    count = patch_pos.shape[2]
    up = [(i, i + 1) for i in range(tiles - 1)]
    down = [(j, i) for i, j in up]

    def edge(start):
        return jnp.concatenate(
            [in_plane_force[:, :, start : start + HALO], stiffness[None, :, start : start + HALO]], axis=0
        )

    before = lax.ppermute(edge(rows - HALO), "tile", up)
    after = lax.ppermute(edge(0), "tile", down)
    forces = pl.pallas_call(
        functools.partial(spread_kernel, layers, inner_rows, blocks),
        out_shape=jax.ShapeDtypeStruct((groups, 3, layers, inner_rows, columns), jnp.float32),
        in_specs=[VMEM] * 4,
        out_specs=VMEM,
        cost_estimate=pl.CostEstimate(flops=6 * 256 * 256 * 384, bytes_accessed=800000, transcendentals=0),
        name="spread_patches",
    )(
        patch_dest.reshape(1, count),
        patch_pos.reshape(1, count),
        patch_flow.reshape(count * 2, width),
        patch_conf.reshape(count, width),
    )
    mixed = pl.pallas_call(
        plane_kernel,
        out_shape=jax.ShapeDtypeStruct((groups, 5, layers, inner_rows, columns), jnp.float32),
        in_specs=[VMEM] * 5,
        out_specs=VMEM,
        cost_estimate=pl.CostEstimate(flops=10000000, bytes_accessed=800000, transcendentals=0),
        name="plane_steps",
    )(in_plane_force, stiffness, before, after, forces)
    moved = lax.all_to_all(mixed, "sec", split_axis=0, concat_axis=0, tiled=True)
    return pl.pallas_call(
        cross_kernel,
        out_shape=jax.ShapeDtypeStruct((2, groups * layers, inner_rows, columns), jnp.float32),
        in_specs=[VMEM] * 2,
        out_specs=VMEM,
        cost_estimate=pl.CostEstimate(flops=10000000, bytes_accessed=800000, transcendentals=0),
        name="cross_steps",
    )(moved, stiffness_z)


def solution(mesh):
    placed = (
        P(None, "sec", "tile", None),
        P("sec", "tile", None),
        P(None, ("tile", "sec"), None),
        P("sec", "tile", None, None),
        P("sec", "tile", None),
        P("sec", "tile", None, None, None),
        P("sec", "tile", None, None),
    )
    return jax.shard_map(
        per_device,
        mesh=mesh,
        in_specs=placed,
        out_specs=P(None, None, ("tile", "sec"), None),
        check_vma=False,
    )
```

```python
import functools

import jax
import jax.numpy as jnp
from jax import lax
from jax.experimental import pallas as pl
from jax.experimental.pallas import tpu as pltpu
from jax.sharding import PartitionSpec as P

ISTEPS = 8
ZSTEPS = 8


STEP_PLANE = 0.12
STEP_CROSS = 0.15

HALO = -(-(ISTEPS - 1) // 8) * 8

VMEM = pl.BlockSpec(memory_space=pltpu.VMEM)


def spread_kernel(layers, inner_rows, blocks, dest_ref, pos_ref, flow_ref, conf_ref, out_ref):
    groups = out_ref.shape[0]
    count, width = conf_ref.shape
    place = pos_ref[...]
    layer = place // (inner_rows * blocks)
    inner_row = place // blocks % inner_rows
    column_block = place % blocks
    slot = (dest_ref[...] * layers + layer) * inner_rows + inner_row
    slots = groups * layers * inner_rows
    conf = conf_ref[...]
    terms = [flow_ref[pl.ds(c, count, stride=2), :] * conf for c in range(2)] + [conf]
    rest = jnp.concatenate(terms, axis=1)
    parts = []
    for _ in range(3):
        parts.append(rest.astype(jnp.bfloat16))
        rest = rest - parts[-1].astype(jnp.float32)
    numbers = lax.broadcasted_iota(jnp.int32, (slots, count), 0)
    for b in range(blocks):
        key = jnp.where(column_block == b, slot, -1)
        hit = jnp.where(numbers == key, 1.0, 0.0).astype(jnp.bfloat16)
        total = sum(jnp.dot(hit, part, preferred_element_type=jnp.float32) for part in reversed(parts))
        for o in range(groups):
            for l in range(layers):
                start = (o * layers + l) * inner_rows
                for c in range(3):
                    out_ref[o, c, l, :, b * width : (b + 1) * width] = total[
                        start : start + inner_rows, c * width : (c + 1) * width
                    ]


def shifted(blocks, lane, width):
    ahead = [pltpu.roll(x, width - 1, 1) for x in blocks]
    behind = [pltpu.roll(x, 1, 1) for x in blocks]
    zero = jnp.zeros_like(blocks[0])
    right = [jnp.where(lane == width - 1, after, own) for own, after in zip(ahead, ahead[1:] + [zero])]
    left = [jnp.where(lane == 0, before, own) for own, before in zip(behind, [zero] + behind[:-1])]
    return left, right


def plane_kernel(force_ref, stiff_ref, before_ref, after_ref, out_ref):
    _, layers, rows, columns = force_ref.shape
    groups = out_ref.shape[0]
    inner_rows = rows // groups
    width = 128
    total = rows + 2 * HALO
    lane = lax.broadcasted_iota(jnp.int32, (total, width), 1)
    spans = [slice(i * width, (i + 1) * width) for i in range(columns // width)]
    for l in range(layers):
        spring, keep = [], []
        for span in spans:
            k = STEP_PLANE * jnp.concatenate(
                [before_ref[2, l, :, span], stiff_ref[l, :, span], after_ref[2, l, :, span]], axis=0
            )
            spring.append(k)
            keep.append(1.0 - 4.0 * k)
        for c in range(2):
            push = [
                STEP_PLANE
                * jnp.concatenate(
                    [before_ref[c, l, :, span], force_ref[c, l, :, span], after_ref[c, l, :, span]], axis=0
                )
                for span in spans
            ]
            field = push
            for step in range(1, ISTEPS):
                left, right = shifted(field, lane, width)
                field = [
                    k * (pltpu.roll(x, 1, 0) + pltpu.roll(x, total - 1, 0) + a + b) + (g * x + f)
                    for x, a, b, k, g, f in zip(field, left, right, spring, keep, push)
                ]
            for span, x in zip(spans, field):
                for o in range(groups):
                    start = HALO + o * inner_rows
                    out_ref[o, c, l, :, span] = x[start : start + inner_rows]


def cross_kernel(moved_ref, forces_ref, stiff_ref, out_ref):
    groups, _, layers, inner_rows, columns = moved_ref.shape
    sections = groups * layers
    width = 128
    zero = jnp.zeros((1, inner_rows, width), jnp.float32)
    for i in range(columns // width):
        span = slice(i * width, (i + 1) * width)

        def channel(ref, c):
            return ref[:, c, :, :, span].reshape(sections, inner_rows, width)

        spring = STEP_CROSS * stiff_ref[:, :, span]
        weight = STEP_CROSS * channel(forces_ref, 2)
        for c in range(2):
            pull = STEP_CROSS * channel(forces_ref, c)
            field = channel(moved_ref, c)
            for step in range(ZSTEPS):
                rise = field - jnp.concatenate([zero, field[:-1]], axis=0)
                rise_above = jnp.concatenate([rise[1:], -field[-1:]], axis=0)
                stretch = pull - weight * rise
                stretch_above = jnp.concatenate([stretch[1:], zero], axis=0)
                field = field + (spring * (rise_above - rise) + (stretch - stretch_above))
            out_ref[c, :, :, span] = field


def per_device(
    in_plane_force, stiffness, stiffness_z, patch_dest, patch_pos, patch_flow, patch_conf
):
    groups = lax.axis_size("sec")
    tiles = lax.axis_size("tile")
    layers, rows, columns = stiffness.shape
    inner_rows = rows // groups
    width = patch_flow.shape[-1]
    blocks = columns // width
    count = patch_pos.shape[2]
    up = [(i, i + 1) for i in range(tiles - 1)]
    down = [(j, i) for i, j in up]

    def edge(start):
        return jnp.concatenate(
            [in_plane_force[:, :, start : start + HALO], stiffness[None, :, start : start + HALO]], axis=0
        )

    before = lax.ppermute(edge(rows - HALO), "tile", up)
    after = lax.ppermute(edge(0), "tile", down)
    forces = pl.pallas_call(
        functools.partial(spread_kernel, layers, inner_rows, blocks),
        out_shape=jax.ShapeDtypeStruct((groups, 3, layers, inner_rows, columns), jnp.float32),
        in_specs=[VMEM] * 4,
        out_specs=VMEM,
        cost_estimate=pl.CostEstimate(flops=6 * 256 * 256 * 384, bytes_accessed=800000, transcendentals=0),
        name="spread_patches",
    )(
        patch_dest.reshape(1, count),
        patch_pos.reshape(1, count),
        patch_flow.reshape(count * 2, width),
        patch_conf.reshape(count, width),
    )
    forces = lax.all_to_all(forces, "sec", split_axis=0, concat_axis=0, tiled=True)
    planar = pl.pallas_call(
        plane_kernel,
        out_shape=jax.ShapeDtypeStruct((groups, 2, layers, inner_rows, columns), jnp.float32),
        in_specs=[VMEM] * 4,
        out_specs=VMEM,
        cost_estimate=pl.CostEstimate(flops=10000000, bytes_accessed=800000, transcendentals=0),
        name="plane_steps",
    )(in_plane_force, stiffness, before, after)
    moved = lax.all_to_all(planar, "sec", split_axis=0, concat_axis=0, tiled=True)
    return pl.pallas_call(
        cross_kernel,
        out_shape=jax.ShapeDtypeStruct((2, groups * layers, inner_rows, columns), jnp.float32),
        in_specs=[VMEM] * 3,
        out_specs=VMEM,
        cost_estimate=pl.CostEstimate(flops=10000000, bytes_accessed=800000, transcendentals=0),
        name="cross_steps",
    )(moved, forces, stiffness_z)


def solution(mesh):
    placed = (
        P(None, "sec", "tile", None),
        P("sec", "tile", None),
        P(None, ("tile", "sec"), None),
        P("sec", "tile", None, None),
        P("sec", "tile", None),
        P("sec", "tile", None, None, None),
        P("sec", "tile", None, None),
    )
    return jax.shard_map(
        per_device,
        mesh=mesh,
        in_specs=placed,
        out_specs=P(None, None, ("tile", "sec"), None),
        check_vma=False,
    )
```

```python
import functools

import jax
import jax.numpy as jnp
from jax import lax
from jax.experimental import pallas as pl
from jax.experimental.pallas import tpu as pltpu
from jax.sharding import PartitionSpec as P

ISTEPS = 8
ZSTEPS = 8


STEP_PLANE = 0.12
STEP_CROSS = 0.15

HALO = -(-(ISTEPS - 1) // 8) * 8

VMEM = pl.BlockSpec(memory_space=pltpu.VMEM)
HBM = pl.BlockSpec(memory_space=pltpu.HBM)
ANY = pl.BlockSpec(memory_space=pl.ANY)


def spread_kernel(layers, inner_rows, blocks, dest_ref, pos_ref, flow_ref, conf_ref, out_ref):
    groups = out_ref.shape[0]
    count, width = conf_ref.shape
    place = pos_ref[...]
    layer = place // (inner_rows * blocks)
    inner_row = place // blocks % inner_rows
    column_block = place % blocks
    slot = (dest_ref[...] * layers + layer) * inner_rows + inner_row
    slots = groups * layers * inner_rows
    conf = conf_ref[...]
    terms = [flow_ref[pl.ds(c, count, stride=2), :] * conf for c in range(2)] + [conf]
    rest = jnp.concatenate(terms, axis=1)
    parts = []
    for _ in range(3):
        parts.append(rest.astype(jnp.bfloat16))
        rest = rest - parts[-1].astype(jnp.float32)
    numbers = lax.broadcasted_iota(jnp.int32, (slots, count), 0)
    for b in range(blocks):
        key = jnp.where(column_block == b, slot, -1)
        hit = jnp.where(numbers == key, 1.0, 0.0).astype(jnp.bfloat16)
        total = sum(jnp.dot(hit, part, preferred_element_type=jnp.float32) for part in reversed(parts))
        for o in range(groups):
            for l in range(layers):
                start = (o * layers + l) * inner_rows
                for c in range(3):
                    out_ref[o, c, l, :, b * width : (b + 1) * width] = total[
                        start : start + inner_rows, c * width : (c + 1) * width
                    ]


def shifted(blocks, lane, width):
    ahead = [pltpu.roll(x, width - 1, 1) for x in blocks]
    behind = [pltpu.roll(x, 1, 1) for x in blocks]
    zero = jnp.zeros_like(blocks[0])
    right = [jnp.where(lane == width - 1, after, own) for own, after in zip(ahead, ahead[1:] + [zero])]
    left = [jnp.where(lane == 0, before, own) for own, before in zip(behind, [zero] + behind[:-1])]
    return left, right


def start_all(copies):
    for copy in copies:
        copy.start()
    return copies


def wait_all(copies):
    for copy in copies:
        copy.wait()


def edge_kernel(force_ref, stiff_ref, first_ref, last_ref, sems):
    rows = stiff_ref.shape[1]
    copies = []
    for start, out_ref in ((0, first_ref), (rows - HALO, last_ref)):
        span = pl.ds(start, HALO)
        copies.append(pltpu.make_async_copy(force_ref.at[:, :, span], out_ref.at[pl.ds(0, 2)], sems.at[len(copies)]))
        copies.append(pltpu.make_async_copy(stiff_ref.at[:, span], out_ref.at[2], sems.at[len(copies)]))
    wait_all(start_all(copies))


def plane_kernel(force_ref, stiff_ref, before_ref, after_ref, order_ref, out_ref, held, done, sems):
    _, layers, rows, columns = force_ref.shape
    groups = out_ref.shape[0]
    inner_rows = rows // groups
    width = held.shape[-1]
    total = rows + 2 * HALO
    stride = total // 8
    blocks = columns // width
    copies = []
    for b in range(blocks):
        span = pl.ds(b * width, width)
        for source, start, length in (
            (before_ref.at[:, :, :, span], 0, HALO),
            (after_ref.at[:, :, :, span], HALO + rows, HALO),
        ):
            target = held.at[:, :, b, pl.ds(start, length)]
            copies.append(pltpu.make_async_copy(source, target, sems.at[len(copies)]))
        own = pl.ds(HALO, rows)
        copies.append(
            pltpu.make_async_copy(force_ref.at[:, :, :, span], held.at[pl.ds(0, 2), :, b, own], sems.at[len(copies)])
        )
        copies.append(pltpu.make_async_copy(stiff_ref.at[:, :, span], held.at[2, :, b, own], sems.at[len(copies)]))
    wait_all(start_all(copies))
    lane = lax.broadcasted_iota(jnp.int32, (8, width), 1)

    def rows_of(c, l):
        return [
            [STEP_PLANE * held[c, l, b, pl.ds(j, 8, stride=stride), :] for b in range(blocks)] for j in range(stride)
        ]

    for l in range(layers):
        spring = rows_of(2, l)
        keep = [[1.0 - 4.0 * k for k in row] for row in spring]
        for c in range(2):
            push = rows_of(c, l)
            field = push
            for step in range(1, ISTEPS):
                above = [[pltpu.roll(x, 1, 0) for x in field[-1]]] + field[:-1]
                below = field[1:] + [[pltpu.roll(x, 7, 0) for x in field[0]]]
                moved = []
                for j in range(stride):
                    left, right = shifted(field[j], lane, width)
                    moved.append(
                        [
                            k * ((u + d) + (a + b)) + (g * x + f)
                            for x, u, d, a, b, k, g, f in zip(
                                field[j], above[j], below[j], left, right, spring[j], keep[j], push[j]
                            )
                        ]
                    )
                field = moved
            for j in range(stride):
                for b in range(blocks):
                    done[c, l, b, pl.ds(j, 8, stride=stride), :] = field[j][b]
            for b in range(blocks):
                for o in range(groups):
                    out_ref[o, c, l, :, b * width : (b + 1) * width] = done[
                        c, l, b, HALO + o * inner_rows : HALO + (o + 1) * inner_rows, :
                    ]


def cross_kernel(moved_ref, forces_ref, stiff_ref, out_ref, held, spring_held, result, sems, out_sems):
    groups, _, layers, inner_rows, columns = moved_ref.shape
    sections = groups * layers
    width = held.shape[-1]
    blocks = columns // width
    zero = jnp.zeros((1, inner_rows, width), jnp.float32)
    copies = []
    for b in range(blocks):
        span = pl.ds(b * width, width)
        pieces = [(stiff_ref.at[:, :, span], spring_held.at[b])]
        pieces += [(forces_ref.at[:, c, :, :, span], held.at[b, 2 + c]) for c in (2, 0)]
        pieces += [(moved_ref.at[:, 0, :, :, span], held.at[b, 0])]
        pieces += [(forces_ref.at[:, 1, :, :, span], held.at[b, 3]), (moved_ref.at[:, 1, :, :, span], held.at[b, 1])]
        copies.append(
            start_all([pltpu.make_async_copy(source, target, sems.at[b, i]) for i, (source, target) in enumerate(pieces)])
        )
    outgoing = []
    for b in range(blocks):
        span = pl.ds(b * width, width)

        def channel(c):
            return held[b, c].reshape(sections, inner_rows, width)

        wait_all(copies[b][:4])
        spring = STEP_CROSS * spring_held[b]
        weight = STEP_CROSS * channel(4)
        for c in range(2):
            if c:
                wait_all(copies[b][4:])
            pull = STEP_CROSS * channel(2 + c)
            field = channel(c)
            for step in range(ZSTEPS):
                rise = field - jnp.concatenate([zero, field[:-1]], axis=0)
                rise_above = jnp.concatenate([rise[1:], -field[-1:]], axis=0)
                stretch = pull - weight * rise
                stretch_above = jnp.concatenate([stretch[1:], zero], axis=0)
                field = field + (spring * (rise_above - rise) + (stretch - stretch_above))
            result[b, c] = field
            outgoing += start_all(
                [pltpu.make_async_copy(result.at[b, c], out_ref.at[c, :, :, span], out_sems.at[b, c])]
            )
    wait_all(outgoing)


def per_device(
    in_plane_force, stiffness, stiffness_z, patch_dest, patch_pos, patch_flow, patch_conf
):
    groups = lax.axis_size("sec")
    tiles = lax.axis_size("tile")
    layers, rows, columns = stiffness.shape
    inner_rows = rows // groups
    width = patch_flow.shape[-1]
    blocks = columns // width
    count = patch_pos.shape[2]
    up = [(i, i + 1) for i in range(tiles - 1)]
    down = [(j, i) for i, j in up]

    edge_shape = jax.ShapeDtypeStruct((3, layers, HALO, columns), jnp.float32)
    first, last = pl.pallas_call(
        edge_kernel,
        out_shape=[edge_shape] * 2,
        in_specs=[HBM] * 2,
        out_specs=[ANY] * 2,
        scratch_shapes=[pltpu.SemaphoreType.DMA((4,))],
        cost_estimate=pl.CostEstimate(flops=0, bytes_accessed=200000, transcendentals=0),
        name="pack_edges",
    )(in_plane_force, stiffness)
    before = lax.ppermute(last, "tile", up)
    after = lax.ppermute(first, "tile", down)
    forces = pl.pallas_call(
        functools.partial(spread_kernel, layers, inner_rows, blocks),
        out_shape=jax.ShapeDtypeStruct((groups, 3, layers, inner_rows, columns), jnp.float32),
        in_specs=[VMEM] * 4,
        out_specs=VMEM,
        cost_estimate=pl.CostEstimate(flops=6 * 256 * 256 * 384, bytes_accessed=800000, transcendentals=0),
        name="spread_patches",
    )(
        patch_dest.reshape(1, count),
        patch_pos.reshape(1, count),
        patch_flow.reshape(count * 2, width),
        patch_conf.reshape(count, width),
    )
    moved_forces = lax.all_to_all(forces, "sec", split_axis=0, concat_axis=0, tiled=True)
    planar = pl.pallas_call(
        plane_kernel,
        out_shape=jax.ShapeDtypeStruct((groups, 2, layers, inner_rows, columns), jnp.float32),
        in_specs=[HBM] * 2 + [ANY] * 3,
        out_specs=VMEM,
        scratch_shapes=[
            pltpu.VMEM((3, layers, blocks, rows + 2 * HALO, width), jnp.float32),
            pltpu.VMEM((2, layers, blocks, rows + 2 * HALO, width), jnp.float32),
            pltpu.SemaphoreType.DMA((4 * blocks,)),
        ],
        cost_estimate=pl.CostEstimate(flops=10000000, bytes_accessed=10000000, transcendentals=0),
        name="plane_steps",
    )(in_plane_force, stiffness, before, after, forces)
    moved = lax.all_to_all(planar, "sec", split_axis=0, concat_axis=0, tiled=True)
    return pl.pallas_call(
        cross_kernel,
        out_shape=jax.ShapeDtypeStruct((2, groups * layers, inner_rows, columns), jnp.float32),
        in_specs=[ANY] * 2 + [HBM],
        out_specs=HBM,
        scratch_shapes=[
            pltpu.VMEM((blocks, 5, groups, layers, inner_rows, width), jnp.float32),
            pltpu.VMEM((blocks, groups * layers, inner_rows, width), jnp.float32),
            pltpu.VMEM((blocks, 2, groups * layers, inner_rows, width), jnp.float32),
            pltpu.SemaphoreType.DMA((blocks, 6)),
            pltpu.SemaphoreType.DMA((blocks, 2)),
        ],
        cost_estimate=pl.CostEstimate(flops=10000000, bytes_accessed=800000, transcendentals=0),
        name="cross_steps",
    )(moved, moved_forces, stiffness_z)


def solution(mesh):
    placed = (
        P(None, "sec", "tile", None),
        P("sec", "tile", None),
        P(None, ("tile", "sec"), None),
        P("sec", "tile", None, None),
        P("sec", "tile", None),
        P("sec", "tile", None, None, None),
        P("sec", "tile", None, None),
    )
    return jax.shard_map(
        per_device,
        mesh=mesh,
        in_specs=placed,
        out_specs=P(None, None, ("tile", "sec"), None),
        check_vma=False,
    )
```

```python
import functools

import jax
import jax.numpy as jnp
from jax import lax
from jax.experimental import pallas as pl
from jax.experimental.pallas import tpu as pltpu
from jax.sharding import PartitionSpec as P

ISTEPS = 8
ZSTEPS = 8


STEP_PLANE = 0.12
STEP_CROSS = 0.15

HALO = -(-(ISTEPS - 1) // 8) * 8

VMEM = pl.BlockSpec(memory_space=pltpu.VMEM)
LIMIT = pltpu.CompilerParams(vmem_limit_bytes=8 * 1024 * 1024)
ANY = pl.BlockSpec(memory_space=pl.ANY)


def spread_kernel(layers, inner_rows, blocks, dest_ref, pos_ref, flow_ref, conf_ref, out_ref):
    groups = out_ref.shape[0]
    count, width = conf_ref.shape
    place = pos_ref[...]
    layer = place // (inner_rows * blocks)
    inner_row = place // blocks % inner_rows
    column_block = place % blocks
    slot = (dest_ref[...] * layers + layer) * inner_rows + inner_row
    slots = groups * layers * inner_rows
    conf = conf_ref[...]
    terms = [flow_ref[pl.ds(c, count, stride=2), :] * conf for c in range(2)] + [conf]
    rest = jnp.concatenate(terms, axis=1)
    parts = []
    for _ in range(3):
        parts.append(rest.astype(jnp.bfloat16))
        rest = rest - parts[-1].astype(jnp.float32)
    numbers = lax.broadcasted_iota(jnp.int32, (slots, count), 0)
    for b in range(blocks):
        key = jnp.where(column_block == b, slot, -1)
        hit = jnp.where(numbers == key, 1.0, 0.0).astype(jnp.bfloat16)
        total = sum(jnp.dot(hit, part, preferred_element_type=jnp.float32) for part in reversed(parts))
        for o in range(groups):
            for l in range(layers):
                start = (o * layers + l) * inner_rows
                for c in range(3):
                    out_ref[o, c, l, :, b * width : (b + 1) * width] = total[
                        start : start + inner_rows, c * width : (c + 1) * width
                    ]


def shifted(blocks, lane, width):
    ahead = [pltpu.roll(x, width - 1, 1) for x in blocks]
    behind = [pltpu.roll(x, 1, 1) for x in blocks]
    zero = jnp.zeros_like(blocks[0])
    right = [jnp.where(lane == width - 1, after, own) for own, after in zip(ahead, ahead[1:] + [zero])]
    left = [jnp.where(lane == 0, before, own) for own, before in zip(behind, [zero] + behind[:-1])]
    return left, right


def start_all(copies):
    for copy in copies:
        copy.start()
    return copies


def wait_all(copies):
    for copy in copies:
        copy.wait()


def edge_kernel(force_ref, stiff_ref, first_ref, last_ref, sems):
    rows = stiff_ref.shape[1]
    copies = []
    for start, out_ref in ((0, first_ref), (rows - HALO, last_ref)):
        span = pl.ds(start, HALO)
        copies.append(pltpu.make_async_copy(force_ref.at[:, :, span], out_ref.at[pl.ds(0, 2)], sems.at[len(copies)]))
        copies.append(pltpu.make_async_copy(stiff_ref.at[:, span], out_ref.at[2], sems.at[len(copies)]))
    wait_all(start_all(copies))


def plane_kernel(force_ref, stiff_ref, before_ref, after_ref, forces_ref, out_ref, held, coefs, done, sems):
    _, layers, rows, columns = force_ref.shape
    groups = out_ref.shape[0]
    inner_rows = rows // groups
    width = held.shape[-1]
    total = rows + 2 * HALO
    stride = total // 8
    blocks = columns // width
    copies = []
    for b in range(blocks):
        span = pl.ds(b * width, width)
        for source, start, length in (
            (before_ref.at[:, :, :, span], 0, HALO),
            (after_ref.at[:, :, :, span], HALO + rows, HALO),
        ):
            target = held.at[:, :, b, pl.ds(start, length)]
            copies.append(pltpu.make_async_copy(source, target, sems.at[len(copies)]))
        own = pl.ds(HALO, rows)
        copies.append(
            pltpu.make_async_copy(force_ref.at[:, :, :, span], held.at[pl.ds(0, 2), :, b, own], sems.at[len(copies)])
        )
        copies.append(pltpu.make_async_copy(stiff_ref.at[:, :, span], held.at[2, :, b, own], sems.at[len(copies)]))
    start_all(copies)
    passed = start_all([pltpu.make_async_copy(forces_ref, out_ref.at[:, pl.ds(2, 3)], sems.at[len(copies)])])
    wait_all(copies)
    lane = lax.broadcasted_iota(jnp.int32, (8, width), 1)
    places = [(j, b) for j in range(stride) for b in range(blocks)]

    def one(index, carry):
        l, c = index // 2, index % 2
        field = []
        for n, (j, b) in enumerate(places):
            k = STEP_PLANE * held[2, l, b, pl.ds(j, 8, stride=stride), :]
            f = STEP_PLANE * held[c, l, b, pl.ds(j, 8, stride=stride), :]
            coefs[0, n] = k
            coefs[1, n] = 1.0 - 4.0 * k
            coefs[2, n] = f
            field.append(f)

        def step(_, flat):
            field = [flat[j * blocks : (j + 1) * blocks] for j in range(stride)]
            above = [[pltpu.roll(x, 1, 0) for x in field[-1]]] + field[:-1]
            below = field[1:] + [[pltpu.roll(x, 7, 0) for x in field[0]]]
            moved = []
            for j in range(stride):
                left, right = shifted(field[j], lane, width)
                for b in range(blocks):
                    n = len(moved)
                    near = (above[j][b] + below[j][b]) + (left[b] + right[b])
                    moved.append(coefs[0, n] * near + (coefs[1, n] * field[j][b] + coefs[2, n]))
            return moved

        field = lax.fori_loop(1, ISTEPS, step, field)
        for x, (j, b) in zip(field, places):
            done[b, pl.ds(j, 8, stride=stride), :] = x
        for b in range(blocks):
            for o in range(groups):
                out_ref[o, c, l, :, b * width : (b + 1) * width] = done[
                    b, HALO + o * inner_rows : HALO + (o + 1) * inner_rows, :
                ]
        return carry

    lax.fori_loop(0, 2 * layers, one, 0)
    wait_all(passed)


def cross_kernel(moved_ref, stiff_ref, out_ref, result, sems):
    groups, _, layers, inner_rows, columns = moved_ref.shape
    sections = groups * layers
    width = result.shape[-1]
    blocks = columns // width
    zero = jnp.zeros((1, inner_rows, width), jnp.float32)

    def outgoing(index):
        b, c = index // 2, index % 2
        span = pl.ds(pl.multiple_of(b * width, width), width)
        return pltpu.make_async_copy(result.at[index], out_ref.at[c, :, :, span], sems.at[index])

    def one(index, carry):
        b, c = index // 2, index % 2
        span = pl.ds(pl.multiple_of(b * width, width), width)

        def channel(c):
            return moved_ref[:, c, :, :, span].reshape(sections, inner_rows, width)

        spring = STEP_CROSS * stiff_ref[:, :, span]
        weight = STEP_CROSS * channel(4)
        pull = STEP_CROSS * channel(2 + c)

        def step(_, field):
            rise = field - jnp.concatenate([zero, field[:-1]], axis=0)
            rise_above = jnp.concatenate([rise[1:], -field[-1:]], axis=0)
            stretch = pull - weight * rise
            stretch_above = jnp.concatenate([stretch[1:], zero], axis=0)
            return field + (spring * (rise_above - rise) + (stretch - stretch_above))

        result[index] = lax.fori_loop(0, ZSTEPS, step, channel(c))
        outgoing(index).start()
        return carry

    lax.fori_loop(0, 2 * blocks, one, 0)
    for index in range(2 * blocks):
        outgoing(index).wait()


def per_device(
    in_plane_force, stiffness, stiffness_z, patch_dest, patch_pos, patch_flow, patch_conf
):
    groups = lax.axis_size("sec")
    tiles = lax.axis_size("tile")
    layers, rows, columns = stiffness.shape
    inner_rows = rows // groups
    width = patch_flow.shape[-1]
    blocks = columns // width
    count = patch_pos.shape[2]
    up = [(i, i + 1) for i in range(tiles - 1)]
    down = [(j, i) for i, j in up]

    edge_shape = jax.ShapeDtypeStruct((3, layers, HALO, columns), jnp.float32)
    first, last = pl.pallas_call(
        edge_kernel,
        out_shape=[edge_shape] * 2,
        in_specs=[ANY] * 2,
        out_specs=[ANY] * 2,
        scratch_shapes=[pltpu.SemaphoreType.DMA((4,))],
        compiler_params=LIMIT,
        cost_estimate=pl.CostEstimate(flops=0, bytes_accessed=200000, transcendentals=0),
        name="pack_edges",
    )(in_plane_force, stiffness)
    before = lax.ppermute(last, "tile", up)
    after = lax.ppermute(first, "tile", down)
    forces = pl.pallas_call(
        functools.partial(spread_kernel, layers, inner_rows, blocks),
        out_shape=jax.ShapeDtypeStruct((groups, 3, layers, inner_rows, columns), jnp.float32),
        in_specs=[VMEM] * 4,
        out_specs=VMEM,
        compiler_params=LIMIT,
        cost_estimate=pl.CostEstimate(flops=6 * 256 * 256 * 384, bytes_accessed=800000, transcendentals=0),
        name="spread_patches",
    )(
        patch_dest.reshape(1, count),
        patch_pos.reshape(1, count),
        patch_flow.reshape(count * 2, width),
        patch_conf.reshape(count, width),
    )
    mixed = pl.pallas_call(
        plane_kernel,
        out_shape=jax.ShapeDtypeStruct((groups, 5, layers, inner_rows, columns), jnp.float32),
        in_specs=[ANY] * 5,
        out_specs=VMEM,
        scratch_shapes=[
            pltpu.VMEM((3, layers, blocks, rows + 2 * HALO, width), jnp.float32),
            pltpu.VMEM((3, (rows + 2 * HALO) // 8 * blocks, 8, width), jnp.float32),
            pltpu.VMEM((blocks, rows + 2 * HALO, width), jnp.float32),
            pltpu.SemaphoreType.DMA((4 * blocks + 1,)),
        ],
        compiler_params=LIMIT,
        cost_estimate=pl.CostEstimate(flops=10000000, bytes_accessed=10000000, transcendentals=0),
        name="plane_steps",
    )(in_plane_force, stiffness, before, after, forces)
    moved = lax.all_to_all(mixed, "sec", split_axis=0, concat_axis=0, tiled=True)
    return pl.pallas_call(
        cross_kernel,
        out_shape=jax.ShapeDtypeStruct((2, groups * layers, inner_rows, columns), jnp.float32),
        in_specs=[VMEM] * 2,
        out_specs=ANY,
        scratch_shapes=[
            pltpu.VMEM((2 * blocks, groups * layers, inner_rows, width), jnp.float32),
            pltpu.SemaphoreType.DMA((2 * blocks,)),
        ],
        compiler_params=LIMIT,
        cost_estimate=pl.CostEstimate(flops=10000000, bytes_accessed=800000, transcendentals=0),
        name="cross_steps",
    )(moved, stiffness_z)


def solution(mesh):
    placed = (
        P(None, "sec", "tile", None),
        P("sec", "tile", None),
        P(None, ("tile", "sec"), None),
        P("sec", "tile", None, None),
        P("sec", "tile", None),
        P("sec", "tile", None, None, None),
        P("sec", "tile", None, None),
    )
    return jax.shard_map(
        per_device,
        mesh=mesh,
        in_specs=placed,
        out_specs=P(None, None, ("tile", "sec"), None),
        check_vma=False,
    )
```

```python
import functools

import jax
import jax.numpy as jnp
from jax import lax
from jax.experimental import pallas as pl
from jax.experimental.pallas import tpu as pltpu
from jax.sharding import PartitionSpec as P

ISTEPS = 8
ZSTEPS = 8


STEP_PLANE = 0.12
STEP_CROSS = 0.15

HALO = -(-(ISTEPS - 1) // 8) * 8

VMEM = pl.BlockSpec(memory_space=pltpu.VMEM)
LIMIT = pltpu.CompilerParams(vmem_limit_bytes=8 * 1024 * 1024)
ANY = pl.BlockSpec(memory_space=pl.ANY)


def spread_kernel(layers, inner_rows, blocks, dest_ref, pos_ref, flow_ref, conf_ref, out_ref):
    groups = out_ref.shape[0]
    count, width = conf_ref.shape
    place = pos_ref[...]
    layer = place // (inner_rows * blocks)
    inner_row = place // blocks % inner_rows
    column_block = place % blocks
    slot = (dest_ref[...] * layers + layer) * inner_rows + inner_row
    slots = groups * layers * inner_rows
    conf = conf_ref[...]
    terms = [flow_ref[pl.ds(c, count, stride=2), :] * conf for c in range(2)] + [conf]
    rest = jnp.concatenate(terms, axis=1)
    parts = []
    for _ in range(3):
        parts.append(rest.astype(jnp.bfloat16))
        rest = rest - parts[-1].astype(jnp.float32)
    numbers = lax.broadcasted_iota(jnp.int32, (slots, count), 0)
    for b in range(blocks):
        key = jnp.where(column_block == b, slot, -1)
        hit = jnp.where(numbers == key, 1.0, 0.0).astype(jnp.bfloat16)
        total = sum(jnp.dot(hit, part, preferred_element_type=jnp.float32) for part in reversed(parts))
        for o in range(groups):
            for l in range(layers):
                start = (o * layers + l) * inner_rows
                for c in range(3):
                    out_ref[o, c, l, :, b * width : (b + 1) * width] = total[
                        start : start + inner_rows, c * width : (c + 1) * width
                    ]


def shifted(blocks, lane, width):
    ahead = [pltpu.roll(x, width - 1, 1) for x in blocks]
    behind = [pltpu.roll(x, 1, 1) for x in blocks]
    zero = jnp.zeros_like(blocks[0])
    right = [jnp.where(lane == width - 1, after, own) for own, after in zip(ahead, ahead[1:] + [zero])]
    left = [jnp.where(lane == 0, before, own) for own, before in zip(behind, [zero] + behind[:-1])]
    return left, right


def edge_kernel(force_ref, stiff_ref, first_ref, last_ref, sems):
    rows = stiff_ref.shape[1]
    copies = []
    for start, out_ref in ((0, first_ref), (rows - HALO, last_ref)):
        span = pl.ds(start, HALO)
        copies.append(pltpu.make_async_copy(force_ref.at[:, :, span], out_ref.at[pl.ds(0, 2)], sems.at[len(copies)]))
        copies.append(pltpu.make_async_copy(stiff_ref.at[:, span], out_ref.at[2], sems.at[len(copies)]))
    for copy in copies:
        copy.start()
    for copy in copies:
        copy.wait()


def plane_kernel(force_ref, stiff_ref, before_ref, after_ref, order_ref, out_ref, held, springs, keeps, pushes, even, odd):
    _, layers, rows, columns = force_ref.shape
    groups = out_ref.shape[0]
    inner_rows = rows // groups
    width = held.shape[-1]
    stride = held.shape[-2] // 8
    blocks = columns // width
    lane = lax.broadcasted_iota(jnp.int32, (8, width), 1)
    places = [(j, b) for j in range(stride) for b in range(blocks)]

    for l in range(layers):
        for c in (2, 0, 1):
            for b in range(blocks):
                span = slice(b * width, (b + 1) * width)
                held[c, l, b, :HALO] = before_ref[c, l, :, span]
                held[c, l, b, HALO : HALO + rows] = stiff_ref[l, :, span] if c == 2 else force_ref[c, l, :, span]
                held[c, l, b, HALO + rows :] = after_ref[c, l, :, span]
            for n, (j, b) in enumerate(places):
                part = STEP_PLANE * held[c, l, b, pl.ds(j, 8, stride=stride), :]
                if c == 2:
                    springs[l, n] = part
                    keeps[l, n] = 1.0 - 4.0 * part
                else:
                    pushes[l, c, n] = part

    def step(source, store):
        for l in range(layers):
            for c in range(2):
                field = [[source[l, c, j * blocks + b] for b in range(blocks)] for j in range(stride)]
                above = [[pltpu.roll(x, 1, 0) for x in field[-1]]] + field[:-1]
                below = field[1:] + [[pltpu.roll(x, 7, 0) for x in field[0]]]
                for j in range(stride):
                    left, right = shifted(field[j], lane, width)
                    for b in range(blocks):
                        n = j * blocks + b
                        near = (above[j][b] + below[j][b]) + (left[b] + right[b])
                        store(l, c, n, springs[l, n] * near + (keeps[l, n] * field[j][b] + pushes[l, c, n]))

    def to(target):
        def store(l, c, n, value):
            target[l, c, n] = value

        return store

    def to_rows(l, c, n, value):
        j, b = places[n]
        held[c, l, b, pl.ds(j, 8, stride=stride), :] = value

    def pair(_, carry):
        step(even, to(odd))
        step(odd, to(even))
        return carry

    inner = ISTEPS - 2
    source = pushes
    if inner % 2:
        step(source, to(even))
        source = even
    elif inner:
        step(source, to(odd))
        step(odd, to(even))
        source = even
    lax.fori_loop(0, (inner - 1) // 2, pair, 0)
    step(source, to_rows)
    for c in range(2):
        for l in range(layers):
            for b in range(blocks):
                for o in range(groups):
                    out_ref[o, c, l, :, b * width : (b + 1) * width] = held[
                        c, l, b, HALO + o * inner_rows : HALO + (o + 1) * inner_rows, :
                    ]


def tie_kernel(passed_ref, first_ref, out_ref):
    del passed_ref, first_ref, out_ref


def cross_kernel(moved_ref, forces_ref, stiff_ref, out_ref, result, sems):
    groups, _, layers, inner_rows, columns = moved_ref.shape
    sections = groups * layers
    width = result.shape[-1]
    blocks = columns // width
    zero = jnp.zeros((1, inner_rows, width), jnp.float32)

    def outgoing(index):
        b, c = index // 2, index % 2
        span = pl.ds(pl.multiple_of(b * width, width), width)
        return pltpu.make_async_copy(result.at[index], out_ref.at[c, :, :, span], sems.at[index])

    def one(index, carry):
        b, c = index // 2, index % 2
        span = pl.ds(pl.multiple_of(b * width, width), width)

        def channel(ref, c):
            return ref[:, c, :, :, span].reshape(sections, inner_rows, width)

        spring = STEP_CROSS * stiff_ref[:, :, span]
        weight = STEP_CROSS * channel(forces_ref, 2)
        pull = STEP_CROSS * channel(forces_ref, c)

        def step(_, field):
            rise = field - jnp.concatenate([zero, field[:-1]], axis=0)
            rise_above = jnp.concatenate([rise[1:], -field[-1:]], axis=0)
            stretch = pull - weight * rise
            stretch_above = jnp.concatenate([stretch[1:], zero], axis=0)
            return field + (spring * (rise_above - rise) + (stretch - stretch_above))

        result[index] = lax.fori_loop(0, ZSTEPS, step, channel(moved_ref, c))
        outgoing(index).start()
        return carry

    lax.fori_loop(0, 2 * blocks, one, 0)
    for index in range(2 * blocks):
        outgoing(index).wait()


def per_device(
    in_plane_force, stiffness, stiffness_z, patch_dest, patch_pos, patch_flow, patch_conf
):
    groups = lax.axis_size("sec")
    tiles = lax.axis_size("tile")
    layers, rows, columns = stiffness.shape
    inner_rows = rows // groups
    width = patch_flow.shape[-1]
    blocks = columns // width
    count = patch_pos.shape[2]
    up = [(i, i + 1) for i in range(tiles - 1)]
    down = [(j, i) for i, j in up]

    edge_shape = jax.ShapeDtypeStruct((3, layers, HALO, columns), jnp.float32)
    first, last = pl.pallas_call(
        edge_kernel,
        out_shape=[edge_shape] * 2,
        in_specs=[ANY] * 2,
        out_specs=[ANY] * 2,
        scratch_shapes=[pltpu.SemaphoreType.DMA((4,))],
        compiler_params=LIMIT,
        cost_estimate=pl.CostEstimate(flops=0, bytes_accessed=200000, transcendentals=0),
        name="pack_edges",
    )(in_plane_force, stiffness)
    before = lax.ppermute(last, "tile", up)
    after = lax.ppermute(first, "tile", down)
    forces = pl.pallas_call(
        functools.partial(spread_kernel, layers, inner_rows, blocks),
        out_shape=jax.ShapeDtypeStruct((groups, 3, layers, inner_rows, columns), jnp.float32),
        in_specs=[VMEM] * 4,
        out_specs=VMEM,
        compiler_params=LIMIT,
        cost_estimate=pl.CostEstimate(flops=6 * 256 * 256 * 384, bytes_accessed=800000, transcendentals=0),
        name="spread_patches",
    )(
        patch_dest.reshape(1, count),
        patch_pos.reshape(1, count),
        patch_flow.reshape(count * 2, width),
        patch_conf.reshape(count, width),
    )
    moved_forces = lax.all_to_all(forces, "sec", split_axis=0, concat_axis=0, tiled=True)
    planar_shape = jax.ShapeDtypeStruct((groups, 2, layers, inner_rows, columns), jnp.float32)
    parts = (rows + 2 * HALO) // 8 * blocks
    planar = pl.pallas_call(
        plane_kernel,
        out_shape=planar_shape,
        in_specs=[VMEM] * 4 + [ANY],
        out_specs=VMEM,
        scratch_shapes=[
            pltpu.VMEM((3, layers, blocks, rows + 2 * HALO, width), jnp.float32),
            pltpu.VMEM((layers, parts, 8, width), jnp.float32),
            pltpu.VMEM((layers, parts, 8, width), jnp.float32),
            pltpu.VMEM((layers, 2, parts, 8, width), jnp.float32),
            pltpu.VMEM((layers, 2, parts, 8, width), jnp.float32),
            pltpu.VMEM((layers, 2, parts, 8, width), jnp.float32),
        ],
        compiler_params=LIMIT,
        cost_estimate=pl.CostEstimate(flops=10000000, bytes_accessed=10000000, transcendentals=0),
        name="plane_steps",
    )(in_plane_force, stiffness, before, after, forces)
    planar = pl.pallas_call(
        tie_kernel,
        out_shape=planar_shape,
        in_specs=[ANY] * 2,
        out_specs=ANY,
        input_output_aliases={0: 0},
        compiler_params=LIMIT,
        name="forces_first",
    )(planar, moved_forces)
    moved = lax.all_to_all(planar, "sec", split_axis=0, concat_axis=0, tiled=True)
    return pl.pallas_call(
        cross_kernel,
        out_shape=jax.ShapeDtypeStruct((2, groups * layers, inner_rows, columns), jnp.float32),
        in_specs=[VMEM] * 3,
        out_specs=ANY,
        scratch_shapes=[
            pltpu.VMEM((2 * blocks, groups * layers, inner_rows, width), jnp.float32),
            pltpu.SemaphoreType.DMA((2 * blocks,)),
        ],
        compiler_params=LIMIT,
        cost_estimate=pl.CostEstimate(flops=10000000, bytes_accessed=800000, transcendentals=0),
        name="cross_steps",
    )(moved, moved_forces, stiffness_z)


def solution(mesh):
    placed = (
        P(None, "sec", "tile", None),
        P("sec", "tile", None),
        P(None, ("tile", "sec"), None),
        P("sec", "tile", None, None),
        P("sec", "tile", None),
        P("sec", "tile", None, None, None),
        P("sec", "tile", None, None),
    )
    return jax.shard_map(
        per_device,
        mesh=mesh,
        in_specs=placed,
        out_specs=P(None, None, ("tile", "sec"), None),
        check_vma=False,
    )
```

```python
import functools

import jax
import jax.numpy as jnp
from jax import lax
from jax.experimental import pallas as pl
from jax.experimental.pallas import tpu as pltpu
from jax.sharding import PartitionSpec as P

ISTEPS = 8
ZSTEPS = 8


STEP_PLANE = 0.12
STEP_CROSS = 0.15

HALO = -(-(ISTEPS - 1) // 8) * 8

VMEM = pl.BlockSpec(memory_space=pltpu.VMEM)
LIMIT = pltpu.CompilerParams(vmem_limit_bytes=8 * 1024 * 1024)
ANY = pl.BlockSpec(memory_space=pl.ANY)


def spread_kernel(layers, inner_rows, blocks, dest_ref, pos_ref, flow_ref, conf_ref, order_ref, out_ref):
    groups = out_ref.shape[0]
    count, width = conf_ref.shape
    place = pos_ref[...]
    layer = place // (inner_rows * blocks)
    inner_row = place // blocks % inner_rows
    column_block = place % blocks
    slot = (dest_ref[...] * layers + layer) * inner_rows + inner_row
    slots = groups * layers * inner_rows
    conf = conf_ref[...]
    terms = [flow_ref[pl.ds(c, count, stride=2), :] * conf for c in range(2)] + [conf]
    rest = jnp.concatenate(terms, axis=1)
    parts = []
    for _ in range(3):
        parts.append(rest.astype(jnp.bfloat16))
        rest = rest - parts[-1].astype(jnp.float32)
    numbers = lax.broadcasted_iota(jnp.int32, (slots, count), 0)
    for b in range(blocks):
        key = jnp.where(column_block == b, slot, -1)
        hit = jnp.where(numbers == key, 1.0, 0.0).astype(jnp.bfloat16)
        total = sum(jnp.dot(hit, part, preferred_element_type=jnp.float32) for part in reversed(parts))
        for o in range(groups):
            for l in range(layers):
                start = (o * layers + l) * inner_rows
                for c in range(3):
                    out_ref[o, c, l, :, b * width : (b + 1) * width] = total[
                        start : start + inner_rows, c * width : (c + 1) * width
                    ]


def shifted(blocks, lane, width):
    ahead = [pltpu.roll(x, width - 1, 1) for x in blocks]
    behind = [pltpu.roll(x, 1, 1) for x in blocks]
    zero = jnp.zeros_like(blocks[0])
    right = [jnp.where(lane == width - 1, after, own) for own, after in zip(ahead, ahead[1:] + [zero])]
    left = [jnp.where(lane == 0, before, own) for own, before in zip(behind, [zero] + behind[:-1])]
    return left, right


def plane_kernel(force_ref, stiff_ref, before_ref, after_ref, order_ref, out_ref, held, springs, keeps, pushes, even, odd):
    _, layers, rows, columns = force_ref.shape
    groups = out_ref.shape[0]
    inner_rows = rows // groups
    width = held.shape[-1]
    stride = held.shape[-2] // 8
    blocks = columns // width
    lane = lax.broadcasted_iota(jnp.int32, (8, width), 1)
    places = [(j, b) for j in range(stride) for b in range(blocks)]

    for l in range(layers):
        for c in (2, 0, 1):
            for b in range(blocks):
                span = slice(b * width, (b + 1) * width)
                held[c, l, b, :HALO] = before_ref[c, l, :, span]
                held[c, l, b, HALO : HALO + rows] = stiff_ref[l, :, span] if c == 2 else force_ref[c, l, :, span]
                held[c, l, b, HALO + rows :] = after_ref[c, l, :, span]
            for n, (j, b) in enumerate(places):
                part = STEP_PLANE * held[c, l, b, pl.ds(j, 8, stride=stride), :]
                if c == 2:
                    springs[l, n] = part
                    keeps[l, n] = 1.0 - 4.0 * part
                else:
                    pushes[l, c, n] = part

    def step(source, store):
        for l in range(layers):
            for c in range(2):
                field = [[source[l, c, j * blocks + b] for b in range(blocks)] for j in range(stride)]
                above = [[pltpu.roll(x, 1, 0) for x in field[-1]]] + field[:-1]
                below = field[1:] + [[pltpu.roll(x, 7, 0) for x in field[0]]]
                for j in range(stride):
                    left, right = shifted(field[j], lane, width)
                    for b in range(blocks):
                        n = j * blocks + b
                        near = (above[j][b] + below[j][b]) + (left[b] + right[b])
                        store(l, c, n, springs[l, n] * near + (keeps[l, n] * field[j][b] + pushes[l, c, n]))

    def to(target):
        def store(l, c, n, value):
            target[l, c, n] = value

        return store

    def to_rows(l, c, n, value):
        j, b = places[n]
        held[c, l, b, pl.ds(j, 8, stride=stride), :] = value

    def pair(_, carry):
        step(even, to(odd))
        step(odd, to(even))
        return carry

    inner = ISTEPS - 2
    source = pushes
    if inner % 2:
        step(source, to(even))
        source = even
    elif inner:
        step(source, to(odd))
        step(odd, to(even))
        source = even
    lax.fori_loop(0, (inner - 1) // 2, pair, 0)
    step(source, to_rows)
    for c in range(2):
        for l in range(layers):
            for b in range(blocks):
                for o in range(groups):
                    out_ref[o, c, l, :, b * width : (b + 1) * width] = held[
                        c, l, b, HALO + o * inner_rows : HALO + (o + 1) * inner_rows, :
                    ]


def tie_kernel(passed_ref, first_ref, out_ref):
    del passed_ref, first_ref, out_ref


def cross_kernel(moved_ref, forces_ref, stiff_ref, out_ref, result, sems):
    groups, _, layers, inner_rows, columns = moved_ref.shape
    sections = groups * layers
    width = result.shape[-1]
    blocks = columns // width
    zero = jnp.zeros((1, inner_rows, width), jnp.float32)

    def outgoing(index):
        b, c = index // 2, index % 2
        span = pl.ds(pl.multiple_of(b * width, width), width)
        return pltpu.make_async_copy(result.at[index], out_ref.at[c, :, :, span], sems.at[index])

    def one(index, carry):
        b, c = index // 2, index % 2
        span = pl.ds(pl.multiple_of(b * width, width), width)

        def channel(ref, c):
            return ref[:, c, :, :, span].reshape(sections, inner_rows, width)

        spring = STEP_CROSS * stiff_ref[:, :, span]
        weight = STEP_CROSS * channel(forces_ref, 2)
        pull = STEP_CROSS * channel(forces_ref, c)

        def step(_, field):
            rise = field - jnp.concatenate([zero, field[:-1]], axis=0)
            rise_above = jnp.concatenate([rise[1:], -field[-1:]], axis=0)
            stretch = pull - weight * rise
            stretch_above = jnp.concatenate([stretch[1:], zero], axis=0)
            return field + (spring * (rise_above - rise) + (stretch - stretch_above))

        result[index] = lax.fori_loop(0, ZSTEPS, step, channel(moved_ref, c))
        outgoing(index).start()
        return carry

    lax.fori_loop(0, 2 * blocks, one, 0)
    for index in range(2 * blocks):
        outgoing(index).wait()


def per_device(
    in_plane_force, stiffness, stiffness_z, patch_dest, patch_pos, patch_flow, patch_conf
):
    groups = lax.axis_size("sec")
    tiles = lax.axis_size("tile")
    layers, rows, columns = stiffness.shape
    inner_rows = rows // groups
    width = patch_flow.shape[-1]
    blocks = columns // width
    count = patch_pos.shape[2]
    up = [(i, i + 1) for i in range(tiles - 1)]
    down = [(j, i) for i, j in up]

    def ends(field):
        cut = field.reshape(field.shape[0], layers, rows // HALO, HALO, columns)
        return cut[:, :, :: rows // HALO - 1]

    edges = jnp.concatenate([ends(in_plane_force), ends(stiffness[None])], axis=0)
    before = lax.ppermute(edges[:, :, 1], "tile", up)
    after = lax.ppermute(edges[:, :, 0], "tile", down)
    forces = pl.pallas_call(
        functools.partial(spread_kernel, layers, inner_rows, blocks),
        out_shape=jax.ShapeDtypeStruct((groups, 3, layers, inner_rows, columns), jnp.float32),
        in_specs=[VMEM] * 4 + [ANY],
        out_specs=VMEM,
        compiler_params=LIMIT,
        cost_estimate=pl.CostEstimate(flops=6 * 256 * 256 * 384, bytes_accessed=800000, transcendentals=0),
        name="spread_patches",
    )(
        patch_dest.reshape(1, count),
        patch_pos.reshape(1, count),
        patch_flow.reshape(count * 2, width),
        patch_conf.reshape(count, width),
        edges,
    )
    moved_forces = lax.all_to_all(forces, "sec", split_axis=0, concat_axis=0, tiled=True)
    planar_shape = jax.ShapeDtypeStruct((groups, 2, layers, inner_rows, columns), jnp.float32)
    parts = (rows + 2 * HALO) // 8 * blocks
    planar = pl.pallas_call(
        plane_kernel,
        out_shape=planar_shape,
        in_specs=[VMEM] * 4 + [ANY],
        out_specs=VMEM,
        scratch_shapes=[
            pltpu.VMEM((3, layers, blocks, rows + 2 * HALO, width), jnp.float32),
            pltpu.VMEM((layers, parts, 8, width), jnp.float32),
            pltpu.VMEM((layers, parts, 8, width), jnp.float32),
            pltpu.VMEM((layers, 2, parts, 8, width), jnp.float32),
            pltpu.VMEM((layers, 2, parts, 8, width), jnp.float32),
            pltpu.VMEM((layers, 2, parts, 8, width), jnp.float32),
        ],
        compiler_params=LIMIT,
        cost_estimate=pl.CostEstimate(flops=10000000, bytes_accessed=100000000, transcendentals=0),
        name="plane_steps",
    )(in_plane_force, stiffness, before, after, forces)
    planar = pl.pallas_call(
        tie_kernel,
        out_shape=planar_shape,
        in_specs=[ANY] * 2,
        out_specs=ANY,
        input_output_aliases={0: 0},
        compiler_params=LIMIT,
        name="forces_first",
    )(planar, moved_forces)
    moved = lax.all_to_all(planar, "sec", split_axis=0, concat_axis=0, tiled=True)
    return pl.pallas_call(
        cross_kernel,
        out_shape=jax.ShapeDtypeStruct((2, groups * layers, inner_rows, columns), jnp.float32),
        in_specs=[VMEM] * 3,
        out_specs=ANY,
        scratch_shapes=[
            pltpu.VMEM((2 * blocks, groups * layers, inner_rows, width), jnp.float32),
            pltpu.SemaphoreType.DMA((2 * blocks,)),
        ],
        compiler_params=LIMIT,
        cost_estimate=pl.CostEstimate(flops=10000000, bytes_accessed=800000, transcendentals=0),
        name="cross_steps",
    )(moved, moved_forces, stiffness_z)


def solution(mesh):
    placed = (
        P(None, "sec", "tile", None),
        P("sec", "tile", None),
        P(None, ("tile", "sec"), None),
        P("sec", "tile", None, None),
        P("sec", "tile", None),
        P("sec", "tile", None, None, None),
        P("sec", "tile", None, None),
    )
    return jax.shard_map(
        per_device,
        mesh=mesh,
        in_specs=placed,
        out_specs=P(None, None, ("tile", "sec"), None),
        check_vma=False,
    )
```

```python
import functools

import jax
import jax.numpy as jnp
from jax import lax
from jax.experimental import pallas as pl
from jax.experimental.pallas import tpu as pltpu
from jax.sharding import PartitionSpec as P

ISTEPS = 8
ZSTEPS = 8


STEP_PLANE = 0.12
STEP_CROSS = 0.15

HALO = -(-(ISTEPS - 1) // 8) * 8

VMEM = pl.BlockSpec(memory_space=pltpu.VMEM)
LIMIT = pltpu.CompilerParams(vmem_limit_bytes=8 * 1024 * 1024)
ANY = pl.BlockSpec(memory_space=pl.ANY)


def spread_kernel(layers, inner_rows, blocks, dest_ref, pos_ref, flow_ref, conf_ref, order_ref, out_ref):
    groups = out_ref.shape[0]
    count, width = conf_ref.shape
    place = pos_ref[...]
    layer = place // (inner_rows * blocks)
    inner_row = place // blocks % inner_rows
    column_block = place % blocks
    slot = (dest_ref[...] * layers + layer) * inner_rows + inner_row
    slots = groups * layers * inner_rows
    conf = conf_ref[...]
    terms = [flow_ref[pl.ds(c, count, stride=2), :] * conf for c in range(2)] + [conf]
    rest = jnp.concatenate(terms, axis=1)
    parts = []
    for _ in range(3):
        parts.append(rest.astype(jnp.bfloat16))
        rest = rest - parts[-1].astype(jnp.float32)
    numbers = lax.broadcasted_iota(jnp.int32, (slots, count), 0)
    for b in range(blocks):
        key = jnp.where(column_block == b, slot, -1)
        hit = jnp.where(numbers == key, 1.0, 0.0).astype(jnp.bfloat16)
        total = sum(jnp.dot(hit, part, preferred_element_type=jnp.float32) for part in reversed(parts))
        for o in range(groups):
            for l in range(layers):
                start = (o * layers + l) * inner_rows
                for c in range(3):
                    out_ref[o, c, l, :, b * width : (b + 1) * width] = total[
                        start : start + inner_rows, c * width : (c + 1) * width
                    ]


def shifted(blocks, lane, width):
    ahead = [pltpu.roll(x, width - 1, 1) for x in blocks]
    behind = [pltpu.roll(x, 1, 1) for x in blocks]
    zero = jnp.zeros_like(blocks[0])
    right = [jnp.where(lane == width - 1, after, own) for own, after in zip(ahead, ahead[1:] + [zero])]
    left = [jnp.where(lane == 0, before, own) for own, before in zip(behind, [zero] + behind[:-1])]
    return left, right


def plane_kernel(force_ref, stiff_ref, before_ref, after_ref, order_ref, out_ref, held, springs, keeps, pushes, even, odd):
    _, layers, rows, columns = force_ref.shape
    groups = out_ref.shape[0]
    inner_rows = rows // groups
    width = held.shape[-1]
    stride = held.shape[-2] // 8
    blocks = columns // width
    lane = lax.broadcasted_iota(jnp.int32, (8, width), 1)
    places = [(j, b) for j in range(stride) for b in range(blocks)]

    for l in range(layers):
        for c in (2, 0, 1):
            for b in range(blocks):
                span = slice(b * width, (b + 1) * width)
                held[c, l, b, :HALO] = before_ref[c, l, :, span]
                held[c, l, b, HALO : HALO + rows] = stiff_ref[l, :, span] if c == 2 else force_ref[c, l, :, span]
                held[c, l, b, HALO + rows :] = after_ref[c, l, :, span]
            for n, (j, b) in enumerate(places):
                part = STEP_PLANE * held[c, l, b, pl.ds(j, 8, stride=stride), :]
                if c == 2:
                    springs[l, n] = part
                    keeps[l, n] = 1.0 - 4.0 * part
                else:
                    pushes[l, c, n] = part

    def step(source, store):
        for l in range(layers):
            for c in range(2):
                field = [[source[l, c, j * blocks + b] for b in range(blocks)] for j in range(stride)]
                above = [[pltpu.roll(x, 1, 0) for x in field[-1]]] + field[:-1]
                below = field[1:] + [[pltpu.roll(x, 7, 0) for x in field[0]]]
                for j in range(stride):
                    left, right = shifted(field[j], lane, width)
                    for b in range(blocks):
                        n = j * blocks + b
                        near = (above[j][b] + below[j][b]) + (left[b] + right[b])
                        store(l, c, n, springs[l, n] * near + (keeps[l, n] * field[j][b] + pushes[l, c, n]))

    def to(target):
        def store(l, c, n, value):
            target[l, c, n] = value

        return store

    def to_rows(l, c, n, value):
        j, b = places[n]
        held[c, l, b, pl.ds(j, 8, stride=stride), :] = value

    def pair(_, carry):
        step(even, to(odd))
        step(odd, to(even))
        return carry

    inner = ISTEPS - 2
    source = pushes
    if inner % 2:
        step(source, to(even))
        source = even
    elif inner:
        step(source, to(odd))
        step(odd, to(even))
        source = even
    lax.fori_loop(0, (inner - 1) // 2, pair, 0)
    step(source, to_rows)
    for c in range(2):
        for l in range(layers):
            for b in range(blocks):
                for o in range(groups):
                    out_ref[o, c, l, :, b * width : (b + 1) * width] = held[
                        c, l, b, HALO + o * inner_rows : HALO + (o + 1) * inner_rows, :
                    ]


def tie_kernel(passed_ref, first_ref, out_ref):
    del passed_ref, first_ref, out_ref


def cross_kernel(moved_ref, forces_ref, stiff_ref, out_ref, result, sems):
    groups, _, layers, inner_rows, columns = moved_ref.shape
    sections = groups * layers
    width = result.shape[-1]
    blocks = columns // width
    zero = jnp.zeros((1, inner_rows, width), jnp.float32)

    def outgoing(index):
        b, c = index // 2, index % 2
        span = pl.ds(pl.multiple_of(b * width, width), width)
        return pltpu.make_async_copy(result.at[index], out_ref.at[c, :, :, span], sems.at[index])

    def one(index, carry):
        b, c = index // 2, index % 2
        span = pl.ds(pl.multiple_of(b * width, width), width)

        def channel(ref, c):
            return ref[:, c, :, :, span].reshape(sections, inner_rows, width)

        spring = STEP_CROSS * stiff_ref[:, :, span]
        weight = STEP_CROSS * channel(forces_ref, 2)
        pull = STEP_CROSS * channel(forces_ref, c)

        def step(_, field):
            rise = field - jnp.concatenate([zero, field[:-1]], axis=0)
            rise_above = jnp.concatenate([rise[1:], -field[-1:]], axis=0)
            stretch = pull - weight * rise
            stretch_above = jnp.concatenate([stretch[1:], zero], axis=0)
            return field + (spring * (rise_above - rise) + (stretch - stretch_above))

        result[index] = lax.fori_loop(0, ZSTEPS, step, channel(moved_ref, c))
        outgoing(index).start()
        return carry

    lax.fori_loop(0, 2 * blocks, one, 0)
    for index in range(2 * blocks):
        outgoing(index).wait()


def per_device(
    in_plane_force, stiffness, stiffness_z, patch_dest, patch_pos, patch_flow, patch_conf
):
    groups = lax.axis_size("sec")
    tiles = lax.axis_size("tile")
    layers, rows, columns = stiffness.shape
    inner_rows = rows // groups
    width = patch_flow.shape[-1]
    blocks = columns // width
    count = patch_pos.shape[2]
    up = [(i, i + 1) for i in range(tiles - 1)]
    down = [(j, i) for i, j in up]

    def ends(field):
        cut = field.reshape(field.shape[0], layers, rows // HALO, HALO, columns)
        return cut[:, :, :: rows // HALO - 1]

    edges = jnp.concatenate([ends(in_plane_force), ends(stiffness[None])], axis=0)
    before = lax.ppermute(edges[:, :, 1], "tile", up)
    after = lax.ppermute(edges[:, :, 0], "tile", down)
    forces = pl.pallas_call(
        functools.partial(spread_kernel, layers, inner_rows, blocks),
        out_shape=jax.ShapeDtypeStruct((groups, 3, layers, inner_rows, columns), jnp.float32),
        in_specs=[VMEM] * 4 + [ANY],
        out_specs=VMEM,
        compiler_params=LIMIT,
        cost_estimate=pl.CostEstimate(flops=6 * 256 * 256 * 384, bytes_accessed=800000, transcendentals=0),
        name="spread_patches",
    )(
        patch_dest.reshape(1, count),
        patch_pos.reshape(1, count),
        patch_flow.reshape(count * 2, width),
        patch_conf.reshape(count, width),
        edges,
    )
    moved_forces = lax.all_to_all(forces, "sec", split_axis=0, concat_axis=0, tiled=True)
    planar_shape = jax.ShapeDtypeStruct((groups, 2, layers, inner_rows, columns), jnp.float32)
    parts = (rows + 2 * HALO) // 8 * blocks
    planar = pl.pallas_call(
        plane_kernel,
        out_shape=planar_shape,
        in_specs=[VMEM] * 4 + [ANY],
        out_specs=VMEM,
        scratch_shapes=[
            pltpu.VMEM((3, layers, blocks, rows + 2 * HALO, width), jnp.float32),
            pltpu.VMEM((layers, parts, 8, width), jnp.float32),
            pltpu.VMEM((layers, parts, 8, width), jnp.float32),
            pltpu.VMEM((layers, 2, parts, 8, width), jnp.float32),
            pltpu.VMEM((layers, 2, parts, 8, width), jnp.float32),
            pltpu.VMEM((layers, 2, parts, 8, width), jnp.float32),
        ],
        compiler_params=LIMIT,
        cost_estimate=pl.CostEstimate(flops=10**13, bytes_accessed=10**11, transcendentals=0),
        name="plane_steps",
    )(in_plane_force, stiffness, before, after, forces)
    planar = pl.pallas_call(
        tie_kernel,
        out_shape=planar_shape,
        in_specs=[ANY] * 2,
        out_specs=ANY,
        input_output_aliases={0: 0},
        compiler_params=LIMIT,
        name="forces_first",
    )(planar, moved_forces)
    moved = lax.all_to_all(planar, "sec", split_axis=0, concat_axis=0, tiled=True)
    return pl.pallas_call(
        cross_kernel,
        out_shape=jax.ShapeDtypeStruct((2, groups * layers, inner_rows, columns), jnp.float32),
        in_specs=[VMEM] * 3,
        out_specs=ANY,
        scratch_shapes=[
            pltpu.VMEM((2 * blocks, groups * layers, inner_rows, width), jnp.float32),
            pltpu.SemaphoreType.DMA((2 * blocks,)),
        ],
        compiler_params=LIMIT,
        cost_estimate=pl.CostEstimate(flops=10000000, bytes_accessed=800000, transcendentals=0),
        name="cross_steps",
    )(moved, moved_forces, stiffness_z)


def solution(mesh):
    placed = (
        P(None, "sec", "tile", None),
        P("sec", "tile", None),
        P(None, ("tile", "sec"), None),
        P("sec", "tile", None, None),
        P("sec", "tile", None),
        P("sec", "tile", None, None, None),
        P("sec", "tile", None, None),
    )
    return jax.shard_map(
        per_device,
        mesh=mesh,
        in_specs=placed,
        out_specs=P(None, None, ("tile", "sec"), None),
        check_vma=False,
    )
```

```python
import functools

import jax
import jax.numpy as jnp
from jax import lax
from jax.experimental import pallas as pl
from jax.experimental.pallas import tpu as pltpu
from jax.sharding import PartitionSpec as P

ISTEPS = 8
ZSTEPS = 8


STEP_PLANE = 0.12
STEP_CROSS = 0.15

HALO = -(-(ISTEPS - 1) // 8) * 8

VMEM = pl.BlockSpec(memory_space=pltpu.VMEM)
LIMIT = pltpu.CompilerParams(vmem_limit_bytes=8 * 1024 * 1024)
ANY = pl.BlockSpec(memory_space=pl.ANY)


def spread_kernel(layers, inner_rows, blocks, dest_ref, pos_ref, flow_ref, conf_ref, order_ref, out_ref):
    groups = out_ref.shape[0]
    count, width = conf_ref.shape
    place = pos_ref[...]
    layer = place // (inner_rows * blocks)
    inner_row = place // blocks % inner_rows
    column_block = place % blocks
    slot = (dest_ref[...] * layers + layer) * inner_rows + inner_row
    slots = groups * layers * inner_rows
    conf = conf_ref[...]
    terms = [flow_ref[pl.ds(c, count, stride=2), :] * conf for c in range(2)] + [conf]
    rest = jnp.concatenate(terms, axis=1)
    parts = []
    for _ in range(3):
        parts.append(rest.astype(jnp.bfloat16))
        rest = rest - parts[-1].astype(jnp.float32)
    numbers = lax.broadcasted_iota(jnp.int32, (slots, count), 0)
    for b in range(blocks):
        key = jnp.where(column_block == b, slot, -1)
        hit = jnp.where(numbers == key, 1.0, 0.0).astype(jnp.bfloat16)
        total = sum(jnp.dot(hit, part, preferred_element_type=jnp.float32) for part in reversed(parts))
        for o in range(groups):
            for l in range(layers):
                start = (o * layers + l) * inner_rows
                for c in range(3):
                    out_ref[o, c, l, :, b * width : (b + 1) * width] = total[
                        start : start + inner_rows, c * width : (c + 1) * width
                    ]


def shifted(blocks, lane, width):
    ahead = [pltpu.roll(x, width - 1, 1) for x in blocks]
    behind = [pltpu.roll(x, 1, 1) for x in blocks]
    zero = jnp.zeros_like(blocks[0])
    right = [jnp.where(lane == width - 1, after, own) for own, after in zip(ahead, ahead[1:] + [zero])]
    left = [jnp.where(lane == 0, before, own) for own, before in zip(behind, [zero] + behind[:-1])]
    return left, right


def plane_kernel(tile_ref, force_ref, stiff_ref, edges_ref, order_ref, out_ref, held, springs, keeps, pushes, even, odd):
    _, layers, rows, columns = force_ref.shape
    groups = out_ref.shape[0]
    inner_rows = rows // groups
    width = held.shape[-1]
    stride = held.shape[-2] // 8
    blocks = columns // width
    lane = lax.broadcasted_iota(jnp.int32, (8, width), 1)
    places = [(j, b) for j in range(stride) for b in range(blocks)]

    tile, tiles = tile_ref[0], edges_ref.shape[0]
    before, has_before = jnp.maximum(tile - 1, 0), jnp.where(tile > 0, 1.0, 0.0)
    after, has_after = jnp.minimum(tile + 1, tiles - 1), jnp.where(tile < tiles - 1, 1.0, 0.0)

    for l in range(layers):
        for c in (2, 0, 1):
            for b in range(blocks):
                span = slice(b * width, (b + 1) * width)
                held[c, l, b, :HALO] = edges_ref[before, c, l, 1, :, span] * has_before
                held[c, l, b, HALO : HALO + rows] = stiff_ref[l, :, span] if c == 2 else force_ref[c, l, :, span]
                held[c, l, b, HALO + rows :] = edges_ref[after, c, l, 0, :, span] * has_after
            for n, (j, b) in enumerate(places):
                part = STEP_PLANE * held[c, l, b, pl.ds(j, 8, stride=stride), :]
                if c == 2:
                    springs[l, n] = part
                    keeps[l, n] = 1.0 - 4.0 * part
                else:
                    pushes[l, c, n] = part

    def step(source, store):
        for l in range(layers):
            for c in range(2):
                field = [[source[l, c, j * blocks + b] for b in range(blocks)] for j in range(stride)]
                above = [[pltpu.roll(x, 1, 0) for x in field[-1]]] + field[:-1]
                below = field[1:] + [[pltpu.roll(x, 7, 0) for x in field[0]]]
                for j in range(stride):
                    left, right = shifted(field[j], lane, width)
                    for b in range(blocks):
                        n = j * blocks + b
                        near = (above[j][b] + below[j][b]) + (left[b] + right[b])
                        store(l, c, n, springs[l, n] * near + (keeps[l, n] * field[j][b] + pushes[l, c, n]))

    def to(target):
        def store(l, c, n, value):
            target[l, c, n] = value

        return store

    def to_rows(l, c, n, value):
        j, b = places[n]
        held[c, l, b, pl.ds(j, 8, stride=stride), :] = value

    def pair(_, carry):
        step(even, to(odd))
        step(odd, to(even))
        return carry

    inner = ISTEPS - 2
    source = pushes
    if inner % 2:
        step(source, to(even))
        source = even
    elif inner:
        step(source, to(odd))
        step(odd, to(even))
        source = even
    lax.fori_loop(0, (inner - 1) // 2, pair, 0)
    step(source, to_rows)
    for c in range(2):
        for l in range(layers):
            for b in range(blocks):
                for o in range(groups):
                    out_ref[o, c, l, :, b * width : (b + 1) * width] = held[
                        c, l, b, HALO + o * inner_rows : HALO + (o + 1) * inner_rows, :
                    ]


def tie_kernel(passed_ref, first_ref, out_ref):
    del passed_ref, first_ref, out_ref


def cross_kernel(moved_ref, forces_ref, stiff_ref, out_ref, result, sems):
    groups, _, layers, inner_rows, columns = moved_ref.shape
    sections = groups * layers
    width = result.shape[-1]
    blocks = columns // width
    zero = jnp.zeros((1, inner_rows, width), jnp.float32)

    def outgoing(index):
        b, c = index // 2, index % 2
        span = pl.ds(pl.multiple_of(b * width, width), width)
        return pltpu.make_async_copy(result.at[index], out_ref.at[c, :, :, span], sems.at[index])

    def one(index, carry):
        b, c = index // 2, index % 2
        span = pl.ds(pl.multiple_of(b * width, width), width)

        def channel(ref, c):
            return ref[:, c, :, :, span].reshape(sections, inner_rows, width)

        spring = STEP_CROSS * stiff_ref[:, :, span]
        weight = STEP_CROSS * channel(forces_ref, 2)
        pull = STEP_CROSS * channel(forces_ref, c)

        def step(_, field):
            rise = field - jnp.concatenate([zero, field[:-1]], axis=0)
            rise_above = jnp.concatenate([rise[1:], -field[-1:]], axis=0)
            stretch = pull - weight * rise
            stretch_above = jnp.concatenate([stretch[1:], zero], axis=0)
            return field + (spring * (rise_above - rise) + (stretch - stretch_above))

        result[index] = lax.fori_loop(0, ZSTEPS, step, channel(moved_ref, c))
        outgoing(index).start()
        return carry

    lax.fori_loop(0, 2 * blocks, one, 0)
    for index in range(2 * blocks):
        outgoing(index).wait()


def per_device(
    in_plane_force, stiffness, stiffness_z, patch_dest, patch_pos, patch_flow, patch_conf
):
    groups = lax.axis_size("sec")
    layers, rows, columns = stiffness.shape
    inner_rows = rows // groups
    width = patch_flow.shape[-1]
    blocks = columns // width
    count = patch_pos.shape[2]

    def ends(field):
        cut = field.reshape(field.shape[0], layers, rows // HALO, HALO, columns)
        return cut[:, :, :: rows // HALO - 1]

    edges = jnp.concatenate([ends(in_plane_force), ends(stiffness[None])], axis=0)
    gathered = lax.all_gather(edges, "tile", axis=0, tiled=False)
    tile = lax.axis_index("tile").reshape(1)
    forces = pl.pallas_call(
        functools.partial(spread_kernel, layers, inner_rows, blocks),
        out_shape=jax.ShapeDtypeStruct((groups, 3, layers, inner_rows, columns), jnp.float32),
        in_specs=[VMEM] * 4 + [ANY],
        out_specs=VMEM,
        compiler_params=LIMIT,
        cost_estimate=pl.CostEstimate(flops=6 * 256 * 256 * 384, bytes_accessed=800000, transcendentals=0),
        name="spread_patches",
    )(
        patch_dest.reshape(1, count),
        patch_pos.reshape(1, count),
        patch_flow.reshape(count * 2, width),
        patch_conf.reshape(count, width),
        edges,
    )
    moved_forces = lax.all_to_all(forces, "sec", split_axis=0, concat_axis=0, tiled=True)
    planar_shape = jax.ShapeDtypeStruct((groups, 2, layers, inner_rows, columns), jnp.float32)
    parts = (rows + 2 * HALO) // 8 * blocks
    planar = pl.pallas_call(
        plane_kernel,
        out_shape=planar_shape,
        in_specs=[pl.BlockSpec(memory_space=pltpu.SMEM)] + [VMEM] * 3 + [ANY],
        out_specs=VMEM,
        scratch_shapes=[
            pltpu.VMEM((3, layers, blocks, rows + 2 * HALO, width), jnp.float32),
            pltpu.VMEM((layers, parts, 8, width), jnp.float32),
            pltpu.VMEM((layers, parts, 8, width), jnp.float32),
            pltpu.VMEM((layers, 2, parts, 8, width), jnp.float32),
            pltpu.VMEM((layers, 2, parts, 8, width), jnp.float32),
            pltpu.VMEM((layers, 2, parts, 8, width), jnp.float32),
        ],
        compiler_params=LIMIT,
        cost_estimate=pl.CostEstimate(flops=10**11, bytes_accessed=4 * 10**8, transcendentals=0),
        name="plane_steps",
    )(tile, in_plane_force, stiffness, gathered, forces)
    planar = pl.pallas_call(
        tie_kernel,
        out_shape=planar_shape,
        in_specs=[ANY] * 2,
        out_specs=ANY,
        input_output_aliases={0: 0},
        compiler_params=LIMIT,
        name="forces_first",
    )(planar, moved_forces)
    moved = lax.all_to_all(planar, "sec", split_axis=0, concat_axis=0, tiled=True)
    return pl.pallas_call(
        cross_kernel,
        out_shape=jax.ShapeDtypeStruct((2, groups * layers, inner_rows, columns), jnp.float32),
        in_specs=[VMEM] * 3,
        out_specs=ANY,
        scratch_shapes=[
            pltpu.VMEM((2 * blocks, groups * layers, inner_rows, width), jnp.float32),
            pltpu.SemaphoreType.DMA((2 * blocks,)),
        ],
        compiler_params=LIMIT,
        cost_estimate=pl.CostEstimate(flops=10000000, bytes_accessed=800000, transcendentals=0),
        name="cross_steps",
    )(moved, moved_forces, stiffness_z)


def solution(mesh):
    placed = (
        P(None, "sec", "tile", None),
        P("sec", "tile", None),
        P(None, ("tile", "sec"), None),
        P("sec", "tile", None, None),
        P("sec", "tile", None),
        P("sec", "tile", None, None, None),
        P("sec", "tile", None, None),
    )
    return jax.shard_map(
        per_device,
        mesh=mesh,
        in_specs=placed,
        out_specs=P(None, None, ("tile", "sec"), None),
        check_vma=False,
    )
```

```python
import jax
import jax.numpy as jnp
from jax import lax
from jax.experimental import pallas as pl
from jax.experimental.pallas import tpu as pltpu
from jax.sharding import PartitionSpec as P

ISTEPS = 8
ZSTEPS = 8


STEP_PLANE = 0.12
STEP_CROSS = 0.15

HALO = -(-(ISTEPS - 1) // 8) * 8

VMEM = pl.BlockSpec(memory_space=pltpu.VMEM)
LIMIT = pltpu.CompilerParams(vmem_limit_bytes=8 * 1024 * 1024)
ANY = pl.BlockSpec(memory_space=pl.ANY)


def spread(layers, inner_rows, blocks, dest_ref, pos_ref, flow_ref, conf_ref, out_ref):
    groups = out_ref.shape[0]
    count, width = conf_ref.shape
    place = pos_ref[...]
    layer = place // (inner_rows * blocks)
    inner_row = place // blocks % inner_rows
    column_block = place % blocks
    slot = (dest_ref[...] * layers + layer) * inner_rows + inner_row
    slots = groups * layers * inner_rows
    conf = conf_ref[...]
    terms = [flow_ref[pl.ds(c, count, stride=2), :] * conf for c in range(2)] + [conf]
    rest = jnp.concatenate(terms, axis=1)
    parts = []
    for _ in range(3):
        parts.append(rest.astype(jnp.bfloat16))
        rest = rest - parts[-1].astype(jnp.float32)
    numbers = lax.broadcasted_iota(jnp.int32, (slots, count), 0)
    for b in range(blocks):
        key = jnp.where(column_block == b, slot, -1)
        hit = jnp.where(numbers == key, 1.0, 0.0).astype(jnp.bfloat16)
        total = sum(jnp.dot(hit, part, preferred_element_type=jnp.float32) for part in reversed(parts))
        for o in range(groups):
            for l in range(layers):
                start = (o * layers + l) * inner_rows
                for c in range(3):
                    out_ref[o, 2 + c, l, :, b * width : (b + 1) * width] = total[
                        start : start + inner_rows, c * width : (c + 1) * width
                    ]


def shifted(blocks, lane, width):
    ahead = [pltpu.roll(x, width - 1, 1) for x in blocks]
    behind = [pltpu.roll(x, 1, 1) for x in blocks]
    zero = jnp.zeros_like(blocks[0])
    right = [jnp.where(lane == width - 1, after, own) for own, after in zip(ahead, ahead[1:] + [zero])]
    left = [jnp.where(lane == 0, before, own) for own, before in zip(behind, [zero] + behind[:-1])]
    return left, right


def relax(held, springs, keeps, pushes, even, odd):
    _, layers, blocks, total, width = held.shape
    stride = total // 8
    lane = lax.broadcasted_iota(jnp.int32, (8, width), 1)
    places = [(j, b) for j in range(stride) for b in range(blocks)]

    for l in range(layers):
        for c in (2, 0, 1):
            for n, (j, b) in enumerate(places):
                part = STEP_PLANE * held[c, l, b, pl.ds(j, 8, stride=stride), :]
                if c == 2:
                    springs[l, n] = part
                    keeps[l, n] = 1.0 - 4.0 * part
                else:
                    pushes[l, c, n] = part

    def step(source, store):
        for l in range(layers):
            for c in range(2):
                field = [[source[l, c, j * blocks + b] for b in range(blocks)] for j in range(stride)]
                above = [[pltpu.roll(x, 1, 0) for x in field[-1]]] + field[:-1]
                below = field[1:] + [[pltpu.roll(x, 7, 0) for x in field[0]]]
                for j in range(stride):
                    left, right = shifted(field[j], lane, width)
                    for b in range(blocks):
                        n = j * blocks + b
                        near = (above[j][b] + below[j][b]) + (left[b] + right[b])
                        store(l, c, n, springs[l, n] * near + (keeps[l, n] * field[j][b] + pushes[l, c, n]))

    def to(target):
        def store(l, c, n, value):
            target[l, c, n] = value

        return store

    def to_rows(l, c, n, value):
        j, b = places[n]
        held[c, l, b, pl.ds(j, 8, stride=stride), :] = value

    def pair(_, carry):
        step(even, to(odd))
        step(odd, to(even))
        return carry

    inner = ISTEPS - 2
    source = pushes
    if inner % 2:
        step(source, to(even))
        source = even
    elif inner:
        step(source, to(odd))
        step(odd, to(even))
        source = even
    lax.fori_loop(0, (inner - 1) // 2, pair, 0)
    step(source, to_rows)


def put_rows(held, out_ref, start, first, last):
    _, layers, blocks, _, width = held.shape
    inner_rows = out_ref.shape[3]
    for c in range(2):
        for l in range(layers):
            for b in range(blocks):
                for o in range(first // inner_rows, last // inner_rows):
                    at = start + o * inner_rows - first
                    out_ref[o, c, l, :, b * width : (b + 1) * width] = held[c, l, b, at : at + inner_rows, :]


def inner_kernel(dest_ref, pos_ref, flow_ref, conf_ref, force_ref, stiff_ref, order_ref, out_ref, held, *scratch):
    layers, rows, columns = stiff_ref.shape
    blocks, width = held.shape[2], held.shape[-1]
    spread(layers, out_ref.shape[3], blocks, dest_ref, pos_ref, flow_ref, conf_ref, out_ref)
    for b in range(blocks):
        span = slice(b * width, (b + 1) * width)
        for l in range(layers):
            held[2, l, b] = stiff_ref[l, :, span]
            for c in range(2):
                held[c, l, b] = force_ref[c, l, :, span]
    relax(held, *scratch)
    put_rows(held, out_ref, HALO, HALO, rows - HALO)


def ends_kernel(force_ref, stiff_ref, before_ref, after_ref, mixed_ref, out_ref, held, *scratch):
    layers, rows, columns = stiff_ref.shape
    blocks, width = held.shape[2], held.shape[-1]
    edge = HALO // out_ref.shape[3]
    for b in range(blocks):
        span = slice(b * width, (b + 1) * width)
        for c in range(3):
            for l in range(layers):
                own = stiff_ref.at[l] if c == 2 else force_ref.at[c, l]
                held[c, l, b, :HALO] = before_ref[c, l, :, span]
                held[c, l, b, HALO : 3 * HALO] = own[: 2 * HALO, span]
                held[c, l, b, 3 * HALO : 5 * HALO] = own[rows - 2 * HALO :, span]
                held[c, l, b, 5 * HALO :] = after_ref[c, l, :, span]
    out_ref[:, 2:] = mixed_ref[:, 2:]
    out_ref[edge:-edge, :2] = mixed_ref[edge:-edge, :2]
    relax(held, *scratch)
    put_rows(held, out_ref, HALO, 0, HALO)
    put_rows(held, out_ref, 4 * HALO, rows - HALO, rows)


def relax_scratch(layers, blocks, total, width):
    parts = total // 8 * blocks
    return [pltpu.VMEM((3, layers, blocks, total, width), jnp.float32)] + [
        pltpu.VMEM((layers, parts, 8, width), jnp.float32),
        pltpu.VMEM((layers, parts, 8, width), jnp.float32),
        pltpu.VMEM((layers, 2, parts, 8, width), jnp.float32),
        pltpu.VMEM((layers, 2, parts, 8, width), jnp.float32),
        pltpu.VMEM((layers, 2, parts, 8, width), jnp.float32),
    ]


def cross_kernel(moved_ref, stiff_ref, out_ref, result, sems):
    groups, _, layers, inner_rows, columns = moved_ref.shape
    sections = groups * layers
    width = result.shape[-1]
    blocks = columns // width
    zero = jnp.zeros((1, inner_rows, width), jnp.float32)

    def outgoing(index):
        b, c = index // 2, index % 2
        span = pl.ds(pl.multiple_of(b * width, width), width)
        return pltpu.make_async_copy(result.at[index], out_ref.at[c, :, :, span], sems.at[index])

    def one(index, carry):
        b, c = index // 2, index % 2
        span = pl.ds(pl.multiple_of(b * width, width), width)

        def channel(c):
            return moved_ref[:, c, :, :, span].reshape(sections, inner_rows, width)

        spring = STEP_CROSS * stiff_ref[:, :, span]
        weight = STEP_CROSS * channel(4)
        pull = STEP_CROSS * channel(2 + c)

        def step(_, field):
            rise = field - jnp.concatenate([zero, field[:-1]], axis=0)
            rise_above = jnp.concatenate([rise[1:], -field[-1:]], axis=0)
            stretch = pull - weight * rise
            stretch_above = jnp.concatenate([stretch[1:], zero], axis=0)
            return field + (spring * (rise_above - rise) + (stretch - stretch_above))

        result[index] = lax.fori_loop(0, ZSTEPS, step, channel(c))
        outgoing(index).start()
        return carry

    lax.fori_loop(0, 2 * blocks, one, 0)
    for index in range(2 * blocks):
        outgoing(index).wait()


def per_device(
    in_plane_force, stiffness, stiffness_z, patch_dest, patch_pos, patch_flow, patch_conf
):
    groups = lax.axis_size("sec")
    tiles = lax.axis_size("tile")
    layers, rows, columns = stiffness.shape
    inner_rows = rows // groups
    width = patch_flow.shape[-1]
    blocks = columns // width
    count = patch_pos.shape[2]
    up = [(i, i + 1) for i in range(tiles - 1)]
    down = [(j, i) for i, j in up]

    def ends(field):
        cut = field.reshape(field.shape[0], layers, rows // HALO, HALO, columns)
        return cut[:, :, :: rows // HALO - 1]

    edges = jnp.concatenate([ends(in_plane_force), ends(stiffness[None])], axis=0)
    before = lax.ppermute(edges[:, :, 1], "tile", up)
    after = lax.ppermute(edges[:, :, 0], "tile", down)
    mixed_shape = jax.ShapeDtypeStruct((groups, 5, layers, inner_rows, columns), jnp.float32)
    mixed = pl.pallas_call(
        inner_kernel,
        out_shape=mixed_shape,
        in_specs=[VMEM] * 6 + [ANY],
        out_specs=VMEM,
        scratch_shapes=relax_scratch(layers, blocks, rows, width),
        compiler_params=LIMIT,
        cost_estimate=pl.CostEstimate(flops=10**9, bytes_accessed=10**7, transcendentals=0),
        name="spread_and_inner_rows",
    )(
        patch_dest.reshape(1, count),
        patch_pos.reshape(1, count),
        patch_flow.reshape(count * 2, width),
        patch_conf.reshape(count, width),
        in_plane_force,
        stiffness,
        edges,
    )
    mixed = pl.pallas_call(
        ends_kernel,
        out_shape=mixed_shape,
        in_specs=[VMEM] * 5,
        out_specs=VMEM,
        scratch_shapes=relax_scratch(layers, blocks, 6 * HALO, width),
        compiler_params=LIMIT,
        cost_estimate=pl.CostEstimate(flops=10**7, bytes_accessed=10**6, transcendentals=0),
        name="end_rows",
    )(in_plane_force, stiffness, before, after, mixed)
    moved = lax.all_to_all(mixed, "sec", split_axis=0, concat_axis=0, tiled=True)
    return pl.pallas_call(
        cross_kernel,
        out_shape=jax.ShapeDtypeStruct((2, groups * layers, inner_rows, columns), jnp.float32),
        in_specs=[VMEM] * 2,
        out_specs=ANY,
        scratch_shapes=[
            pltpu.VMEM((2 * blocks, groups * layers, inner_rows, width), jnp.float32),
            pltpu.SemaphoreType.DMA((2 * blocks,)),
        ],
        compiler_params=LIMIT,
        cost_estimate=pl.CostEstimate(flops=10000000, bytes_accessed=800000, transcendentals=0),
        name="cross_steps",
    )(moved, stiffness_z)


def solution(mesh):
    placed = (
        P(None, "sec", "tile", None),
        P("sec", "tile", None),
        P(None, ("tile", "sec"), None),
        P("sec", "tile", None, None),
        P("sec", "tile", None),
        P("sec", "tile", None, None, None),
        P("sec", "tile", None, None),
    )
    return jax.shard_map(
        per_device,
        mesh=mesh,
        in_specs=placed,
        out_specs=P(None, None, ("tile", "sec"), None),
        check_vma=False,
    )
```

```python
import jax
import jax.numpy as jnp
from jax import lax
from jax.experimental import pallas as pl
from jax.experimental.pallas import tpu as pltpu
from jax.sharding import PartitionSpec as P

ISTEPS = 8
ZSTEPS = 8


STEP_PLANE = 0.12
STEP_CROSS = 0.15

HALO = -(-(ISTEPS - 1) // 8) * 8

VMEM = pl.BlockSpec(memory_space=pltpu.VMEM)
LIMIT = pltpu.CompilerParams(vmem_limit_bytes=8 * 1024 * 1024)
ANY = pl.BlockSpec(memory_space=pl.ANY)


def spread(layers, inner_rows, blocks, dest_ref, pos_ref, flow_ref, conf_ref, out_ref):
    groups = out_ref.shape[0]
    count, width = conf_ref.shape
    place = pos_ref[...]
    layer = place // (inner_rows * blocks)
    inner_row = place // blocks % inner_rows
    column_block = place % blocks
    slot = (dest_ref[...] * layers + layer) * inner_rows + inner_row
    slots = groups * layers * inner_rows
    conf = conf_ref[...]
    terms = [flow_ref[pl.ds(c, count, stride=2), :] * conf for c in range(2)] + [conf]
    rest = jnp.concatenate(terms, axis=1)
    parts = []
    for _ in range(3):
        parts.append(rest.astype(jnp.bfloat16))
        rest = rest - parts[-1].astype(jnp.float32)
    numbers = lax.broadcasted_iota(jnp.int32, (slots, count), 0)
    for b in range(blocks):
        key = jnp.where(column_block == b, slot, -1)
        hit = jnp.where(numbers == key, 1.0, 0.0).astype(jnp.bfloat16)
        total = sum(jnp.dot(hit, part, preferred_element_type=jnp.float32) for part in reversed(parts))
        for o in range(groups):
            for l in range(layers):
                start = (o * layers + l) * inner_rows
                for c in range(3):
                    out_ref[o, 2 + c, l, :, b * width : (b + 1) * width] = total[
                        start : start + inner_rows, c * width : (c + 1) * width
                    ]


def shifted(blocks, lane, width):
    ahead = [pltpu.roll(x, width - 1, 1) for x in blocks]
    behind = [pltpu.roll(x, 1, 1) for x in blocks]
    zero = jnp.zeros_like(blocks[0])
    right = [jnp.where(lane == width - 1, after, own) for own, after in zip(ahead, ahead[1:] + [zero])]
    left = [jnp.where(lane == 0, before, own) for own, before in zip(behind, [zero] + behind[:-1])]
    return left, right


def relax(held, springs, keeps, pushes, even, odd):
    _, layers, blocks, total, width = held.shape
    stride = total // 8
    lane = lax.broadcasted_iota(jnp.int32, (8, width), 1)
    places = [(j, b) for j in range(stride) for b in range(blocks)]

    for l in range(layers):
        for c in (2, 0, 1):
            for n, (j, b) in enumerate(places):
                part = STEP_PLANE * held[c, l, b, pl.ds(j, 8, stride=stride), :]
                if c == 2:
                    springs[l, n] = part
                    keeps[l, n] = 1.0 - 4.0 * part
                else:
                    pushes[l, c, n] = part

    def step(source, store):
        for l in range(layers):
            for c in range(2):
                field = [[source[l, c, j * blocks + b] for b in range(blocks)] for j in range(stride)]
                above = [[pltpu.roll(x, 1, 0) for x in field[-1]]] + field[:-1]
                below = field[1:] + [[pltpu.roll(x, 7, 0) for x in field[0]]]
                for j in range(stride):
                    left, right = shifted(field[j], lane, width)
                    for b in range(blocks):
                        n = j * blocks + b
                        near = (above[j][b] + below[j][b]) + (left[b] + right[b])
                        store(l, c, n, springs[l, n] * near + (keeps[l, n] * field[j][b] + pushes[l, c, n]))

    def to(target):
        def store(l, c, n, value):
            target[l, c, n] = value

        return store

    def to_rows(l, c, n, value):
        j, b = places[n]
        held[c, l, b, pl.ds(j, 8, stride=stride), :] = value

    source = pushes
    for n in range(ISTEPS - 2):
        target = odd if n % 2 else even
        step(source, to(target))
        source = target
    step(source, to_rows)


def put_rows(held, out_ref, start, first, last):
    _, layers, blocks, _, width = held.shape
    inner_rows = out_ref.shape[3]
    for c in range(2):
        for l in range(layers):
            for b in range(blocks):
                for o in range(first // inner_rows, last // inner_rows):
                    at = start + o * inner_rows - first
                    out_ref[o, c, l, :, b * width : (b + 1) * width] = held[c, l, b, at : at + inner_rows, :]


def inner_kernel(dest_ref, pos_ref, flow_ref, conf_ref, force_ref, stiff_ref, out_ref, held, *scratch):
    layers, rows, columns = stiff_ref.shape
    blocks, width = held.shape[2], held.shape[-1]
    spread(layers, out_ref.shape[3], blocks, dest_ref, pos_ref, flow_ref, conf_ref, out_ref)
    for b in range(blocks):
        span = slice(b * width, (b + 1) * width)
        for l in range(layers):
            held[2, l, b] = stiff_ref[l, :, span]
            for c in range(2):
                held[c, l, b] = force_ref[c, l, :, span]
    relax(held, *scratch)
    put_rows(held, out_ref, HALO, HALO, rows - HALO)


def ends_kernel(force_ref, stiff_ref, before_ref, after_ref, mixed_ref, out_ref, held, *scratch):
    layers, rows, columns = stiff_ref.shape
    blocks, width = held.shape[2], held.shape[-1]
    edge = HALO // out_ref.shape[3]
    for b in range(blocks):
        span = slice(b * width, (b + 1) * width)
        for c in range(3):
            for l in range(layers):
                own = stiff_ref.at[l] if c == 2 else force_ref.at[c, l]
                held[c, l, b, :HALO] = before_ref[c, l, :, span]
                held[c, l, b, HALO : 3 * HALO] = own[: 2 * HALO, span]
                held[c, l, b, 3 * HALO : 5 * HALO] = own[rows - 2 * HALO :, span]
                held[c, l, b, 5 * HALO :] = after_ref[c, l, :, span]
    out_ref[:, 2:] = mixed_ref[:, 2:]
    out_ref[edge:-edge, :2] = mixed_ref[edge:-edge, :2]
    relax(held, *scratch)
    put_rows(held, out_ref, HALO, 0, HALO)
    put_rows(held, out_ref, 4 * HALO, rows - HALO, rows)


def relax_scratch(layers, blocks, total, width):
    parts = total // 8 * blocks
    return [pltpu.VMEM((3, layers, blocks, total, width), jnp.float32)] + [
        pltpu.VMEM((layers, parts, 8, width), jnp.float32),
        pltpu.VMEM((layers, parts, 8, width), jnp.float32),
        pltpu.VMEM((layers, 2, parts, 8, width), jnp.float32),
        pltpu.VMEM((layers, 2, parts, 8, width), jnp.float32),
        pltpu.VMEM((layers, 2, parts, 8, width), jnp.float32),
    ]


def cross_kernel(moved_ref, stiff_ref, out_ref, result, sems):
    groups, _, layers, inner_rows, columns = moved_ref.shape
    sections = groups * layers
    width = result.shape[-1]
    blocks = columns // width
    zero = jnp.zeros((1, inner_rows, width), jnp.float32)

    def outgoing(index):
        b, c = index // 2, index % 2
        span = pl.ds(pl.multiple_of(b * width, width), width)
        return pltpu.make_async_copy(result.at[index], out_ref.at[c, :, :, span], sems.at[index])

    def one(index, carry):
        b, c = index // 2, index % 2
        span = pl.ds(pl.multiple_of(b * width, width), width)

        def channel(c):
            return moved_ref[:, c, :, :, span].reshape(sections, inner_rows, width)

        spring = STEP_CROSS * stiff_ref[:, :, span]
        weight = STEP_CROSS * channel(4)
        pull = STEP_CROSS * channel(2 + c)

        def step(_, field):
            rise = field - jnp.concatenate([zero, field[:-1]], axis=0)
            rise_above = jnp.concatenate([rise[1:], -field[-1:]], axis=0)
            stretch = pull - weight * rise
            stretch_above = jnp.concatenate([stretch[1:], zero], axis=0)
            return field + (spring * (rise_above - rise) + (stretch - stretch_above))

        result[index] = lax.fori_loop(0, ZSTEPS, step, channel(c), unroll=True)
        outgoing(index).start()
        return carry

    lax.fori_loop(0, 2 * blocks, one, 0)
    for index in range(2 * blocks):
        outgoing(index).wait()


def per_device(
    in_plane_force, stiffness, stiffness_z, patch_dest, patch_pos, patch_flow, patch_conf
):
    groups = lax.axis_size("sec")
    tiles = lax.axis_size("tile")
    layers, rows, columns = stiffness.shape
    inner_rows = rows // groups
    width = patch_flow.shape[-1]
    blocks = columns // width
    count = patch_pos.shape[2]
    up = [(i, i + 1) for i in range(tiles - 1)]
    down = [(j, i) for i, j in up]

    def ends(field):
        cut = field.reshape(field.shape[0], layers, rows // HALO, HALO, columns)
        return cut[:, :, :: rows // HALO - 1]

    edges = jnp.pad(ends(in_plane_force), ((0, 1),) + ((0, 0),) * 4) + jnp.pad(ends(stiffness[None]), ((2, 0),) + ((0, 0),) * 4)
    before = lax.ppermute(edges[:, :, 1], "tile", up)
    after = lax.ppermute(edges[:, :, 0], "tile", down)
    mixed_shape = jax.ShapeDtypeStruct((groups, 5, layers, inner_rows, columns), jnp.float32)
    mixed = pl.pallas_call(
        inner_kernel,
        out_shape=mixed_shape,
        in_specs=[VMEM] * 6,
        out_specs=VMEM,
        scratch_shapes=relax_scratch(layers, blocks, rows, width),
        compiler_params=LIMIT,
        cost_estimate=pl.CostEstimate(flops=10**9, bytes_accessed=10**7, transcendentals=0),
        name="spread_and_inner_rows",
    )(
        patch_dest.reshape(1, count),
        patch_pos.reshape(1, count),
        patch_flow.reshape(count * 2, width),
        patch_conf.reshape(count, width),
        in_plane_force,
        stiffness,
    )
    mixed = pl.pallas_call(
        ends_kernel,
        out_shape=mixed_shape,
        in_specs=[VMEM] * 5,
        out_specs=VMEM,
        scratch_shapes=relax_scratch(layers, blocks, 6 * HALO, width),
        compiler_params=LIMIT,
        cost_estimate=pl.CostEstimate(flops=10**7, bytes_accessed=10**6, transcendentals=0),
        name="end_rows",
    )(in_plane_force, stiffness, before, after, mixed)
    moved = lax.all_to_all(mixed, "sec", split_axis=0, concat_axis=0, tiled=True)
    return pl.pallas_call(
        cross_kernel,
        out_shape=jax.ShapeDtypeStruct((2, groups * layers, inner_rows, columns), jnp.float32),
        in_specs=[VMEM] * 2,
        out_specs=ANY,
        scratch_shapes=[
            pltpu.VMEM((2 * blocks, groups * layers, inner_rows, width), jnp.float32),
            pltpu.SemaphoreType.DMA((2 * blocks,)),
        ],
        compiler_params=LIMIT,
        cost_estimate=pl.CostEstimate(flops=10000000, bytes_accessed=800000, transcendentals=0),
        name="cross_steps",
    )(moved, stiffness_z)


def solution(mesh):
    placed = (
        P(None, "sec", "tile", None),
        P("sec", "tile", None),
        P(None, ("tile", "sec"), None),
        P("sec", "tile", None, None),
        P("sec", "tile", None),
        P("sec", "tile", None, None, None),
        P("sec", "tile", None, None),
    )
    return jax.shard_map(
        per_device,
        mesh=mesh,
        in_specs=placed,
        out_specs=P(None, None, ("tile", "sec"), None),
        check_vma=False,
    )
```

```python
import jax
import jax.numpy as jnp
from jax import lax
from jax.experimental import pallas as pl
from jax.experimental.pallas import tpu as pltpu
from jax.sharding import PartitionSpec as P

ISTEPS = 8
ZSTEPS = 8


STEP_PLANE = 0.12
STEP_CROSS = 0.15

HALO = -(-(ISTEPS - 1) // 8) * 8

VMEM = pl.BlockSpec(memory_space=pltpu.VMEM)
LIMIT = pltpu.CompilerParams(vmem_limit_bytes=8 * 1024 * 1024)
ANY = pl.BlockSpec(memory_space=pl.ANY)


def spread(layers, inner_rows, blocks, dest_ref, pos_ref, flow_ref, conf_ref, out_ref):
    groups = out_ref.shape[0]
    count, width = conf_ref.shape
    place = pos_ref[...]
    layer = place // (inner_rows * blocks)
    inner_row = place // blocks % inner_rows
    column_block = place % blocks
    slot = (dest_ref[...] * layers + layer) * inner_rows + inner_row
    slots = groups * layers * inner_rows
    conf = conf_ref[...]
    terms = [flow_ref[pl.ds(c, count, stride=2), :] * conf for c in range(2)] + [conf]
    rest = jnp.concatenate(terms, axis=1)
    parts = []
    for _ in range(3):
        parts.append(rest.astype(jnp.bfloat16))
        rest = rest - parts[-1].astype(jnp.float32)
    numbers = lax.broadcasted_iota(jnp.int32, (slots, count), 0)
    for b in range(blocks):
        key = jnp.where(column_block == b, slot, -1)
        hit = jnp.where(numbers == key, 1.0, 0.0).astype(jnp.bfloat16)
        total = sum(jnp.dot(hit, part, preferred_element_type=jnp.float32) for part in reversed(parts))
        for o in range(groups):
            for l in range(layers):
                start = (o * layers + l) * inner_rows
                for c in range(3):
                    out_ref[o, 2 + c, l, :, b * width : (b + 1) * width] = total[
                        start : start + inner_rows, c * width : (c + 1) * width
                    ]


def shifted(blocks, lane, width):
    ahead = [pltpu.roll(x, width - 1, 1) for x in blocks]
    behind = [pltpu.roll(x, 1, 1) for x in blocks]
    zero = jnp.zeros_like(blocks[0])
    right = [jnp.where(lane == width - 1, after, own) for own, after in zip(ahead, ahead[1:] + [zero])]
    left = [jnp.where(lane == 0, before, own) for own, before in zip(behind, [zero] + behind[:-1])]
    return left, right


def relax(held, springs, keeps, pushes, even, odd):
    _, layers, blocks, total, width = held.shape
    stride = total // 8
    lane = lax.broadcasted_iota(jnp.int32, (8, width), 1)
    places = [(j, b) for j in range(stride) for b in range(blocks)]

    for l in range(layers):
        for c in (2, 0, 1):
            for n, (j, b) in enumerate(places):
                part = STEP_PLANE * held[c, l, b, pl.ds(j, 8, stride=stride), :]
                if c == 2:
                    springs[l, n] = part
                    keeps[l, n] = 1.0 - 4.0 * part
                else:
                    pushes[l, c, n] = part

    def step(source, store):
        for l in range(layers):
            for c in range(2):
                field = [[source[l, c, j * blocks + b] for b in range(blocks)] for j in range(stride)]
                above = [[pltpu.roll(x, 1, 0) for x in field[-1]]] + field[:-1]
                below = field[1:] + [[pltpu.roll(x, 7, 0) for x in field[0]]]
                for j in range(stride):
                    left, right = shifted(field[j], lane, width)
                    for b in range(blocks):
                        n = j * blocks + b
                        near = (above[j][b] + below[j][b]) + (left[b] + right[b])
                        store(l, c, n, springs[l, n] * near + (keeps[l, n] * field[j][b] + pushes[l, c, n]))

    def to(target):
        def store(l, c, n, value):
            target[l, c, n] = value

        return store

    def to_rows(l, c, n, value):
        j, b = places[n]
        held[c, l, b, pl.ds(j, 8, stride=stride), :] = value

    source = pushes
    for n in range(ISTEPS - 2):
        target = odd if n % 2 else even
        step(source, to(target))
        source = target
    step(source, to_rows)


def put_rows(held, out_ref, start, first, last):
    _, layers, blocks, _, width = held.shape
    inner_rows = out_ref.shape[3]
    for c in range(2):
        for l in range(layers):
            for b in range(blocks):
                for o in range(first // inner_rows, last // inner_rows):
                    at = start + o * inner_rows - first
                    out_ref[o, c, l, :, b * width : (b + 1) * width] = held[c, l, b, at : at + inner_rows, :]


def inner_kernel(dest_ref, pos_ref, flow_ref, conf_ref, own_ref, out_ref, edge_ref, held, *scratch):
    _, layers, rows, columns = own_ref.shape
    blocks, width = held.shape[2], held.shape[-1]
    spread(layers, out_ref.shape[3], blocks, dest_ref, pos_ref, flow_ref, conf_ref, out_ref)
    for b in range(blocks):
        held[:, :, b] = own_ref[:, :, :, b * width : (b + 1) * width]
    edge_ref[:, :, :, : 2 * HALO] = held[:, :, :, : 2 * HALO]
    edge_ref[:, :, :, 2 * HALO :] = held[:, :, :, rows - 2 * HALO :]
    relax(held, *scratch)
    put_rows(held, out_ref, HALO, HALO, rows - HALO)


def ends_kernel(edge_ref, before_ref, after_ref, mixed_ref, out_ref, held, *scratch):
    blocks, width = held.shape[2], held.shape[-1]
    rows = out_ref.shape[0] * out_ref.shape[3]
    edge = HALO // out_ref.shape[3]
    held[:, :, :, HALO : 5 * HALO] = edge_ref[...]
    for b in range(blocks):
        span = slice(b * width, (b + 1) * width)
        held[:, :, b, :HALO] = before_ref[:, :, :, span]
        held[:, :, b, 5 * HALO :] = after_ref[:, :, :, span]
    out_ref[:, 2:] = mixed_ref[:, 2:]
    out_ref[edge:-edge, :2] = mixed_ref[edge:-edge, :2]
    relax(held, *scratch)
    put_rows(held, out_ref, HALO, 0, HALO)
    put_rows(held, out_ref, 4 * HALO, rows - HALO, rows)


def relax_scratch(layers, blocks, total, width):
    parts = total // 8 * blocks
    return [pltpu.VMEM((3, layers, blocks, total, width), jnp.float32)] + [
        pltpu.VMEM((layers, parts, 8, width), jnp.float32),
        pltpu.VMEM((layers, parts, 8, width), jnp.float32),
        pltpu.VMEM((layers, 2, parts, 8, width), jnp.float32),
        pltpu.VMEM((layers, 2, parts, 8, width), jnp.float32),
        pltpu.VMEM((layers, 2, parts, 8, width), jnp.float32),
    ]


def cross_kernel(moved_ref, stiff_ref, out_ref, result, sems):
    groups, _, layers, inner_rows, columns = moved_ref.shape
    sections = groups * layers
    width = result.shape[-1]
    blocks = columns // width
    zero = jnp.zeros((1, inner_rows, width), jnp.float32)

    def outgoing(index):
        b, c = index // 2, index % 2
        span = pl.ds(pl.multiple_of(b * width, width), width)
        return pltpu.make_async_copy(result.at[index], out_ref.at[c, :, :, span], sems.at[index])

    def one(index, carry):
        b, c = index // 2, index % 2
        span = pl.ds(pl.multiple_of(b * width, width), width)

        def channel(c):
            return moved_ref[:, c, :, :, span].reshape(sections, inner_rows, width)

        spring = STEP_CROSS * stiff_ref[:, :, span]
        weight = STEP_CROSS * channel(4)
        pull = STEP_CROSS * channel(2 + c)

        def step(_, field):
            rise = field - jnp.concatenate([zero, field[:-1]], axis=0)
            rise_above = jnp.concatenate([rise[1:], -field[-1:]], axis=0)
            stretch = pull - weight * rise
            stretch_above = jnp.concatenate([stretch[1:], zero], axis=0)
            return field + (spring * (rise_above - rise) + (stretch - stretch_above))

        result[index] = lax.fori_loop(0, ZSTEPS, step, channel(c), unroll=True)
        outgoing(index).start()
        return carry

    lax.fori_loop(0, 2 * blocks, one, 0)
    for index in range(2 * blocks):
        outgoing(index).wait()


def per_device(
    in_plane_force, stiffness, stiffness_z, patch_dest, patch_pos, patch_flow, patch_conf
):
    groups = lax.axis_size("sec")
    tiles = lax.axis_size("tile")
    layers, rows, columns = stiffness.shape
    inner_rows = rows // groups
    width = patch_flow.shape[-1]
    blocks = columns // width
    count = patch_pos.shape[2]
    up = [(i, i + 1) for i in range(tiles - 1)]
    down = [(j, i) for i, j in up]

    rest = ((0, 0),) * 3
    own = jnp.pad(in_plane_force, ((0, 1),) + rest) + jnp.pad(stiffness[None], ((2, 0),) + rest)

    before = lax.ppermute(own[:, :, rows - HALO :], "tile", up)
    after = lax.ppermute(own[:, :, :HALO], "tile", down)
    mixed_shape = jax.ShapeDtypeStruct((groups, 5, layers, inner_rows, columns), jnp.float32)
    mixed, own_edges = pl.pallas_call(
        inner_kernel,
        out_shape=[mixed_shape, jax.ShapeDtypeStruct((3, layers, blocks, 4 * HALO, width), jnp.float32)],
        in_specs=[VMEM] * 5,
        out_specs=[VMEM] * 2,
        scratch_shapes=relax_scratch(layers, blocks, rows, width),
        compiler_params=LIMIT,
        cost_estimate=pl.CostEstimate(flops=10**9, bytes_accessed=10**7, transcendentals=0),
        name="spread_and_inner_rows",
    )(
        patch_dest.reshape(1, count),
        patch_pos.reshape(1, count),
        patch_flow.reshape(count * 2, width),
        patch_conf.reshape(count, width),
        own,
    )
    mixed = pl.pallas_call(
        ends_kernel,
        out_shape=mixed_shape,
        in_specs=[VMEM] * 4,
        out_specs=VMEM,
        scratch_shapes=relax_scratch(layers, blocks, 6 * HALO, width),
        compiler_params=LIMIT,
        cost_estimate=pl.CostEstimate(flops=10**7, bytes_accessed=10**6, transcendentals=0),
        name="end_rows",
    )(own_edges, before, after, mixed)
    moved = lax.all_to_all(mixed, "sec", split_axis=0, concat_axis=0, tiled=True)
    return pl.pallas_call(
        cross_kernel,
        out_shape=jax.ShapeDtypeStruct((2, groups * layers, inner_rows, columns), jnp.float32),
        in_specs=[VMEM] * 2,
        out_specs=ANY,
        scratch_shapes=[
            pltpu.VMEM((2 * blocks, groups * layers, inner_rows, width), jnp.float32),
            pltpu.SemaphoreType.DMA((2 * blocks,)),
        ],
        compiler_params=LIMIT,
        cost_estimate=pl.CostEstimate(flops=10000000, bytes_accessed=800000, transcendentals=0),
        name="cross_steps",
    )(moved, stiffness_z)


def solution(mesh):
    placed = (
        P(None, "sec", "tile", None),
        P("sec", "tile", None),
        P(None, ("tile", "sec"), None),
        P("sec", "tile", None, None),
        P("sec", "tile", None),
        P("sec", "tile", None, None, None),
        P("sec", "tile", None, None),
    )
    return jax.shard_map(
        per_device,
        mesh=mesh,
        in_specs=placed,
        out_specs=P(None, None, ("tile", "sec"), None),
        check_vma=False,
    )
```

```python
import jax
import jax.numpy as jnp
from jax import lax
from jax.experimental import pallas as pl
from jax.experimental.pallas import tpu as pltpu
from jax.sharding import PartitionSpec as P

ISTEPS = 8
ZSTEPS = 8


STEP_PLANE = 0.12
STEP_CROSS = 0.15

HALO = -(-(ISTEPS - 1) // 8) * 8

VMEM = pl.BlockSpec(memory_space=pltpu.VMEM)
LIMIT = pltpu.CompilerParams(vmem_limit_bytes=8 * 1024 * 1024)
ANY = pl.BlockSpec(memory_space=pl.ANY)


def spread(layers, inner_rows, blocks, dest_ref, pos_ref, flow_ref, conf_ref, out_ref):
    groups = out_ref.shape[0]
    count, width = conf_ref.shape
    place = pos_ref[...]
    layer = place // (inner_rows * blocks)
    inner_row = place // blocks % inner_rows
    column_block = place % blocks
    slot = (dest_ref[...] * layers + layer) * inner_rows + inner_row
    slots = groups * layers * inner_rows
    conf = conf_ref[...]
    terms = [flow_ref[pl.ds(c, count, stride=2), :] * conf for c in range(2)] + [conf]
    rest = jnp.concatenate(terms, axis=1)
    parts = []
    for _ in range(3):
        parts.append(rest.astype(jnp.bfloat16))
        rest = rest - parts[-1].astype(jnp.float32)
    numbers = lax.broadcasted_iota(jnp.int32, (slots, count), 0)
    for b in range(blocks):
        key = jnp.where(column_block == b, slot, -1)
        hit = jnp.where(numbers == key, 1.0, 0.0).astype(jnp.bfloat16)
        total = sum(jnp.dot(hit, part, preferred_element_type=jnp.float32) for part in reversed(parts))
        for o in range(groups):
            for l in range(layers):
                start = (o * layers + l) * inner_rows
                for c in range(3):
                    out_ref[o, 2 + c, l, :, b * width : (b + 1) * width] = total[
                        start : start + inner_rows, c * width : (c + 1) * width
                    ]


def shifted(blocks, lane, width):
    ahead = [pltpu.roll(x, width - 1, 1) for x in blocks]
    behind = [pltpu.roll(x, 1, 1) for x in blocks]
    zero = jnp.zeros_like(blocks[0])
    right = [jnp.where(lane == width - 1, after, own) for own, after in zip(ahead, ahead[1:] + [zero])]
    left = [jnp.where(lane == 0, before, own) for own, before in zip(behind, [zero] + behind[:-1])]
    return left, right


def relax(held, springs, keeps, pushes, even, odd):
    _, layers, blocks, total, width = held.shape
    stride = total // 8
    lane = lax.broadcasted_iota(jnp.int32, (8, width), 1)
    places = [(j, b) for j in range(stride) for b in range(blocks)]

    for l in range(layers):
        for c in (2, 0, 1):
            for n, (j, b) in enumerate(places):
                part = STEP_PLANE * held[c, l, b, pl.ds(j, 8, stride=stride), :]
                if c == 2:
                    springs[l, n] = part
                    keeps[l, n] = 1.0 - 4.0 * part
                else:
                    pushes[l, c, n] = part

    def step(source, store):
        for l in range(layers):
            for c in range(2):
                field = [[source[l, c, j * blocks + b] for b in range(blocks)] for j in range(stride)]
                above = [[pltpu.roll(x, 1, 0) for x in field[-1]]] + field[:-1]
                below = field[1:] + [[pltpu.roll(x, 7, 0) for x in field[0]]]
                for j in range(stride):
                    left, right = shifted(field[j], lane, width)
                    for b in range(blocks):
                        n = j * blocks + b
                        near = (above[j][b] + below[j][b]) + (left[b] + right[b])
                        store(l, c, n, springs[l, n] * near + (keeps[l, n] * field[j][b] + pushes[l, c, n]))

    def to(target):
        def store(l, c, n, value):
            target[l, c, n] = value

        return store

    def to_rows(l, c, n, value):
        j, b = places[n]
        held[c, l, b, pl.ds(j, 8, stride=stride), :] = value

    source = pushes
    for n in range(ISTEPS - 2):
        target = odd if n % 2 else even
        step(source, to(target))
        source = target
    step(source, to_rows)


def put_rows(held, out_ref, start, first, last):
    _, layers, blocks, _, width = held.shape
    inner_rows = out_ref.shape[3]
    for c in range(2):
        for l in range(layers):
            for b in range(blocks):
                for o in range(first // inner_rows, last // inner_rows):
                    at = start + o * inner_rows - first
                    out_ref[o, c, l, :, b * width : (b + 1) * width] = held[c, l, b, at : at + inner_rows, :]


def inner_kernel(dest_ref, pos_ref, flow_ref, conf_ref, own_ref, out_ref, edge_ref, held, *scratch):
    _, layers, rows, columns = own_ref.shape
    blocks, width = held.shape[2], held.shape[-1]
    spread(layers, out_ref.shape[3], blocks, dest_ref, pos_ref, flow_ref, conf_ref, out_ref)
    for b in range(blocks):
        held[:, :, b] = own_ref[:, :, :, b * width : (b + 1) * width]
    edge_ref[:, :, :, : 2 * HALO] = held[:, :, :, : 2 * HALO]
    edge_ref[:, :, :, 2 * HALO :] = held[:, :, :, rows - 2 * HALO :]
    relax(held, *scratch)
    put_rows(held, out_ref, HALO, HALO, rows - HALO)


def ends_kernel(odd_ref, edge_ref, two_ref, one_ref, mixed_ref, out_ref, held, *scratch):
    blocks, width = held.shape[2], held.shape[-1]
    rows = out_ref.shape[0] * out_ref.shape[3]
    edge = HALO // out_ref.shape[3]
    held[:, :, :, HALO : 5 * HALO] = edge_ref[...]
    odd = odd_ref[0] == 1
    for b in range(blocks):
        span = slice(b * width, (b + 1) * width)
        one, two = one_ref[:, :, :, span], two_ref[:, :, :, span]
        held[:, :, b, :HALO] = jnp.where(odd, one, two)
        held[:, :, b, 5 * HALO :] = jnp.where(odd, two, one)
    out_ref[:, 2:] = mixed_ref[:, 2:]
    out_ref[edge:-edge, :2] = mixed_ref[edge:-edge, :2]
    relax(held, *scratch)
    put_rows(held, out_ref, HALO, 0, HALO)
    put_rows(held, out_ref, 4 * HALO, rows - HALO, rows)


def relax_scratch(layers, blocks, total, width):
    parts = total // 8 * blocks
    return [pltpu.VMEM((3, layers, blocks, total, width), jnp.float32)] + [
        pltpu.VMEM((layers, parts, 8, width), jnp.float32),
        pltpu.VMEM((layers, parts, 8, width), jnp.float32),
        pltpu.VMEM((layers, 2, parts, 8, width), jnp.float32),
        pltpu.VMEM((layers, 2, parts, 8, width), jnp.float32),
        pltpu.VMEM((layers, 2, parts, 8, width), jnp.float32),
    ]


def cross_kernel(moved_ref, stiff_ref, out_ref, result, sems):
    groups, _, layers, inner_rows, columns = moved_ref.shape
    sections = groups * layers
    width = result.shape[-1]
    blocks = columns // width
    zero = jnp.zeros((1, inner_rows, width), jnp.float32)

    def outgoing(index):
        b, c = index // 2, index % 2
        span = pl.ds(pl.multiple_of(b * width, width), width)
        return pltpu.make_async_copy(result.at[index], out_ref.at[c, :, :, span], sems.at[index])

    def one(index, carry):
        b, c = index // 2, index % 2
        span = pl.ds(pl.multiple_of(b * width, width), width)

        def channel(c):
            return moved_ref[:, c, :, :, span].reshape(sections, inner_rows, width)

        spring = STEP_CROSS * stiff_ref[:, :, span]
        weight = STEP_CROSS * channel(4)
        pull = STEP_CROSS * channel(2 + c)

        def step(_, field):
            rise = field - jnp.concatenate([zero, field[:-1]], axis=0)
            rise_above = jnp.concatenate([rise[1:], -field[-1:]], axis=0)
            stretch = pull - weight * rise
            stretch_above = jnp.concatenate([stretch[1:], zero], axis=0)
            return field + (spring * (rise_above - rise) + (stretch - stretch_above))

        result[index] = lax.fori_loop(0, ZSTEPS, step, channel(c), unroll=True)
        outgoing(index).start()
        return carry

    lax.fori_loop(0, 2 * blocks, one, 0)
    for index in range(2 * blocks):
        outgoing(index).wait()


def per_device(
    in_plane_force, stiffness, stiffness_z, patch_dest, patch_pos, patch_flow, patch_conf
):
    groups = lax.axis_size("sec")
    tiles = lax.axis_size("tile")
    layers, rows, columns = stiffness.shape
    inner_rows = rows // groups
    width = patch_flow.shape[-1]
    blocks = columns // width
    count = patch_pos.shape[2]
    swaps = [[pair for i in range(n, tiles - 1, 2) for pair in ((i, i + 1), (i + 1, i))] for n in range(2)]
    odd = lax.axis_index("tile") & 1

    rest = ((0, 0),) * 3
    own = jnp.pad(in_plane_force, ((0, 1),) + rest) + jnp.pad(stiffness[None], ((2, 0),) + rest)

    first, last = own[:, :, :HALO], own[:, :, rows - HALO :]
    two = lax.ppermute(jnp.where(odd == 1, last, first), "tile", swaps[1])
    one = lax.ppermute(jnp.where(odd == 1, first, last), "tile", swaps[0])
    mixed_shape = jax.ShapeDtypeStruct((groups, 5, layers, inner_rows, columns), jnp.float32)
    mixed, own_edges = pl.pallas_call(
        inner_kernel,
        out_shape=[mixed_shape, jax.ShapeDtypeStruct((3, layers, blocks, 4 * HALO, width), jnp.float32)],
        in_specs=[VMEM] * 5,
        out_specs=[VMEM] * 2,
        scratch_shapes=relax_scratch(layers, blocks, rows, width),
        compiler_params=LIMIT,
        cost_estimate=pl.CostEstimate(flops=10**9, bytes_accessed=10**7, transcendentals=0),
        name="spread_and_inner_rows",
    )(
        patch_dest.reshape(1, count),
        patch_pos.reshape(1, count),
        patch_flow.reshape(count * 2, width),
        patch_conf.reshape(count, width),
        own,
    )
    mixed = pl.pallas_call(
        ends_kernel,
        out_shape=mixed_shape,
        in_specs=[pl.BlockSpec(memory_space=pltpu.SMEM)] + [VMEM] * 4,
        out_specs=VMEM,
        scratch_shapes=relax_scratch(layers, blocks, 6 * HALO, width),
        compiler_params=LIMIT,
        cost_estimate=pl.CostEstimate(flops=10**7, bytes_accessed=10**6, transcendentals=0),
        name="end_rows",
    )(odd.reshape(1), own_edges, two, one, mixed)
    moved = lax.all_to_all(mixed, "sec", split_axis=0, concat_axis=0, tiled=True)
    return pl.pallas_call(
        cross_kernel,
        out_shape=jax.ShapeDtypeStruct((2, groups * layers, inner_rows, columns), jnp.float32),
        in_specs=[VMEM] * 2,
        out_specs=ANY,
        scratch_shapes=[
            pltpu.VMEM((2 * blocks, groups * layers, inner_rows, width), jnp.float32),
            pltpu.SemaphoreType.DMA((2 * blocks,)),
        ],
        compiler_params=LIMIT,
        cost_estimate=pl.CostEstimate(flops=10000000, bytes_accessed=800000, transcendentals=0),
        name="cross_steps",
    )(moved, stiffness_z)


def solution(mesh):
    placed = (
        P(None, "sec", "tile", None),
        P("sec", "tile", None),
        P(None, ("tile", "sec"), None),
        P("sec", "tile", None, None),
        P("sec", "tile", None),
        P("sec", "tile", None, None, None),
        P("sec", "tile", None, None),
    )
    return jax.shard_map(
        per_device,
        mesh=mesh,
        in_specs=placed,
        out_specs=P(None, None, ("tile", "sec"), None),
        check_vma=False,
    )
```

```python
import functools

import jax
import jax.numpy as jnp
from jax import lax
from jax.experimental import pallas as pl
from jax.experimental.pallas import tpu as pltpu
from jax.sharding import PartitionSpec as P

ISTEPS = 8
ZSTEPS = 8


STEP_PLANE = 0.12
STEP_CROSS = 0.15

HALO = -(-(ISTEPS - 1) // 8) * 8

VMEM = pl.BlockSpec(memory_space=pltpu.VMEM)
LIMIT = pltpu.CompilerParams(vmem_limit_bytes=8 * 1024 * 1024)
ANY = pl.BlockSpec(memory_space=pl.ANY)


def spread(layers, inner_rows, blocks, dest_ref, pos_ref, flow_ref, conf_ref, out_ref):
    groups = out_ref.shape[0]
    count, width = conf_ref.shape
    place = pos_ref[...]
    layer = place // (inner_rows * blocks)
    inner_row = place // blocks % inner_rows
    column_block = place % blocks
    slot = (dest_ref[...] * layers + layer) * inner_rows + inner_row
    slots = groups * layers * inner_rows
    conf = conf_ref[...]
    terms = [flow_ref[pl.ds(c, count, stride=2), :] * conf for c in range(2)] + [conf]
    rest = jnp.concatenate(terms, axis=1)
    parts = []
    for _ in range(3):
        parts.append(rest.astype(jnp.bfloat16))
        rest = rest - parts[-1].astype(jnp.float32)
    numbers = lax.broadcasted_iota(jnp.int32, (slots, count), 0)
    for b in range(blocks):
        key = jnp.where(column_block == b, slot, -1)
        hit = jnp.where(numbers == key, 1.0, 0.0).astype(jnp.bfloat16)
        total = sum(jnp.dot(hit, part, preferred_element_type=jnp.float32) for part in reversed(parts))
        for o in range(groups):
            for l in range(layers):
                start = (o * layers + l) * inner_rows
                for c in range(3):
                    out_ref[o, 2 + c, l, :, b * width : (b + 1) * width] = total[
                        start : start + inner_rows, c * width : (c + 1) * width
                    ]


def shifted(blocks, lane, width):
    ahead = [pltpu.roll(x, width - 1, 1) for x in blocks]
    behind = [pltpu.roll(x, 1, 1) for x in blocks]
    zero = jnp.zeros_like(blocks[0])
    right = [jnp.where(lane == width - 1, after, own) for own, after in zip(ahead, ahead[1:] + [zero])]
    left = [jnp.where(lane == 0, before, own) for own, before in zip(behind, [zero] + behind[:-1])]
    return left, right


def relax(held, springs, keeps, pushes, even, odd):
    _, layers, blocks, total, width = held.shape
    stride = total // 8
    lane = lax.broadcasted_iota(jnp.int32, (8, width), 1)
    places = [(j, b) for j in range(stride) for b in range(blocks)]

    for l in range(layers):
        for c in (2, 0, 1):
            for n, (j, b) in enumerate(places):
                part = STEP_PLANE * held[c, l, b, pl.ds(j, 8, stride=stride), :]
                if c == 2:
                    springs[l, n] = part
                    keeps[l, n] = 1.0 - 4.0 * part
                else:
                    pushes[l, c, n] = part

    def step(source, store):
        for l in range(layers):
            for c in range(2):
                field = [[source[l, c, j * blocks + b] for b in range(blocks)] for j in range(stride)]
                above = [[pltpu.roll(x, 1, 0) for x in field[-1]]] + field[:-1]
                below = field[1:] + [[pltpu.roll(x, 7, 0) for x in field[0]]]
                for j in range(stride):
                    left, right = shifted(field[j], lane, width)
                    for b in range(blocks):
                        n = j * blocks + b
                        near = (above[j][b] + below[j][b]) + (left[b] + right[b])
                        store(l, c, n, springs[l, n] * near + (keeps[l, n] * field[j][b] + pushes[l, c, n]))

    def to(target):
        def store(l, c, n, value):
            target[l, c, n] = value

        return store

    def to_rows(l, c, n, value):
        j, b = places[n]
        held[c, l, b, pl.ds(j, 8, stride=stride), :] = value

    source = pushes
    for n in range(ISTEPS - 2):
        target = odd if n % 2 else even
        step(source, to(target))
        source = target
    step(source, to_rows)


def put_rows(held, out_ref, start, first, last):
    _, layers, blocks, _, width = held.shape
    inner_rows = out_ref.shape[3]
    for c in range(2):
        for l in range(layers):
            for b in range(blocks):
                for o in range(first // inner_rows, last // inner_rows):
                    at = start + o * inner_rows - first
                    out_ref[o, c, l, :, b * width : (b + 1) * width] = held[c, l, b, at : at + inner_rows, :]


def inner_kernel(dest_ref, pos_ref, flow_ref, conf_ref, own_ref, out_ref, edge_ref, held, *scratch):
    _, layers, rows, columns = own_ref.shape
    blocks, width = held.shape[2], held.shape[-1]
    spread(layers, out_ref.shape[3], blocks, dest_ref, pos_ref, flow_ref, conf_ref, out_ref)
    for b in range(blocks):
        held[:, :, b] = own_ref[:, :, :, b * width : (b + 1) * width]
    edge_ref[:, :, :, : 2 * HALO] = held[:, :, :, : 2 * HALO]
    edge_ref[:, :, :, 2 * HALO :] = held[:, :, :, rows - 2 * HALO :]
    relax(held, *scratch)
    put_rows(held, out_ref, HALO, HALO, rows - HALO)


def ends_kernel(tiles, tile_ref, edge_ref, two_ref, one_ref, mixed_ref, out_ref, held, *scratch):
    blocks, width = held.shape[2], held.shape[-1]
    rows = out_ref.shape[0] * out_ref.shape[3]
    edge = HALO // out_ref.shape[3]
    held[:, :, :, HALO : 5 * HALO] = edge_ref[...]
    tile = tile_ref[0]
    odd = (tile & 1) == 1
    for b in range(blocks):
        span = slice(b * width, (b + 1) * width)
        one, two = one_ref[:, :, :, span], two_ref[:, :, :, span]
        held[:, :, b, :HALO] = jnp.where(tile == 0, 0.0, jnp.where(odd, one, two))
        held[:, :, b, 5 * HALO :] = jnp.where(tile == tiles - 1, 0.0, jnp.where(odd, two, one))
    out_ref[:, 2:] = mixed_ref[:, 2:]
    out_ref[edge:-edge, :2] = mixed_ref[edge:-edge, :2]
    relax(held, *scratch)
    put_rows(held, out_ref, HALO, 0, HALO)
    put_rows(held, out_ref, 4 * HALO, rows - HALO, rows)


def relax_scratch(layers, blocks, total, width):
    parts = total // 8 * blocks
    return [pltpu.VMEM((3, layers, blocks, total, width), jnp.float32)] + [
        pltpu.VMEM((layers, parts, 8, width), jnp.float32),
        pltpu.VMEM((layers, parts, 8, width), jnp.float32),
        pltpu.VMEM((layers, 2, parts, 8, width), jnp.float32),
        pltpu.VMEM((layers, 2, parts, 8, width), jnp.float32),
        pltpu.VMEM((layers, 2, parts, 8, width), jnp.float32),
    ]


def cross_kernel(moved_ref, stiff_ref, out_ref, result, sems):
    groups, _, layers, inner_rows, columns = moved_ref.shape
    sections = groups * layers
    width = result.shape[-1]
    blocks = columns // width
    zero = jnp.zeros((1, inner_rows, width), jnp.float32)

    def outgoing(index):
        b, c = index // 2, index % 2
        span = pl.ds(pl.multiple_of(b * width, width), width)
        return pltpu.make_async_copy(result.at[index], out_ref.at[c, :, :, span], sems.at[index])

    def one(index, carry):
        b, c = index // 2, index % 2
        span = pl.ds(pl.multiple_of(b * width, width), width)

        def channel(c):
            return moved_ref[:, c, :, :, span].reshape(sections, inner_rows, width)

        spring = STEP_CROSS * stiff_ref[:, :, span]
        weight = STEP_CROSS * channel(4)
        pull = STEP_CROSS * channel(2 + c)

        def step(_, field):
            rise = field - jnp.concatenate([zero, field[:-1]], axis=0)
            rise_above = jnp.concatenate([rise[1:], -field[-1:]], axis=0)
            stretch = pull - weight * rise
            stretch_above = jnp.concatenate([stretch[1:], zero], axis=0)
            return field + (spring * (rise_above - rise) + (stretch - stretch_above))

        result[index] = lax.fori_loop(0, ZSTEPS, step, channel(c), unroll=True)
        outgoing(index).start()
        return carry

    lax.fori_loop(0, 2 * blocks, one, 0)
    for index in range(2 * blocks):
        outgoing(index).wait()


def per_device(
    in_plane_force, stiffness, stiffness_z, patch_dest, patch_pos, patch_flow, patch_conf
):
    groups = lax.axis_size("sec")
    tiles = lax.axis_size("tile")
    layers, rows, columns = stiffness.shape
    inner_rows = rows // groups
    width = patch_flow.shape[-1]
    blocks = columns // width
    count = patch_pos.shape[2]
    swaps = []
    for n in range(2):
        other = [i + 1 if i % 2 == n else i - 1 for i in range(tiles)]
        swaps.append([(i, j if 0 <= j < tiles else i) for i, j in enumerate(other)])
    tile = lax.axis_index("tile")
    odd = tile & 1

    rest = ((0, 0),) * 3
    own = jnp.pad(in_plane_force, ((0, 1),) + rest) + jnp.pad(stiffness[None], ((2, 0),) + rest)

    first, last = own[:, :, :HALO], own[:, :, rows - HALO :]
    two = lax.ppermute(jnp.where(odd == 1, last, first), "tile", swaps[1])
    one = lax.ppermute(jnp.where(odd == 1, first, last), "tile", swaps[0])
    mixed_shape = jax.ShapeDtypeStruct((groups, 5, layers, inner_rows, columns), jnp.float32)
    mixed, own_edges = pl.pallas_call(
        inner_kernel,
        out_shape=[mixed_shape, jax.ShapeDtypeStruct((3, layers, blocks, 4 * HALO, width), jnp.float32)],
        in_specs=[VMEM] * 5,
        out_specs=[VMEM] * 2,
        scratch_shapes=relax_scratch(layers, blocks, rows, width),
        compiler_params=LIMIT,
        cost_estimate=pl.CostEstimate(flops=10**9, bytes_accessed=10**7, transcendentals=0),
        name="spread_and_inner_rows",
    )(
        patch_dest.reshape(1, count),
        patch_pos.reshape(1, count),
        patch_flow.reshape(count * 2, width),
        patch_conf.reshape(count, width),
        own,
    )
    mixed = pl.pallas_call(
        functools.partial(ends_kernel, tiles),
        out_shape=mixed_shape,
        in_specs=[pl.BlockSpec(memory_space=pltpu.SMEM)] + [VMEM] * 4,
        out_specs=VMEM,
        scratch_shapes=relax_scratch(layers, blocks, 6 * HALO, width),
        compiler_params=LIMIT,
        cost_estimate=pl.CostEstimate(flops=10**7, bytes_accessed=10**6, transcendentals=0),
        name="end_rows",
    )(tile.reshape(1), own_edges, two, one, mixed)
    moved = lax.all_to_all(mixed, "sec", split_axis=0, concat_axis=0, tiled=True)
    return pl.pallas_call(
        cross_kernel,
        out_shape=jax.ShapeDtypeStruct((2, groups * layers, inner_rows, columns), jnp.float32),
        in_specs=[VMEM] * 2,
        out_specs=ANY,
        scratch_shapes=[
            pltpu.VMEM((2 * blocks, groups * layers, inner_rows, width), jnp.float32),
            pltpu.SemaphoreType.DMA((2 * blocks,)),
        ],
        compiler_params=LIMIT,
        cost_estimate=pl.CostEstimate(flops=10000000, bytes_accessed=800000, transcendentals=0),
        name="cross_steps",
    )(moved, stiffness_z)


def solution(mesh):
    placed = (
        P(None, "sec", "tile", None),
        P("sec", "tile", None),
        P(None, ("tile", "sec"), None),
        P("sec", "tile", None, None),
        P("sec", "tile", None),
        P("sec", "tile", None, None, None),
        P("sec", "tile", None, None),
    )
    return jax.shard_map(
        per_device,
        mesh=mesh,
        in_specs=placed,
        out_specs=P(None, None, ("tile", "sec"), None),
        check_vma=False,
    )
```

```python
import functools

import jax
import jax.numpy as jnp
from jax import lax
from jax.experimental import pallas as pl
from jax.experimental.pallas import tpu as pltpu
from jax.sharding import PartitionSpec as P

ISTEPS = 8
ZSTEPS = 8


STEP_PLANE = 0.12
STEP_CROSS = 0.15

HALO = -(-(ISTEPS - 1) // 8) * 8

VMEM = pl.BlockSpec(memory_space=pltpu.VMEM)
LIMIT = pltpu.CompilerParams(vmem_limit_bytes=8 * 1024 * 1024)
ANY = pl.BlockSpec(memory_space=pl.ANY)


def spread(layers, inner_rows, blocks, dest_ref, pos_ref, flow_ref, conf_ref, out_ref):
    groups = out_ref.shape[0]
    count, width = conf_ref.shape
    place = pos_ref[...]
    layer = place // (inner_rows * blocks)
    inner_row = place // blocks % inner_rows
    column_block = place % blocks
    slot = (dest_ref[...] * layers + layer) * inner_rows + inner_row
    slots = groups * layers * inner_rows
    conf = conf_ref[...]
    terms = [flow_ref[pl.ds(c, count, stride=2), :] * conf for c in range(2)] + [conf]
    rest = jnp.concatenate(terms, axis=1)
    parts = []
    for _ in range(3):
        parts.append(rest.astype(jnp.bfloat16))
        rest = rest - parts[-1].astype(jnp.float32)
    numbers = lax.broadcasted_iota(jnp.int32, (slots, count), 0)
    for b in range(blocks):
        key = jnp.where(column_block == b, slot, -1)
        hit = jnp.where(numbers == key, 1.0, 0.0).astype(jnp.bfloat16)
        total = sum(jnp.dot(hit, part, preferred_element_type=jnp.float32) for part in reversed(parts))
        for o in range(groups):
            for l in range(layers):
                start = (o * layers + l) * inner_rows
                for c in range(3):
                    out_ref[o, 2 + c, l, :, b * width : (b + 1) * width] = total[
                        start : start + inner_rows, c * width : (c + 1) * width
                    ]


def shifted(blocks, lane, width):
    ahead = [pltpu.roll(x, width - 1, 1) for x in blocks]
    behind = [pltpu.roll(x, 1, 1) for x in blocks]
    zero = jnp.zeros_like(blocks[0])
    right = [jnp.where(lane == width - 1, after, own) for own, after in zip(ahead, ahead[1:] + [zero])]
    left = [jnp.where(lane == 0, before, own) for own, before in zip(behind, [zero] + behind[:-1])]
    return left, right


def relax(held, springs, keeps, pushes, even, odd):
    _, layers, blocks, total, width = held.shape
    stride = total // 8
    lane = lax.broadcasted_iota(jnp.int32, (8, width), 1)
    places = [(j, b) for j in range(stride) for b in range(blocks)]

    for l in range(layers):
        for c in (2, 0, 1):
            for n, (j, b) in enumerate(places):
                part = STEP_PLANE * held[c, l, b, pl.ds(j, 8, stride=stride), :]
                if c == 2:
                    springs[l, n] = part
                    keeps[l, n] = 1.0 - 4.0 * part
                else:
                    pushes[l, c, n] = part

    def step(source, store):
        for l in range(layers):
            for c in range(2):
                field = [[source[l, c, j * blocks + b] for b in range(blocks)] for j in range(stride)]
                above = [[pltpu.roll(x, 1, 0) for x in field[-1]]] + field[:-1]
                below = field[1:] + [[pltpu.roll(x, 7, 0) for x in field[0]]]
                for j in range(stride):
                    left, right = shifted(field[j], lane, width)
                    for b in range(blocks):
                        n = j * blocks + b
                        near = (above[j][b] + below[j][b]) + (left[b] + right[b])
                        store(l, c, n, springs[l, n] * near + (keeps[l, n] * field[j][b] + pushes[l, c, n]))

    def to(target):
        def store(l, c, n, value):
            target[l, c, n] = value

        return store

    def to_rows(l, c, n, value):
        j, b = places[n]
        held[c, l, b, pl.ds(j, 8, stride=stride), :] = value

    source = pushes
    for n in range(ISTEPS - 2):
        target = odd if n % 2 else even
        step(source, to(target))
        source = target
    step(source, to_rows)


def put_rows(held, out_ref, start, first, last):
    _, layers, blocks, _, width = held.shape
    inner_rows = out_ref.shape[3]
    for c in range(2):
        for l in range(layers):
            for b in range(blocks):
                for o in range(first // inner_rows, last // inner_rows):
                    at = start + o * inner_rows - first
                    out_ref[o, c, l, :, b * width : (b + 1) * width] = held[c, l, b, at : at + inner_rows, :]


def inner_kernel(dest_ref, pos_ref, flow_ref, conf_ref, own_ref, out_ref, edge_ref, held, *scratch):
    _, layers, rows, columns = own_ref.shape
    blocks, width = held.shape[2], held.shape[-1]
    spread(layers, out_ref.shape[3], blocks, dest_ref, pos_ref, flow_ref, conf_ref, out_ref)
    for b in range(blocks):
        held[:, :, b] = own_ref[:, :, :, b * width : (b + 1) * width]
    edge_ref[:, :, :, : 2 * HALO] = held[:, :, :, : 2 * HALO]
    edge_ref[:, :, :, 2 * HALO :] = held[:, :, :, rows - 2 * HALO :]
    relax(held, *scratch)
    put_rows(held, out_ref, HALO, HALO, rows - HALO)


def ends_kernel(tiles, tile_ref, edge_ref, one_ref, two_ref, mixed_ref, out_ref, held, *scratch):
    blocks, width = held.shape[2], held.shape[-1]
    rows = out_ref.shape[0] * out_ref.shape[3]
    edge = HALO // out_ref.shape[3]
    held[:, :, :, HALO : 5 * HALO] = edge_ref[...]
    tile = tile_ref[0]
    odd = (tile & 1) == 1
    for b in range(blocks):
        span = slice(b * width, (b + 1) * width)
        one, two = one_ref[:, :, :, span], two_ref[:, :, :, span]
        held[:, :, b, :HALO] = jnp.where(tile == 0, 0.0, jnp.where(odd, one, two))
        held[:, :, b, 5 * HALO :] = jnp.where(tile == tiles - 1, 0.0, jnp.where(odd, two, one))
    out_ref[:, 2:] = mixed_ref[:, 2:]
    out_ref[edge:-edge, :2] = mixed_ref[edge:-edge, :2]
    relax(held, *scratch)
    put_rows(held, out_ref, HALO, 0, HALO)
    put_rows(held, out_ref, 4 * HALO, rows - HALO, rows)


def relax_scratch(layers, blocks, total, width):
    parts = total // 8 * blocks
    return [pltpu.VMEM((3, layers, blocks, total, width), jnp.float32)] + [
        pltpu.VMEM((layers, parts, 8, width), jnp.float32),
        pltpu.VMEM((layers, parts, 8, width), jnp.float32),
        pltpu.VMEM((layers, 2, parts, 8, width), jnp.float32),
        pltpu.VMEM((layers, 2, parts, 8, width), jnp.float32),
        pltpu.VMEM((layers, 2, parts, 8, width), jnp.float32),
    ]


def cross_kernel(moved_ref, stiff_ref, out_ref, result, sems):
    groups, _, layers, inner_rows, columns = moved_ref.shape
    sections = groups * layers
    width = result.shape[-1]
    blocks = columns // width
    zero = jnp.zeros((1, inner_rows, width), jnp.float32)

    def outgoing(index):
        b, c = index // 2, index % 2
        span = pl.ds(pl.multiple_of(b * width, width), width)
        return pltpu.make_async_copy(result.at[index], out_ref.at[c, :, :, span], sems.at[index])

    def one(index, carry):
        b, c = index // 2, index % 2
        span = pl.ds(pl.multiple_of(b * width, width), width)

        def channel(c):
            return moved_ref[:, c, :, :, span].reshape(sections, inner_rows, width)

        spring = STEP_CROSS * stiff_ref[:, :, span]
        weight = STEP_CROSS * channel(4)
        pull = STEP_CROSS * channel(2 + c)

        def step(_, field):
            rise = field - jnp.concatenate([zero, field[:-1]], axis=0)
            rise_above = jnp.concatenate([rise[1:], -field[-1:]], axis=0)
            stretch = pull - weight * rise
            stretch_above = jnp.concatenate([stretch[1:], zero], axis=0)
            return field + (spring * (rise_above - rise) + (stretch - stretch_above))

        result[index] = lax.fori_loop(0, ZSTEPS, step, channel(c), unroll=True)
        outgoing(index).start()
        return carry

    lax.fori_loop(0, 2 * blocks, one, 0)
    for index in range(2 * blocks):
        outgoing(index).wait()


def per_device(
    in_plane_force, stiffness, stiffness_z, patch_dest, patch_pos, patch_flow, patch_conf
):
    groups = lax.axis_size("sec")
    tiles = lax.axis_size("tile")
    layers, rows, columns = stiffness.shape
    inner_rows = rows // groups
    width = patch_flow.shape[-1]
    blocks = columns // width
    count = patch_pos.shape[2]
    swaps = []
    for n in range(2):
        other = [i + 1 if i % 2 == n else i - 1 for i in range(tiles)]
        swaps.append([(i, j if 0 <= j < tiles else i) for i, j in enumerate(other)])
    tile = lax.axis_index("tile")
    odd = tile & 1

    rest = ((0, 0),) * 3
    own = jnp.pad(in_plane_force, ((0, 1),) + rest) + jnp.pad(stiffness[None], ((2, 0),) + rest)

    first, last = own[:, :, :HALO], own[:, :, rows - HALO :]
    one = lax.ppermute(jnp.where(odd == 1, first, last), "tile", swaps[0])
    two = lax.ppermute(jnp.where(odd == 1, last, first), "tile", swaps[1])
    mixed_shape = jax.ShapeDtypeStruct((groups, 5, layers, inner_rows, columns), jnp.float32)
    mixed, own_edges = pl.pallas_call(
        inner_kernel,
        out_shape=[mixed_shape, jax.ShapeDtypeStruct((3, layers, blocks, 4 * HALO, width), jnp.float32)],
        in_specs=[VMEM] * 5,
        out_specs=[VMEM] * 2,
        scratch_shapes=relax_scratch(layers, blocks, rows, width),
        compiler_params=LIMIT,
        cost_estimate=pl.CostEstimate(flops=10**9, bytes_accessed=10**7, transcendentals=0),
        name="spread_and_inner_rows",
    )(
        patch_dest.reshape(1, count),
        patch_pos.reshape(1, count),
        patch_flow.reshape(count * 2, width),
        patch_conf.reshape(count, width),
        own,
    )
    mixed = pl.pallas_call(
        functools.partial(ends_kernel, tiles),
        out_shape=mixed_shape,
        in_specs=[pl.BlockSpec(memory_space=pltpu.SMEM)] + [VMEM] * 4,
        out_specs=VMEM,
        scratch_shapes=relax_scratch(layers, blocks, 6 * HALO, width),
        compiler_params=LIMIT,
        cost_estimate=pl.CostEstimate(flops=10**7, bytes_accessed=10**6, transcendentals=0),
        name="end_rows",
    )(tile.reshape(1), own_edges, one, two, mixed)
    moved = lax.all_to_all(mixed, "sec", split_axis=0, concat_axis=0, tiled=True)
    return pl.pallas_call(
        cross_kernel,
        out_shape=jax.ShapeDtypeStruct((2, groups * layers, inner_rows, columns), jnp.float32),
        in_specs=[VMEM] * 2,
        out_specs=ANY,
        scratch_shapes=[
            pltpu.VMEM((2 * blocks, groups * layers, inner_rows, width), jnp.float32),
            pltpu.SemaphoreType.DMA((2 * blocks,)),
        ],
        compiler_params=LIMIT,
        cost_estimate=pl.CostEstimate(flops=10000000, bytes_accessed=800000, transcendentals=0),
        name="cross_steps",
    )(moved, stiffness_z)


def solution(mesh):
    placed = (
        P(None, "sec", "tile", None),
        P("sec", "tile", None),
        P(None, ("tile", "sec"), None),
        P("sec", "tile", None, None),
        P("sec", "tile", None),
        P("sec", "tile", None, None, None),
        P("sec", "tile", None, None),
    )
    return jax.shard_map(
        per_device,
        mesh=mesh,
        in_specs=placed,
        out_specs=P(None, None, ("tile", "sec"), None),
        check_vma=False,
    )
```

```python
import functools

import jax
import jax.numpy as jnp
from jax import lax
from jax.experimental import pallas as pl
from jax.experimental.pallas import tpu as pltpu
from jax.sharding import PartitionSpec as P

ISTEPS = 8
ZSTEPS = 8


STEP_PLANE = 0.12
STEP_CROSS = 0.15

HALO = -(-(ISTEPS - 1) // 8) * 8

VMEM = pl.BlockSpec(memory_space=pltpu.VMEM)
LIMIT = pltpu.CompilerParams(vmem_limit_bytes=8 * 1024 * 1024)
ANY = pl.BlockSpec(memory_space=pl.ANY)


def spread(layers, inner_rows, blocks, dest_ref, pos_ref, flow_ref, conf_ref, out_ref):
    groups = out_ref.shape[0]
    count, width = conf_ref.shape
    place = pos_ref[...]
    layer = place // (inner_rows * blocks)
    inner_row = place // blocks % inner_rows
    column_block = place % blocks
    slot = (dest_ref[...] * layers + layer) * inner_rows + inner_row
    slots = groups * layers * inner_rows
    conf = conf_ref[...]
    terms = [flow_ref[pl.ds(c, count, stride=2), :] * conf for c in range(2)] + [conf]
    rest = jnp.concatenate(terms, axis=1)
    parts = []
    for _ in range(3):
        parts.append(rest.astype(jnp.bfloat16))
        rest = rest - parts[-1].astype(jnp.float32)
    numbers = lax.broadcasted_iota(jnp.int32, (slots, count), 0)
    for b in range(blocks):
        key = jnp.where(column_block == b, slot, -1)
        hit = jnp.where(numbers == key, 1.0, 0.0).astype(jnp.bfloat16)
        total = sum(jnp.dot(hit, part, preferred_element_type=jnp.float32) for part in reversed(parts))
        for o in range(groups):
            for l in range(layers):
                start = (o * layers + l) * inner_rows
                for c in range(3):
                    out_ref[o, 2 + c, l, :, b * width : (b + 1) * width] = total[
                        start : start + inner_rows, c * width : (c + 1) * width
                    ]


def shifted(blocks, lane, width):
    ahead = [pltpu.roll(x, width - 1, 1) for x in blocks]
    behind = [pltpu.roll(x, 1, 1) for x in blocks]
    zero = jnp.zeros_like(blocks[0])
    right = [jnp.where(lane == width - 1, after, own) for own, after in zip(ahead, ahead[1:] + [zero])]
    left = [jnp.where(lane == 0, before, own) for own, before in zip(behind, [zero] + behind[:-1])]
    return left, right


def relax(held, springs, keeps, pushes, even, odd):
    _, layers, blocks, total, width = held.shape
    stride = total // 8
    lane = lax.broadcasted_iota(jnp.int32, (8, width), 1)
    places = [(j, b) for j in range(stride) for b in range(blocks)]

    for l in range(layers):
        for c in (2, 0, 1):
            for n, (j, b) in enumerate(places):
                part = STEP_PLANE * held[c, l, b, pl.ds(j, 8, stride=stride), :]
                if c == 2:
                    springs[l, n] = part
                    keeps[l, n] = 1.0 - 4.0 * part
                else:
                    pushes[l, c, n] = part

    def step(source, store):
        for l in range(layers):
            for c in range(2):
                field = [[source[l, c, j * blocks + b] for b in range(blocks)] for j in range(stride)]
                above = [[pltpu.roll(x, 1, 0) for x in field[-1]]] + field[:-1]
                below = field[1:] + [[pltpu.roll(x, 7, 0) for x in field[0]]]
                for j in range(stride):
                    left, right = shifted(field[j], lane, width)
                    for b in range(blocks):
                        n = j * blocks + b
                        near = (above[j][b] + below[j][b]) + (left[b] + right[b])
                        store(l, c, n, springs[l, n] * near + (keeps[l, n] * field[j][b] + pushes[l, c, n]))

    def to(target):
        def store(l, c, n, value):
            target[l, c, n] = value

        return store

    def to_rows(l, c, n, value):
        j, b = places[n]
        held[c, l, b, pl.ds(j, 8, stride=stride), :] = value

    source = pushes
    for n in range(ISTEPS - 2):
        target = odd if n % 2 else even
        step(source, to(target))
        source = target
    step(source, to_rows)


def put_rows(held, out_ref, start, first, last):
    _, layers, blocks, _, width = held.shape
    inner_rows = out_ref.shape[3]
    for c in range(2):
        for l in range(layers):
            for b in range(blocks):
                for o in range(first // inner_rows, last // inner_rows):
                    at = start + o * inner_rows - first
                    out_ref[o, c, l, :, b * width : (b + 1) * width] = held[c, l, b, at : at + inner_rows, :]


def inner_kernel(dest_ref, pos_ref, flow_ref, conf_ref, own_ref, out_ref, edge_ref, held, *scratch):
    _, layers, rows, columns = own_ref.shape
    blocks, width = held.shape[2], held.shape[-1]
    spread(layers, out_ref.shape[3], blocks, dest_ref, pos_ref, flow_ref, conf_ref, out_ref)
    for b in range(blocks):
        held[:, :, b] = own_ref[:, :, :, b * width : (b + 1) * width]
    edge_ref[:, :, :, : 2 * HALO] = held[:, :, :, : 2 * HALO]
    edge_ref[:, :, :, 2 * HALO :] = held[:, :, :, rows - 2 * HALO :]
    relax(held, *scratch)
    put_rows(held, out_ref, HALO, HALO, rows - HALO)


def end_kernel(tiles, first_swap, tile_ref, edge_ref, halo_ref, mixed_ref, out_ref, held, *scratch):
    _, layers, blocks, _, width = held.shape
    groups, _, _, inner_rows, _ = out_ref.shape
    count = HALO // inner_rows
    tile = tile_ref[0]
    top = (tile & 1) == (1 if first_swap else 0)
    alone = jnp.where(top, tile == 0, tile == tiles - 1)
    for b in range(blocks):
        halo = jnp.where(alone, 0.0, halo_ref[:, :, :, b * width : (b + 1) * width])
        own = [edge_ref[:, :, b, n * HALO : (n + 1) * HALO] for n in range(4)]
        held[:, :, b, :HALO] = jnp.where(top, halo, own[2])
        held[:, :, b, HALO : 2 * HALO] = jnp.where(top, own[0], own[3])
        held[:, :, b, 2 * HALO :] = jnp.where(top, own[1], halo)
    out_ref[...] = mixed_ref[...]
    relax(held, *scratch)
    at = jnp.where(top, 0, groups - count)
    for c in range(2):
        for l in range(layers):
            for b in range(blocks):
                for n in range(count):
                    start = HALO + n * inner_rows
                    out_ref[at + n, c, l, :, b * width : (b + 1) * width] = held[c, l, b, start : start + inner_rows, :]


def relax_scratch(layers, blocks, total, width):
    parts = total // 8 * blocks
    return [pltpu.VMEM((3, layers, blocks, total, width), jnp.float32)] + [
        pltpu.VMEM((layers, parts, 8, width), jnp.float32),
        pltpu.VMEM((layers, parts, 8, width), jnp.float32),
        pltpu.VMEM((layers, 2, parts, 8, width), jnp.float32),
        pltpu.VMEM((layers, 2, parts, 8, width), jnp.float32),
        pltpu.VMEM((layers, 2, parts, 8, width), jnp.float32),
    ]


def cross_kernel(moved_ref, stiff_ref, out_ref, result, sems):
    groups, _, layers, inner_rows, columns = moved_ref.shape
    sections = groups * layers
    width = result.shape[-1]
    blocks = columns // width
    zero = jnp.zeros((1, inner_rows, width), jnp.float32)

    def outgoing(index):
        b, c = index // 2, index % 2
        span = pl.ds(pl.multiple_of(b * width, width), width)
        return pltpu.make_async_copy(result.at[index], out_ref.at[c, :, :, span], sems.at[index])

    def one(index, carry):
        b, c = index // 2, index % 2
        span = pl.ds(pl.multiple_of(b * width, width), width)

        def channel(c):
            return moved_ref[:, c, :, :, span].reshape(sections, inner_rows, width)

        spring = STEP_CROSS * stiff_ref[:, :, span]
        weight = STEP_CROSS * channel(4)
        pull = STEP_CROSS * channel(2 + c)

        def step(_, field):
            rise = field - jnp.concatenate([zero, field[:-1]], axis=0)
            rise_above = jnp.concatenate([rise[1:], -field[-1:]], axis=0)
            stretch = pull - weight * rise
            stretch_above = jnp.concatenate([stretch[1:], zero], axis=0)
            return field + (spring * (rise_above - rise) + (stretch - stretch_above))

        result[index] = lax.fori_loop(0, ZSTEPS, step, channel(c), unroll=True)
        outgoing(index).start()
        return carry

    lax.fori_loop(0, 2 * blocks, one, 0)
    for index in range(2 * blocks):
        outgoing(index).wait()


def per_device(
    in_plane_force, stiffness, stiffness_z, patch_dest, patch_pos, patch_flow, patch_conf
):
    groups = lax.axis_size("sec")
    tiles = lax.axis_size("tile")
    layers, rows, columns = stiffness.shape
    inner_rows = rows // groups
    width = patch_flow.shape[-1]
    blocks = columns // width
    count = patch_pos.shape[2]
    swaps = []
    for n in range(2):
        other = [i + 1 if i % 2 == n else i - 1 for i in range(tiles)]
        swaps.append([(i, j if 0 <= j < tiles else i) for i, j in enumerate(other)])
    tile = lax.axis_index("tile")
    odd = tile & 1

    rest = ((0, 0),) * 3
    own = jnp.pad(in_plane_force, ((0, 1),) + rest) + jnp.pad(stiffness[None], ((2, 0),) + rest)

    first, last = own[:, :, :HALO], own[:, :, rows - HALO :]
    two = lax.ppermute(jnp.where(odd == 1, last, first), "tile", swaps[1])
    one = lax.ppermute(jnp.where(odd == 1, first, last), "tile", swaps[0])
    mixed_shape = jax.ShapeDtypeStruct((groups, 5, layers, inner_rows, columns), jnp.float32)
    mixed, own_edges = pl.pallas_call(
        inner_kernel,
        out_shape=[mixed_shape, jax.ShapeDtypeStruct((3, layers, blocks, 4 * HALO, width), jnp.float32)],
        in_specs=[VMEM] * 5,
        out_specs=[VMEM] * 2,
        scratch_shapes=relax_scratch(layers, blocks, rows, width),
        compiler_params=LIMIT,
        cost_estimate=pl.CostEstimate(flops=10**9, bytes_accessed=10**7, transcendentals=0),
        name="spread_and_inner_rows",
    )(
        patch_dest.reshape(1, count),
        patch_pos.reshape(1, count),
        patch_flow.reshape(count * 2, width),
        patch_conf.reshape(count, width),
        own,
    )
    for halo, first_swap in ((one, True), (two, False)):
        mixed = pl.pallas_call(
            functools.partial(end_kernel, tiles, first_swap),
            out_shape=mixed_shape,
            in_specs=[pl.BlockSpec(memory_space=pltpu.SMEM)] + [VMEM] * 3,
            out_specs=VMEM,
            scratch_shapes=relax_scratch(layers, blocks, 3 * HALO, width),
            compiler_params=LIMIT,
            cost_estimate=pl.CostEstimate(flops=10**7, bytes_accessed=10**6, transcendentals=0),
            name="end_rows",
        )(tile.reshape(1), own_edges, halo, mixed)
    moved = lax.all_to_all(mixed, "sec", split_axis=0, concat_axis=0, tiled=True)
    return pl.pallas_call(
        cross_kernel,
        out_shape=jax.ShapeDtypeStruct((2, groups * layers, inner_rows, columns), jnp.float32),
        in_specs=[VMEM] * 2,
        out_specs=ANY,
        scratch_shapes=[
            pltpu.VMEM((2 * blocks, groups * layers, inner_rows, width), jnp.float32),
            pltpu.SemaphoreType.DMA((2 * blocks,)),
        ],
        compiler_params=LIMIT,
        cost_estimate=pl.CostEstimate(flops=10000000, bytes_accessed=800000, transcendentals=0),
        name="cross_steps",
    )(moved, stiffness_z)


def solution(mesh):
    placed = (
        P(None, "sec", "tile", None),
        P("sec", "tile", None),
        P(None, ("tile", "sec"), None),
        P("sec", "tile", None, None),
        P("sec", "tile", None),
        P("sec", "tile", None, None, None),
        P("sec", "tile", None, None),
    )
    return jax.shard_map(
        per_device,
        mesh=mesh,
        in_specs=placed,
        out_specs=P(None, None, ("tile", "sec"), None),
        check_vma=False,
    )
```

```python
import functools

import jax
import jax.numpy as jnp
from jax import lax
from jax.experimental import pallas as pl
from jax.experimental.pallas import tpu as pltpu
from jax.sharding import PartitionSpec as P

ISTEPS = 8
ZSTEPS = 8


STEP_PLANE = 0.12
STEP_CROSS = 0.15

HALO = -(-(ISTEPS - 1) // 8) * 8

VMEM = pl.BlockSpec(memory_space=pltpu.VMEM)
LIMIT = pltpu.CompilerParams(vmem_limit_bytes=8 * 1024 * 1024)
ANY = pl.BlockSpec(memory_space=pl.ANY)


def spread(layers, inner_rows, blocks, dest_ref, pos_ref, flow_ref, conf_ref, out_ref):
    groups = out_ref.shape[0]
    count, width = conf_ref.shape
    place = pos_ref[...]
    layer = place // (inner_rows * blocks)
    inner_row = place // blocks % inner_rows
    column_block = place % blocks
    slot = (dest_ref[...] * layers + layer) * inner_rows + inner_row
    slots = groups * layers * inner_rows
    conf = conf_ref[...]
    terms = [flow_ref[pl.ds(c, count, stride=2), :] * conf for c in range(2)] + [conf]
    rest = jnp.concatenate(terms, axis=1)
    parts = []
    for _ in range(3):
        parts.append(rest.astype(jnp.bfloat16))
        rest = rest - parts[-1].astype(jnp.float32)
    numbers = lax.broadcasted_iota(jnp.int32, (slots, count), 0)
    for b in range(blocks):
        key = jnp.where(column_block == b, slot, -1)
        hit = jnp.where(numbers == key, 1.0, 0.0).astype(jnp.bfloat16)
        total = sum(jnp.dot(hit, part, preferred_element_type=jnp.float32) for part in reversed(parts))
        for o in range(groups):
            for l in range(layers):
                start = (o * layers + l) * inner_rows
                for c in range(3):
                    out_ref[o, 2 + c, l, :, b * width : (b + 1) * width] = total[
                        start : start + inner_rows, c * width : (c + 1) * width
                    ]


def shifted(blocks, lane, width):
    ahead = [pltpu.roll(x, width - 1, 1) for x in blocks]
    behind = [pltpu.roll(x, 1, 1) for x in blocks]
    zero = jnp.zeros_like(blocks[0])
    right = [jnp.where(lane == width - 1, after, own) for own, after in zip(ahead, ahead[1:] + [zero])]
    left = [jnp.where(lane == 0, before, own) for own, before in zip(behind, [zero] + behind[:-1])]
    return left, right


def relax(held, springs, keeps, pushes, even, odd):
    _, layers, blocks, total, width = held.shape
    stride = total // 8
    lane = lax.broadcasted_iota(jnp.int32, (8, width), 1)
    places = [(j, b) for j in range(stride) for b in range(blocks)]

    for l in range(layers):
        for c in (2, 0, 1):
            for n, (j, b) in enumerate(places):
                part = STEP_PLANE * held[c, l, b, pl.ds(j, 8, stride=stride), :]
                if c == 2:
                    springs[l, n] = part
                    keeps[l, n] = 1.0 - 4.0 * part
                else:
                    pushes[l, c, n] = part

    def step(source, store):
        for l in range(layers):
            for c in range(2):
                field = [[source[l, c, j * blocks + b] for b in range(blocks)] for j in range(stride)]
                above = [[pltpu.roll(x, 1, 0) for x in field[-1]]] + field[:-1]
                below = field[1:] + [[pltpu.roll(x, 7, 0) for x in field[0]]]
                for j in range(stride):
                    left, right = shifted(field[j], lane, width)
                    for b in range(blocks):
                        n = j * blocks + b
                        near = (above[j][b] + below[j][b]) + (left[b] + right[b])
                        store(l, c, n, springs[l, n] * near + (keeps[l, n] * field[j][b] + pushes[l, c, n]))

    def to(target):
        def store(l, c, n, value):
            target[l, c, n] = value

        return store

    def to_rows(l, c, n, value):
        j, b = places[n]
        held[c, l, b, pl.ds(j, 8, stride=stride), :] = value

    source = pushes
    for n in range(ISTEPS - 2):
        target = odd if n % 2 else even
        step(source, to(target))
        source = target
    step(source, to_rows)


def put_rows(held, out_ref, start, first, last):
    _, layers, blocks, _, width = held.shape
    inner_rows = out_ref.shape[3]
    for c in range(2):
        for l in range(layers):
            for b in range(blocks):
                for o in range(first // inner_rows, last // inner_rows):
                    at = start + o * inner_rows - first
                    out_ref[o, c, l, :, b * width : (b + 1) * width] = held[c, l, b, at : at + inner_rows, :]


def inner_kernel(dest_ref, pos_ref, flow_ref, conf_ref, own_ref, out_ref, edge_ref, held, *scratch):
    _, layers, rows, columns = own_ref.shape
    blocks, width = held.shape[2], held.shape[-1]
    spread(layers, out_ref.shape[3], blocks, dest_ref, pos_ref, flow_ref, conf_ref, out_ref)
    for b in range(blocks):
        held[:, :, b] = own_ref[:, :, :, b * width : (b + 1) * width]
    edge_ref[:, :, :, : 2 * HALO] = held[:, :, :, : 2 * HALO]
    edge_ref[:, :, :, 2 * HALO :] = held[:, :, :, rows - 2 * HALO :]
    relax(held, *scratch)
    put_rows(held, out_ref, HALO, HALO, rows - HALO)


def end_kernel(tiles, first_swap, tile_ref, edge_ref, halo_ref, mixed_ref, out_ref, held, *scratch):
    _, layers, blocks, _, width = held.shape
    groups, _, _, inner_rows, _ = out_ref.shape
    count = HALO // inner_rows
    tile = tile_ref[0]
    top = (tile & 1) == (1 if first_swap else 0)
    alone = jnp.where(top, tile == 0, tile == tiles - 1)
    for b in range(blocks):
        halo = jnp.where(alone, 0.0, halo_ref[:, :, :, b * width : (b + 1) * width])
        own = [edge_ref[:, :, b, n * HALO : (n + 1) * HALO] for n in range(4)]
        held[:, :, b, :HALO] = jnp.where(top, halo, own[2])
        held[:, :, b, HALO : 2 * HALO] = jnp.where(top, own[0], own[3])
        held[:, :, b, 2 * HALO :] = jnp.where(top, own[1], halo)
    out_ref[...] = mixed_ref[...]
    relax(held, *scratch)
    at = jnp.where(top, 0, groups - count)
    for c in range(2):
        for l in range(layers):
            for b in range(blocks):
                for n in range(count):
                    start = HALO + n * inner_rows
                    out_ref[at + n, c, l, :, b * width : (b + 1) * width] = held[c, l, b, start : start + inner_rows, :]


def relax_scratch(layers, blocks, total, width):
    parts = total // 8 * blocks
    return [pltpu.VMEM((3, layers, blocks, total, width), jnp.float32)] + [
        pltpu.VMEM((layers, parts, 8, width), jnp.float32),
        pltpu.VMEM((layers, parts, 8, width), jnp.float32),
        pltpu.VMEM((layers, 2, parts, 8, width), jnp.float32),
        pltpu.VMEM((layers, 2, parts, 8, width), jnp.float32),
        pltpu.VMEM((layers, 2, parts, 8, width), jnp.float32),
    ]


def cross_kernel(moved_ref, stiff_ref, out_ref, result, sems):
    groups, _, layers, inner_rows, columns = moved_ref.shape
    sections = groups * layers
    width = result.shape[-1]
    blocks = columns // width
    zero = jnp.zeros((1, inner_rows, width), jnp.float32)

    def outgoing(index):
        b, c = index // 2, index % 2
        span = pl.ds(pl.multiple_of(b * width, width), width)
        return pltpu.make_async_copy(result.at[index], out_ref.at[c, :, :, span], sems.at[index])

    def one(b, carry):
        span = pl.ds(pl.multiple_of(b * width, width), width)

        def channel(c):
            return moved_ref[:, c, :, :, span].reshape(sections, inner_rows, width)

        spring = STEP_CROSS * stiff_ref[:, :, span]
        weight = STEP_CROSS * channel(4)
        pulls = [STEP_CROSS * channel(2 + c) for c in range(2)]

        def step(_, fields):
            stepped = []
            for field, pull in zip(fields, pulls):
                rise = field - jnp.concatenate([zero, field[:-1]], axis=0)
                rise_above = jnp.concatenate([rise[1:], -field[-1:]], axis=0)
                stretch = pull - weight * rise
                stretch_above = jnp.concatenate([stretch[1:], zero], axis=0)
                stepped.append(field + (spring * (rise_above - rise) + (stretch - stretch_above)))
            return stepped

        fields = lax.fori_loop(0, ZSTEPS, step, [channel(c) for c in range(2)], unroll=True)
        for c in range(2):
            result[2 * b + c] = fields[c]
            outgoing(2 * b + c).start()
        return carry

    lax.fori_loop(0, blocks, one, 0)
    for index in range(2 * blocks):
        outgoing(index).wait()


def per_device(
    in_plane_force, stiffness, stiffness_z, patch_dest, patch_pos, patch_flow, patch_conf
):
    groups = lax.axis_size("sec")
    tiles = lax.axis_size("tile")
    layers, rows, columns = stiffness.shape
    inner_rows = rows // groups
    width = patch_flow.shape[-1]
    blocks = columns // width
    count = patch_pos.shape[2]
    swaps = []
    for n in range(2):
        other = [i + 1 if i % 2 == n else i - 1 for i in range(tiles)]
        swaps.append([(i, j if 0 <= j < tiles else i) for i, j in enumerate(other)])
    tile = lax.axis_index("tile")
    odd = tile & 1

    rest = ((0, 0),) * 3
    own = jnp.pad(in_plane_force, ((0, 1),) + rest) + jnp.pad(stiffness[None], ((2, 0),) + rest)

    first, last = own[:, :, :HALO], own[:, :, rows - HALO :]
    two = lax.ppermute(jnp.where(odd == 1, last, first), "tile", swaps[1])
    one = lax.ppermute(jnp.where(odd == 1, first, last), "tile", swaps[0])
    mixed_shape = jax.ShapeDtypeStruct((groups, 5, layers, inner_rows, columns), jnp.float32)
    mixed, own_edges = pl.pallas_call(
        inner_kernel,
        out_shape=[mixed_shape, jax.ShapeDtypeStruct((3, layers, blocks, 4 * HALO, width), jnp.float32)],
        in_specs=[VMEM] * 5,
        out_specs=[VMEM] * 2,
        scratch_shapes=relax_scratch(layers, blocks, rows, width),
        compiler_params=LIMIT,
        cost_estimate=pl.CostEstimate(flops=10**9, bytes_accessed=10**7, transcendentals=0),
        name="spread_and_inner_rows",
    )(
        patch_dest.reshape(1, count),
        patch_pos.reshape(1, count),
        patch_flow.reshape(count * 2, width),
        patch_conf.reshape(count, width),
        own,
    )
    for halo, first_swap in ((one, True), (two, False)):
        mixed = pl.pallas_call(
            functools.partial(end_kernel, tiles, first_swap),
            out_shape=mixed_shape,
            in_specs=[pl.BlockSpec(memory_space=pltpu.SMEM)] + [VMEM] * 3,
            out_specs=VMEM,
            scratch_shapes=relax_scratch(layers, blocks, 3 * HALO, width),
            compiler_params=LIMIT,
            cost_estimate=pl.CostEstimate(flops=10**7, bytes_accessed=10**6, transcendentals=0),
            name="end_rows",
        )(tile.reshape(1), own_edges, halo, mixed)
    moved = lax.all_to_all(mixed, "sec", split_axis=0, concat_axis=0, tiled=True)
    return pl.pallas_call(
        cross_kernel,
        out_shape=jax.ShapeDtypeStruct((2, groups * layers, inner_rows, columns), jnp.float32),
        in_specs=[VMEM] * 2,
        out_specs=ANY,
        scratch_shapes=[
            pltpu.VMEM((2 * blocks, groups * layers, inner_rows, width), jnp.float32),
            pltpu.SemaphoreType.DMA((2 * blocks,)),
        ],
        compiler_params=LIMIT,
        cost_estimate=pl.CostEstimate(flops=10000000, bytes_accessed=800000, transcendentals=0),
        name="cross_steps",
    )(moved, stiffness_z)


def solution(mesh):
    placed = (
        P(None, "sec", "tile", None),
        P("sec", "tile", None),
        P(None, ("tile", "sec"), None),
        P("sec", "tile", None, None),
        P("sec", "tile", None),
        P("sec", "tile", None, None, None),
        P("sec", "tile", None, None),
    )
    return jax.shard_map(
        per_device,
        mesh=mesh,
        in_specs=placed,
        out_specs=P(None, None, ("tile", "sec"), None),
        check_vma=False,
    )
```

```python
import functools

import jax
import jax.numpy as jnp
from jax import lax
from jax.experimental import pallas as pl
from jax.experimental.pallas import tpu as pltpu
from jax.sharding import PartitionSpec as P

ISTEPS = 8
ZSTEPS = 8


STEP_PLANE = 0.12
STEP_CROSS = 0.15

HALO = -(-(ISTEPS - 1) // 8) * 8

VMEM = pl.BlockSpec(memory_space=pltpu.VMEM)
LIMIT = pltpu.CompilerParams(vmem_limit_bytes=8 * 1024 * 1024)
ANY = pl.BlockSpec(memory_space=pl.ANY)


def spread(layers, inner_rows, blocks, dest_ref, pos_ref, flow_ref, conf_ref, out_ref):
    groups = out_ref.shape[0]
    count, width = conf_ref.shape
    place = pos_ref[...]
    layer = place // (inner_rows * blocks)
    inner_row = place // blocks % inner_rows
    column_block = place % blocks
    slot = (dest_ref[...] * layers + layer) * inner_rows + inner_row
    slots = groups * layers * inner_rows
    conf = conf_ref[...]
    terms = [flow_ref[pl.ds(c, count, stride=2), :] * conf for c in range(2)] + [conf]
    rest = jnp.concatenate(terms, axis=1)
    parts = []
    for _ in range(3):
        parts.append(rest.astype(jnp.bfloat16))
        rest = rest - parts[-1].astype(jnp.float32)
    numbers = lax.broadcasted_iota(jnp.int32, (slots, count), 0)
    for b in range(blocks):
        key = jnp.where(column_block == b, slot, -1)
        hit = jnp.where(numbers == key, 1.0, 0.0).astype(jnp.bfloat16)
        total = sum(jnp.dot(hit, part, preferred_element_type=jnp.float32) for part in reversed(parts))
        for o in range(groups):
            for l in range(layers):
                start = (o * layers + l) * inner_rows
                for c in range(3):
                    out_ref[o, 2 + c, l, :, b * width : (b + 1) * width] = total[
                        start : start + inner_rows, c * width : (c + 1) * width
                    ]


def shifted(blocks, lane, width):
    ahead = [pltpu.roll(x, width - 1, 1) for x in blocks]
    behind = [pltpu.roll(x, 1, 1) for x in blocks]
    zero = jnp.zeros_like(blocks[0])
    right = [jnp.where(lane == width - 1, after, own) for own, after in zip(ahead, ahead[1:] + [zero])]
    left = [jnp.where(lane == 0, before, own) for own, before in zip(behind, [zero] + behind[:-1])]
    return left, right


def relax(held, springs, keeps, pushes, even, odd):
    _, layers, blocks, total, width = held.shape
    stride = total // 8
    lane = lax.broadcasted_iota(jnp.int32, (8, width), 1)
    places = [(j, b) for j in range(stride) for b in range(blocks)]

    for l in range(layers):
        for c in (2, 0, 1):
            for n, (j, b) in enumerate(places):
                part = STEP_PLANE * held[c, l, b, pl.ds(j, 8, stride=stride), :]
                if c == 2:
                    springs[l, n] = part
                    keeps[l, n] = 1.0 - 4.0 * part
                else:
                    pushes[l, c, n] = part

    def step(source, store):
        for l in range(layers):
            for c in range(2):
                field = [[source[l, c, j * blocks + b] for b in range(blocks)] for j in range(stride)]
                above = [[pltpu.roll(x, 1, 0) for x in field[-1]]] + field[:-1]
                below = field[1:] + [[pltpu.roll(x, 7, 0) for x in field[0]]]
                for j in range(stride):
                    left, right = shifted(field[j], lane, width)
                    for b in range(blocks):
                        n = j * blocks + b
                        near = (above[j][b] + below[j][b]) + (left[b] + right[b])
                        store(l, c, n, springs[l, n] * near + (keeps[l, n] * field[j][b] + pushes[l, c, n]))

    def to(target):
        def store(l, c, n, value):
            target[l, c, n] = value

        return store

    def to_rows(l, c, n, value):
        j, b = places[n]
        held[c, l, b, pl.ds(j, 8, stride=stride), :] = value

    source = pushes
    for n in range(ISTEPS - 2):
        target = odd if n % 2 else even
        step(source, to(target))
        source = target
    step(source, to_rows)


def put_rows(held, out_ref, start, first, last):
    _, layers, blocks, _, width = held.shape
    inner_rows = out_ref.shape[3]
    for c in range(2):
        for l in range(layers):
            for b in range(blocks):
                for o in range(first // inner_rows, last // inner_rows):
                    at = start + o * inner_rows - first
                    out_ref[o, c, l, :, b * width : (b + 1) * width] = held[c, l, b, at : at + inner_rows, :]


def inner_kernel(dest_ref, pos_ref, flow_ref, conf_ref, own_ref, out_ref, edge_ref, held, *scratch):
    _, layers, rows, columns = own_ref.shape
    blocks, width = held.shape[2], held.shape[-1]
    spread(layers, out_ref.shape[3], blocks, dest_ref, pos_ref, flow_ref, conf_ref, out_ref)
    for b in range(blocks):
        held[:, :, b] = own_ref[:, :, :, b * width : (b + 1) * width]
    edge_ref[:, :, :, : 2 * HALO] = held[:, :, :, : 2 * HALO]
    edge_ref[:, :, :, 2 * HALO :] = held[:, :, :, rows - 2 * HALO :]
    relax(held, *scratch)
    put_rows(held, out_ref, HALO, HALO, rows - HALO)


def end_kernel(tiles, first_swap, tile_ref, edge_ref, halo_ref, mixed_ref, out_ref, held, *scratch):
    _, layers, blocks, _, width = held.shape
    groups, _, _, inner_rows, _ = out_ref.shape
    count = HALO // inner_rows
    tile = tile_ref[0]
    top = (tile & 1) == (1 if first_swap else 0)
    alone = jnp.where(top, tile == 0, tile == tiles - 1)
    for b in range(blocks):
        halo = jnp.where(alone, 0.0, halo_ref[:, :, :, b * width : (b + 1) * width])
        own = [edge_ref[:, :, b, n * HALO : (n + 1) * HALO] for n in range(4)]
        held[:, :, b, :HALO] = jnp.where(top, halo, own[2])
        held[:, :, b, HALO : 2 * HALO] = jnp.where(top, own[0], own[3])
        held[:, :, b, 2 * HALO :] = jnp.where(top, own[1], halo)
    out_ref[...] = mixed_ref[...]
    relax(held, *scratch)
    at = jnp.where(top, 0, groups - count)
    for c in range(2):
        for l in range(layers):
            for b in range(blocks):
                for n in range(count):
                    start = HALO + n * inner_rows
                    out_ref[at + n, c, l, :, b * width : (b + 1) * width] = held[c, l, b, start : start + inner_rows, :]


def relax_scratch(layers, blocks, total, width):
    parts = total // 8 * blocks
    return [pltpu.VMEM((3, layers, blocks, total, width), jnp.float32)] + [
        pltpu.VMEM((layers, parts, 8, width), jnp.float32),
        pltpu.VMEM((layers, parts, 8, width), jnp.float32),
        pltpu.VMEM((layers, 2, parts, 8, width), jnp.float32),
        pltpu.VMEM((layers, 2, parts, 8, width), jnp.float32),
        pltpu.VMEM((layers, 2, parts, 8, width), jnp.float32),
    ]


def cross_kernel(moved_ref, stiff_ref, out_ref, result, sems):
    groups, _, layers, inner_rows, columns = moved_ref.shape
    sections = groups * layers
    width = result.shape[-1]
    blocks = columns // width
    zero = jnp.zeros((1, inner_rows, width), jnp.float32)

    def outgoing(index):
        b, c = index // 2, index % 2
        span = pl.ds(pl.multiple_of(b * width, width), width)
        return pltpu.make_async_copy(result.at[index], out_ref.at[c, :, :, span], sems.at[index])

    def one(b, carry):
        span = pl.ds(pl.multiple_of(b * width, width), width)

        def channel(c):
            return moved_ref[:, c, :, :, span].reshape(sections, inner_rows, width)

        spring = STEP_CROSS * stiff_ref[:, :, span]
        weight = STEP_CROSS * channel(4)
        pulls = [STEP_CROSS * channel(2 + c) for c in range(2)]

        def step(_, fields):
            stepped = []
            for field, pull in zip(fields, pulls):
                rise = field - jnp.concatenate([zero, field[:-1]], axis=0)
                rise_above = jnp.concatenate([rise[1:], -field[-1:]], axis=0)
                stretch = pull - weight * rise
                stretch_above = jnp.concatenate([stretch[1:], zero], axis=0)
                stepped.append(field + (spring * (rise_above - rise) + (stretch - stretch_above)))
            return stepped

        fields = lax.fori_loop(0, ZSTEPS, step, [channel(c) for c in range(2)], unroll=True)
        for c in range(2):
            result[2 * b + c] = fields[c]
            outgoing(2 * b + c).start()
        return carry

    lax.fori_loop(0, blocks, one, 0, unroll=True)
    for index in range(2 * blocks):
        outgoing(index).wait()


def per_device(
    in_plane_force, stiffness, stiffness_z, patch_dest, patch_pos, patch_flow, patch_conf
):
    groups = lax.axis_size("sec")
    tiles = lax.axis_size("tile")
    layers, rows, columns = stiffness.shape
    inner_rows = rows // groups
    width = patch_flow.shape[-1]
    blocks = columns // width
    count = patch_pos.shape[2]
    swaps = []
    for n in range(2):
        other = [i + 1 if i % 2 == n else i - 1 for i in range(tiles)]
        swaps.append([(i, j if 0 <= j < tiles else i) for i, j in enumerate(other)])
    tile = lax.axis_index("tile")
    odd = tile & 1

    rest = ((0, 0),) * 3
    own = jnp.pad(in_plane_force, ((0, 1),) + rest) + jnp.pad(stiffness[None], ((2, 0),) + rest)

    first, last = own[:, :, :HALO], own[:, :, rows - HALO :]
    two = lax.ppermute(jnp.where(odd == 1, last, first), "tile", swaps[1])
    one = lax.ppermute(jnp.where(odd == 1, first, last), "tile", swaps[0])
    mixed_shape = jax.ShapeDtypeStruct((groups, 5, layers, inner_rows, columns), jnp.float32)
    mixed, own_edges = pl.pallas_call(
        inner_kernel,
        out_shape=[mixed_shape, jax.ShapeDtypeStruct((3, layers, blocks, 4 * HALO, width), jnp.float32)],
        in_specs=[VMEM] * 5,
        out_specs=[VMEM] * 2,
        scratch_shapes=relax_scratch(layers, blocks, rows, width),
        compiler_params=LIMIT,
        cost_estimate=pl.CostEstimate(flops=10**9, bytes_accessed=10**7, transcendentals=0),
        name="spread_and_inner_rows",
    )(
        patch_dest.reshape(1, count),
        patch_pos.reshape(1, count),
        patch_flow.reshape(count * 2, width),
        patch_conf.reshape(count, width),
        own,
    )
    for halo, first_swap in ((one, True), (two, False)):
        mixed = pl.pallas_call(
            functools.partial(end_kernel, tiles, first_swap),
            out_shape=mixed_shape,
            in_specs=[pl.BlockSpec(memory_space=pltpu.SMEM)] + [VMEM] * 3,
            out_specs=VMEM,
            scratch_shapes=relax_scratch(layers, blocks, 3 * HALO, width),
            compiler_params=LIMIT,
            cost_estimate=pl.CostEstimate(flops=10**7, bytes_accessed=10**6, transcendentals=0),
            name="end_rows",
        )(tile.reshape(1), own_edges, halo, mixed)
    moved = lax.all_to_all(mixed, "sec", split_axis=0, concat_axis=0, tiled=True)
    return pl.pallas_call(
        cross_kernel,
        out_shape=jax.ShapeDtypeStruct((2, groups * layers, inner_rows, columns), jnp.float32),
        in_specs=[VMEM] * 2,
        out_specs=ANY,
        scratch_shapes=[
            pltpu.VMEM((2 * blocks, groups * layers, inner_rows, width), jnp.float32),
            pltpu.SemaphoreType.DMA((2 * blocks,)),
        ],
        compiler_params=LIMIT,
        cost_estimate=pl.CostEstimate(flops=10000000, bytes_accessed=800000, transcendentals=0),
        name="cross_steps",
    )(moved, stiffness_z)


def solution(mesh):
    placed = (
        P(None, "sec", "tile", None),
        P("sec", "tile", None),
        P(None, ("tile", "sec"), None),
        P("sec", "tile", None, None),
        P("sec", "tile", None),
        P("sec", "tile", None, None, None),
        P("sec", "tile", None, None),
    )
    return jax.shard_map(
        per_device,
        mesh=mesh,
        in_specs=placed,
        out_specs=P(None, None, ("tile", "sec"), None),
        check_vma=False,
    )
```
